32 devices in a mesh: seq: 8 (over y, x, core), fsdp: 4 (over z).
Axes of the slice: x: 2, y: 2, z: 4, core: 2. Of those that a mesh axis runs over, the one named last changes fastest.
Arguments:
- features: bfloat16 [16384, 1280], P(('seq', 'fsdp')), may hold values from -40 to 40
- conv_weight: bfloat16 [5, 1280, 1536], P(None, None, 'fsdp'), may hold values from -0.078125 to 0.078125
- mix_weight: bfloat16 [1536, 1536], P(None, 'fsdp'), may hold values from -0.15625 to 0.15625
- pool_weight: bfloat16 [1536, 1536], P(None, 'fsdp'), may hold values from -0.21875 to 0.21875
- gain_first: bfloat16 [1280], P('fsdp'), may hold values from 0.099609375 to 1.8984375
- shift_first: bfloat16 [1280], P('fsdp'), may hold values from -3 to 3
- gain_second: bfloat16 [1536], P('fsdp'), may hold values from 0.099609375 to 1.8984375
- shift_second: bfloat16 [1536], P('fsdp'), may hold values from -3 to 3
- bias_conv: bfloat16 [1536], P('fsdp'), may hold values from -3 to 3
- bias_mix: bfloat16 [1536], P('fsdp'), may hold values from -3 to 3
- cotangent: bfloat16 [8192, 1536], P(('seq', 'fsdp')), may hold values from -6 to 6
- track_counts: int32 [8], replicated, may hold values from 1 to 5313, as said below
Outputs:
- pooled: bfloat16 [8192, 1536], P(('seq', 'fsdp'))
- grad_features: bfloat16 [16384, 1280], P(('seq', 'fsdp'))
- grad_conv: float32 [5, 1280, 1536], P(None, None, 'fsdp')
- grad_mix: float32 [1536, 1536], P(None, 'fsdp')
- grad_pool: float32 [1536, 1536], P(None, 'fsdp')
- grad_gain_first: float32 [1280], P('fsdp')
- grad_shift_first: float32 [1280], P('fsdp')
- grad_gain_second: float32 [1536], P('fsdp')
- grad_shift_second: float32 [1536], P('fsdp')
- grad_bias_conv: float32 [1536], P('fsdp')
- grad_bias_mix: float32 [1536], P('fsdp')
The draws below stay inside these ranges and needn't reach their ends.
Inputs may be any that keep to these rules, and one draw needn't show every extreme that they name: `track_counts`: each window has between 1 and 5313 present tracks; some window has 5313 and some other window has 1.
All inputs are finite; a program needn't handle non-finite values.
Results may differ from the reference program's by a relative error of at most 0.015.
Values may be sent and summed in bfloat16 or wider, within the bound.
A program may use at most 256 MiB of HBM per device.

```python
import math
import jax
import jax.numpy as jnp
from jax import lax

CIN = 1280
COUT = 1536
WIDTH = 5
TRACKS = 5313
WIN = 2048
POS = 16384
WINDOWS = 8
PAIRS = 8192


def draw_features(key, part):
    key = jax.random.fold_in(key, 11)
    noise_key, column_key, offset_key = jax.random.split(key, 3)
    position = jnp.arange(POS, dtype=jnp.float32) / max(POS - 1, 1)
    row_scale = 0.5 * jnp.power(3.0, position)
    column_scale = jnp.exp(jax.random.uniform(column_key, (CIN,), jnp.float32, math.log(0.3), math.log(3.0)))
    offsets = jax.random.uniform(offset_key, (CIN,), jnp.float32, -1.0, 1.0)
    noise = jax.random.truncated_normal(noise_key, -4.0, 4.0, (POS, CIN), jnp.float32)
    values = (noise + offsets[None, :]) * column_scale[None, :] * row_scale[:, None]
    return values.astype(jnp.bfloat16)


def draw_track_counts(key, part):
    key = jax.random.fold_in(key, 23)
    count_key, high_key, low_key = jax.random.split(key, 3)
    counts = jax.random.randint(count_key, (WINDOWS,), 1, TRACKS + 1)
    high_slot = jax.random.randint(high_key, (), 0, WINDOWS)
    low_slot = (high_slot + 1 + jax.random.randint(low_key, (), 0, WINDOWS - 1)) % WINDOWS
    counts = counts.at[high_slot].set(TRACKS)
    counts = counts.at[low_slot].set(1)
    return counts.astype(jnp.int32)


def block_scale(own_key, shape, pieces, least, largest):
    factor_of, own = 1.0, jax.random.fold_in(own_key, 6)
    for axis_at, shards_of in pieces:
        heights = jnp.exp(jax.random.uniform(jax.random.fold_in(own, axis_at), (shards_of,), jnp.float32, least / len(pieces), largest / len(pieces)))
        factor_of = factor_of * jnp.repeat(heights, shape[axis_at] // shards_of).reshape([-1 if axis == axis_at else 1 for axis in range(len(shape))])
    return factor_of


def bell_draw(rng, dims, scale, reach, pieces=(), kind=jnp.bfloat16):
    drawn = jax.random.normal(rng, dims, jnp.float32) * scale
    if len(pieces) > 0:
        drawn = block_scale(rng, dims, pieces, -0.22, 0.18) * drawn
    return jnp.clip(drawn, min=-reach, max=reach).astype(kind)


def setup_inputs(seed: int = 0) -> dict:
    keys = jax.random.split(jax.random.key(seed), 13)
    return {
        "features": draw_features(jax.random.fold_in(keys[12], 71), 0),
        "conv_weight": bell_draw(keys[1], (WIDTH, CIN, COUT), (WIDTH * CIN) ** -0.5, 0.078125, ((2, 4),)),
        "mix_weight": bell_draw(keys[2], (COUT, COUT), COUT ** -0.5, 0.15625, ((1, 4),)),
        "pool_weight": bell_draw(keys[3], (COUT, COUT), (COUT // 2) ** -0.5, 0.21875, ((1, 4),)),
        "gain_first": jnp.clip(1.0 + 0.18 * jax.random.normal(keys[4], (CIN,), jnp.float32), 0.099609375, 1.8984375).astype(jnp.bfloat16),
        "shift_first": bell_draw(keys[5], (CIN,), 0.5, 3.0, ((0, 4),)),
        "gain_second": jnp.clip(1.0 + 0.18 * jax.random.normal(keys[6], (COUT,), jnp.float32), 0.099609375, 1.8984375).astype(jnp.bfloat16),
        "shift_second": bell_draw(keys[7], (COUT,), 0.5, 3.0, ((0, 4),)),
        "bias_conv": bell_draw(keys[8], (COUT,), 0.5, 3.0, ((0, 4),)),
        "bias_mix": bell_draw(keys[9], (COUT,), 0.5, 3.0, ((0, 4),)),
        "cotangent": bell_draw(keys[10], (PAIRS, COUT), 1.0, 6.0, ((0, 32),)),
        "track_counts": draw_track_counts(jax.random.fold_in(keys[12], 71), 0),
    }


epsilon = 1e-05
highest = lax.Precision.HIGHEST

@jax.custom_vjp
def low(v):
    return lax.optimization_barrier(v.astype(jnp.bfloat16)).astype(jnp.float32)

@jax.custom_vjp
def low_back(v):
    return v

def low_keep(v):
    return (low(v), None)

def low_pass(kept, grad):
    return (grad,)

def back_keep(v):
    return (v, None)

def back_low(kept, grad):
    return (low(grad),)
low.defvjp(low_keep, low_pass)
low_back.defvjp(back_keep, back_low)

def activate(values):
    return jax.nn.gelu(values, approximate=False)

def normalize(values):
    center = lax.optimization_barrier(jnp.mean(values, axis=0))
    spread = lax.optimization_barrier(jnp.mean(jnp.square(values - center), axis=0))
    return (values - center) * lax.rsqrt(spread + epsilon)

def forward(features, conv_weight, mix_weight, pool_weight, gain_first, shift_first, gain_second, shift_second, bias_conv, bias_mix):
    active_one = low(activate(normalize(features) * gain_first + shift_first))
    half_width = (WIDTH - 1) // 2
    windowed = jnp.pad(active_one.reshape(WINDOWS, WIN, CIN), ((0, 0), (half_width, half_width), (0, 0)))
    conv_out = jnp.zeros((WINDOWS, WIN, COUT), jnp.float32)
    for offset in range(WIDTH):
        conv_out = conv_out + jnp.einsum('wpc,cd->wpd', windowed[:, offset:offset + WIN], conv_weight[offset], precision=highest)
    middle = low_back(conv_out.reshape(POS, COUT)) + bias_conv
    active_two = low(activate(normalize(middle) * gain_second + shift_second))
    summed = middle + low_back(jnp.dot(active_two, mix_weight, precision=highest)) + bias_mix
    logits = low_back(jnp.dot(low(summed), pool_weight, precision=highest)).reshape(PAIRS, 2, COUT)
    weights = jax.nn.softmax(logits, axis=1)
    return lax.optimization_barrier(jnp.sum(weights * summed.reshape(PAIRS, 2, COUT), axis=1))

def reference(features, conv_weight, mix_weight, pool_weight, gain_first, shift_first, gain_second, shift_second, bias_conv, bias_mix, cotangent, track_counts):
    params = tuple((item.astype(jnp.float32) for item in (features, conv_weight, mix_weight, pool_weight, gain_first, shift_first, gain_second, shift_second, bias_conv, bias_mix)))
    pooled, pull = jax.vjp(forward, *params)
    window_scale = track_counts.astype(jnp.float32) / TRACKS
    upstream = cotangent.astype(jnp.float32) * jnp.repeat(window_scale, WIN // 2)[:, None]
    grads = pull(upstream)
    return (pooled.astype(jnp.bfloat16), grads[0].astype(jnp.bfloat16), grads[1], grads[2], grads[3], grads[4], grads[5], grads[6], grads[7], grads[8], grads[9])
```

```python
import functools
import math
import jax
import jax.numpy as jnp
from jax import lax
from jax.experimental import pallas as pl
from jax.experimental.pallas import tpu as pltpu
from jax.sharding import PartitionSpec as P

TRACKS = 5313
WIN = 2048
EPSILON = 1e-05
MESH = pl.DeviceIdType.MESH
BF = jnp.bfloat16
F32 = jnp.float32
GROUP = 8


def dot(a, b, ca, cb):
    return lax.dot_general(a, b, (((ca,), (cb,)), ((), ())), preferred_element_type=F32)


def ds(start, size, step):
    return pl.ds(pl.multiple_of(start, step), size)


def fold(v):
    rows, width = v.shape
    return jnp.sum(v.reshape(rows // 8, 8, width), axis=0)


def rows_loop(total, step, body):
    def run(i, carry):
        body(pl.multiple_of(i * step, step))
        return carry

    lax.fori_loop(0, total // step, run, 0)


def row_sums(total, step, width, count, body):
    def run(i, carry):
        parts = body(pl.multiple_of(i * step, step))
        return tuple(c + fold(v) for c, v in zip(carry, parts))

    zero = tuple(jnp.zeros((8, width), F32) for _ in range(count))
    sums = lax.fori_loop(0, total // step, run, zero)
    return [jnp.sum(v, axis=0, keepdims=True) for v in sums]


def normal(b):
    cdf = 0.5 * (1.0 + lax.erf(b * math.sqrt(0.5)))
    pdf = jnp.exp(-0.5 * b * b) * (1.0 / math.sqrt(2.0 * math.pi))
    return cdf, cdf + b * pdf


class Copy:
    def __init__(self, links, src, there, here, device):
        i = links.count
        links.count += 1
        send, recv = links.send.at[i], links.recv.at[i]

        def make(dst):
            return pltpu.make_async_remote_copy(
                src_ref=src,
                dst_ref=dst,
                send_sem=send,
                recv_sem=recv,
                device_id=device,
                device_id_type=MESH,
            )

        self.links = links
        self.out, self.into = functools.partial(make, there), functools.partial(make, here)

    def start(self):
        self.out().start()
        self.links.started.append(self)
        return self

    def wait_recv(self):
        self.into().wait_recv()

    def wait_send(self):
        self.out().wait_send()


class Links:
    def __init__(self, send, recv):
        self.send, self.recv = send, recv
        self.count = 0
        self.started = []

    def copy(self, src, there, here, device):
        return Copy(self, src, there, here, device)

    def drain(self):
        for item in self.started:
            item.wait_send()
        self.started = []


class Place:
    def __init__(self, seq, fsdp):
        self.seq_size, self.fsdp_size = seq, fsdp
        self.s, self.z = lax.axis_index("seq"), lax.axis_index("fsdp")
        self.part = lax.rem(self.s, GROUP)
        self.base = self.s - self.part

    def near(self, mask):
        return (self.base + jnp.bitwise_xor(self.part, mask), self.z)

    def up(self, d):
        return (self.s, lax.rem(self.z + d, self.fsdp_size))

    def barrier(self):
        bar = pltpu.get_barrier_semaphore()

        def greet(i, carry):
            peer = lax.rem(self.s + i, self.seq_size)
            pl.semaphore_signal(bar, inc=1, device_id=(peer, self.z), device_id_type=MESH)
            return carry

        lax.fori_loop(1, self.seq_size, greet, 0)
        for d in range(1, self.fsdp_size):
            pl.semaphore_signal(bar, inc=1, device_id=self.up(d), device_id_type=MESH)
        pl.semaphore_wait(bar, self.seq_size + self.fsdp_size - 2)


class Exchange:
    def __init__(self, place, mine, seq_slots, fsdp_slots, sems):
        self.place, self.mine = place, mine
        self.seq_slots, self.fsdp_slots = seq_slots, fsdp_slots
        self.seq_send, self.seq_recv, self.fsdp_send, self.fsdp_recv = sems

    def _copy(self, i, stage):
        at = self.place
        if stage == 0:
            peer = lax.rem(at.s + i, at.seq_size)
            source = lax.rem(at.s - i + at.seq_size, at.seq_size)
            device, slots, send, recv, me = (peer, at.z), self.seq_slots, self.seq_send, self.seq_recv, at.s
        else:
            peer = lax.rem(at.z + i, at.fsdp_size)
            source = lax.rem(at.z - i + at.fsdp_size, at.fsdp_size)
            device, slots, send, recv, me = (at.s, peer), self.fsdp_slots, self.fsdp_send, self.fsdp_recv, at.z
        make = lambda slot: pltpu.make_async_remote_copy(
            src_ref=self.mine.at[stage],
            dst_ref=slots.at[slot],
            send_sem=send.at[i],
            recv_sem=recv.at[i],
            device_id=device,
            device_id_type=MESH,
        )
        return functools.partial(make, me), functools.partial(make, source)

    def _each(self, stage, what):
        size = self.place.seq_size if stage == 0 else self.place.fsdp_size

        def run(i, carry):
            what(*self._copy(i, stage))
            return carry

        lax.fori_loop(1, size, run, 0)

    def start(self, block):
        self.mine[0] = block
        self.seq_slots[self.place.s] = block
        self._each(0, lambda out, into: out().start())

    def finish(self, combine):
        self._each(0, lambda out, into: into().wait_recv())
        block = combine(self.seq_slots)
        self.mine[1] = block
        self.fsdp_slots[self.place.z] = block
        self._each(1, lambda out, into: out().start())
        self._each(1, lambda out, into: into().wait_recv())
        block = combine(self.fsdp_slots)
        self._each(0, lambda out, into: out().wait_send())
        self._each(1, lambda out, into: out().wait_send())
        return block


def pack(first, second):
    width = first.shape[1] // 4
    pieces = [v[:, i * width : (i + 1) * width] for v in (first, second) for i in range(4)]
    return jnp.concatenate(pieces, axis=0)


def unpack(block):
    return [jnp.concatenate([block[4 * j + i : 4 * j + i + 1] for i in range(4)], axis=1) for j in range(2)]


def combine_sums(slots):
    return jnp.sum(slots[...], axis=0)


def combine_moments(slots):
    v = slots[...]
    center, spread = v[:, :4], v[:, 4:]
    mean = jnp.mean(center, axis=0)
    rest = jnp.mean(spread + jnp.square(center - mean[None]), axis=0)
    return jnp.concatenate([mean, rest], axis=0)


class Gather:
    def __init__(self, links, at, shard, full):
        self.links, self.at, self.shard, self.full = links, at, shard, full
        rows, self.width = shard.shape
        self.share = rows // GROUP

    def rows(self, part, half=None):
        start = part * self.share
        if half is None:
            return ds(start, self.share, 16)
        return ds(start + half * (self.share // 2), self.share // 2, 16)

    def columns(self, z):
        return ds(z * self.width, self.width, 128)

    def _plane(self, z, mask, of, half=None):
        part = self.at.part
        col = self.columns(z)
        mine = self.full.at[self.rows(jnp.bitwise_xor(part, of), half), col]
        theirs = self.full.at[self.rows(jnp.bitwise_xor(part, of ^ mask), half), col]
        return self.links.copy(mine, mine, theirs, self.at.near(mask)).start()

    def send(self, d):
        at = self.at
        src = self.shard.at[self.rows(at.part)]
        there = self.full.at[self.rows(at.part), self.columns(at.z)]
        source = lax.rem(at.z - d + at.fsdp_size, at.fsdp_size)
        here = self.full.at[self.rows(at.part), self.columns(source)]
        return self.links.copy(src, there, here, at.up(d)).start()

    def run(self, d, first):
        at = self.at
        z = lax.rem(at.z - d + at.fsdp_size, at.fsdp_size)
        held = {}

        def one():
            first[d].wait_recv()
            held["x"] = self._plane(z, 2, 0)
            held["y"] = self._plane(z, 4, 0)
            held["c"] = self._plane(z, 1, 0)
            if d + 1 < at.fsdp_size:
                first[d + 1] = self.send(d + 1)

        def two():
            held["x"].wait_recv()
            held["xa"] = self._plane(z, 4, 2, 0)
            held["xc"] = self._plane(z, 1, 2)

        def three():
            held["y"].wait_recv()
            held["yb"] = self._plane(z, 2, 4, 1)
            held["yc"] = self._plane(z, 1, 4)

        def four():
            held["xa"].wait_recv()
            held["ac"] = self._plane(z, 1, 6, 0)
            held["yb"].wait_recv()
            held["bc"] = self._plane(z, 1, 6, 1)

        def five():
            for name in ("c", "xc", "yc", "ac", "bc"):
                held[name].wait_recv()
            return z

        return one, two, three, four, five


def forward_kernel(
    sizes,
    features,
    conv_shard,
    mix_shard,
    row_pack,
    cotangent,
    scale,
    full_conv,
    full_mix,
    term_mix,
    term_pool,
    pooled,
    active_out,
    middle_low,
    vectors,
    ext,
    taps,
    wbuf,
    mixw,
    middle,
    deriv,
    work,
    a2,
    low,
    low2,
    gbuf,
    pair_one,
    pair_two,
    mine,
    seq_slots,
    fsdp_slots,
    packs,
    send,
    recv,
    seq_send,
    seq_recv,
    fsdp_send,
    fsdp_recv,
    local,
):
    seq, fsdp = sizes
    at = Place(seq, fsdp)
    links = Links(send, recv)
    rows, cin = features.shape
    cout = full_conv.shape[1]
    width = cout // fsdp
    total = float(rows * seq * fsdp)
    taps_count = conv_shard.shape[0] // cin
    lead = 8

    def exchange(i):
        sems = (seq_send.at[i], seq_recv.at[i], fsdp_send.at[i], fsdp_recv.at[i])
        return Exchange(at, mine.at[i], seq_slots.at[i], fsdp_slots.at[i], sems)

    own_conv = pltpu.make_async_copy(conv_shard, full_conv.at[:, ds(at.z * width, width, 128)], local.at[0])
    own_mix = pltpu.make_async_copy(mix_shard, full_mix.at[:, ds(at.z * width, width, 128)], local.at[1])
    own_load = pltpu.make_async_copy(conv_shard, wbuf.at[0], local.at[2])

    at.barrier()
    conv = Gather(links, at, conv_shard, full_conv)
    mix = Gather(links, at, mix_shard, full_mix)
    first_conv, first_mix = {}, {}
    parcels = []
    for d in range(1, fsdp):
        source = lax.rem(at.z - d + fsdp, fsdp)
        parcels.append(links.copy(row_pack, packs.at[at.z], packs.at[source], at.up(d)).start())
    first_conv[1] = conv.send(1)
    own_load.start()
    own_conv.start()
    own_mix.start()
    steps_conv = {d: conv.run(d, first_conv) for d in range(1, fsdp)}
    steps_mix = {d: mix.run(d, first_mix) for d in range(1, fsdp)}

    (sum_one,) = row_sums(rows, 64, cin, 1, lambda r: (features[pl.ds(r, 64), :].astype(F32),))
    mean = sum_one / rows
    (dev_one,) = row_sums(rows, 64, cin, 1, lambda r: (jnp.square(features[pl.ds(r, 64), :].astype(F32) - mean),))
    pad = jnp.zeros((1, cout - cin), F32)
    stats = exchange(0)
    stats.start(pack(jnp.concatenate([mean, pad], axis=1), jnp.concatenate([dev_one / rows, pad], axis=1)))
    packs[at.z] = row_pack[...]
    for parcel in parcels:
        parcel.wait_recv()
    everyone = packs[...].astype(F32)
    params = jnp.sum(everyone[:, :8], axis=0)
    gain_one, shift_one = params[0:1, :cin], params[1:2, :cin]
    gain_two, shift_two, bias_one, bias_two = (params[i : i + 1] for i in range(2, 6))
    mean_one, var_one = unpack(stats.finish(combine_moments))
    mean_one, scale_one = mean_one[:, :cin], lax.rsqrt(var_one[:, :cin] + EPSILON)
    steps_conv[1][0]()

    def active(v):
        b = (v - mean_one) * scale_one * gain_one + shift_one
        return b * (0.5 * (1.0 + lax.erf(b * math.sqrt(0.5))))

    def first_active(r):
        v = active(features[pl.ds(r, 32), :].astype(F32)).astype(BF)
        active_out[pl.ds(r, 32), :] = v
        ext[pl.ds(lead + r, 32), :cin] = v.astype(F32)

    rows_loop(rows, 32, first_active)
    before = packs[lax.rem(at.z + fsdp - 1, fsdp)].astype(F32)[8:16, :cin]
    after = packs[lax.rem(at.z + 1, fsdp)].astype(F32)[8:16, :cin]
    row = lax.broadcasted_iota(jnp.int32, (8, cin), 0)
    ext[0:lead, :cin] = jnp.where((row >= 6) & (at.z > 0), active(before), 0.0)
    ext[lead + rows : lead + rows + 8, :cin] = jnp.where((row < 2) & (at.z < fsdp - 1), active(after), 0.0)
    steps_conv[1][1]()
    steps_conv[1][2]()

    def shifted(k):
        def body(i, carry):
            col = ds(i * 128, 128, 128)
            taps[:, ds(k * cin + i * 128, 128, 128)] = ext[pl.ds(lead - 2 + k, rows), col].astype(BF)
            return carry

        lax.fori_loop(0, cin // 128, body, 0)

    for k in range(taps_count):
        shifted(k)

    def load_block(slot, z):
        copy = pltpu.make_async_copy(full_conv.at[:, ds(z * width, width, 128)], wbuf.at[slot], local.at[3])
        copy.start()
        copy.wait()

    def multiply(slot, z):
        middle[:, ds(z * width, width, 128)] = dot(taps[...], wbuf[slot], 1, 0)

    own_load.wait()
    multiply(0, at.z)
    order = []
    for d in range(1, fsdp):
        one, two, three, four, five = steps_conv[d]
        if d > 1:
            two()
            three()
        four()
        if d + 1 < fsdp:
            steps_conv[d + 1][0]()
        else:
            first_mix[1] = mix.send(1)
        z = five()
        load_block(d % 2, z)
        multiply(d % 2, z)

    steps_mix[1][0]()

    def plus_bias(r):
        v = middle[pl.ds(r, 32), :] + bias_one
        middle[pl.ds(r, 32), :] = v
        return (v,)

    (sum_two,) = row_sums(rows, 32, cout, 1, plus_bias)
    mean = sum_two / rows
    (dev_two,) = row_sums(rows, 32, cout, 1, lambda r: (jnp.square(middle[pl.ds(r, 32), :] - mean),))
    stats = exchange(1)
    stats.start(pack(mean, dev_two / rows))
    steps_mix[1][1]()
    steps_mix[1][2]()
    mean_two, var_two = unpack(stats.finish(combine_moments))
    scale_two = lax.rsqrt(var_two + EPSILON)
    steps_mix[1][3]()
    steps_mix[2][0]()

    def second_active(r):
        b = (middle[pl.ds(r, 32), :] - mean_two) * scale_two * gain_two + shift_two
        cdf, slope = normal(b)
        a2[pl.ds(r, 32), :] = (b * cdf).astype(BF)
        deriv[pl.ds(r, 32), :] = slope

    rows_loop(rows, 32, second_active)
    steps_mix[1][4]()
    for d in range(2, fsdp):
        steps_mix[d][1]()
        steps_mix[d][2]()
        if d + 1 < fsdp:
            steps_mix[d + 1][0]()
        steps_mix[d][3]()
        steps_mix[d][4]()
    own_mix.wait()
    load = pltpu.make_async_copy(full_mix, mixw, local.at[3])
    load.start()
    load.wait()

    tile = 512
    tiles = cout // tile

    def column_loop(body):
        def run(i, carry):
            body(ds(i * tile, tile, 128))
            return carry

        lax.fori_loop(0, tiles, run, 0)

    def add_mix(col):
        work[:, col] = dot(a2[...], mixw[0:cout, col], 1, 0)

    column_loop(add_mix)

    def add_residual(r):
        v = middle[pl.ds(r, 32), :] + work[pl.ds(r, 32), :] + bias_two
        ext[pl.ds(r, 32), :] = v
        low[pl.ds(r, 32), :] = v.astype(BF)

    rows_loop(rows, 32, add_residual)

    def add_pool(col):
        work[:, col] = dot(low[...], mixw[cout : 2 * cout, col], 1, 0)

    column_loop(add_pool)

    def pairs(i, carry):
        col = ds(i * 128, 128, 128)
        even, odd = pl.ds(0, rows // 2, 2), pl.ds(1, rows // 2, 2)
        one, two = pair_one, pair_two
        one[...], two[...] = work[:, col], ext[0:rows, col]
        l0, l1 = one[even, :], one[odd, :]
        s0, s1 = two[even, :], two[odd, :]
        top = jnp.maximum(l0, l1)
        e0, e1 = jnp.exp(l0 - top), jnp.exp(l1 - top)
        inverse = 1.0 / (e0 + e1)
        w0, w1 = e0 * inverse, e1 * inverse
        up = cotangent[:, col].astype(F32) * scale[:, col]
        pooled[:, col] = (w0 * s0 + w1 * s1).astype(BF)
        g0, g1 = s0 * up, s1 * up
        both = w0 * g0 + w1 * g1
        one[even, :] = w0 * up
        one[odd, :] = w1 * up
        two[even, :] = w0 * (g0 - both)
        two[odd, :] = w1 * (g1 - both)
        work[:, col] = one[...]
        low2[:, col] = two[...].astype(BF)
        return carry

    lax.fori_loop(0, cout // 128, pairs, 0)

    def product(left, right):
        def body(i, carry):
            part = ds(i * tile, tile, 128)
            gbuf[part, :] = dot(left[:, part], right[...], 0, 0).astype(BF)
            return carry

        lax.fori_loop(0, tiles, body, 0)

    product(low, low2)
    out_pool = pltpu.make_async_copy(gbuf, term_pool, local.at[4])
    out_pool.start()

    def back_pool(col):
        ext[0:rows, col] = dot(low2[...], mixw[ds(cout + col.start, tile, 128), :], 1, 1)

    column_loop(back_pool)

    def grad_summed(r):
        v = work[pl.ds(r, 32), :] + ext[pl.ds(r, 32), :]
        work[pl.ds(r, 32), :] = v
        low[pl.ds(r, 32), :] = v.astype(BF)
        return (v,)

    (sum_bias_two,) = row_sums(rows, 32, cout, 1, grad_summed)

    def back_mix(col):
        ext[0:rows, col] = dot(low[...], mixw[ds(col.start, tile, 128), :], 1, 1)

    column_loop(back_mix)

    def normed(r):
        return (middle[pl.ds(r, 32), :] - mean_two) * scale_two

    def grad_before(r):
        v = ext[pl.ds(r, 32), :] * deriv[pl.ds(r, 32), :]
        ext[pl.ds(r, 32), :] = v
        return v, v * normed(r)

    sum_shift, sum_gain = row_sums(rows, 32, cout, 2, grad_before)
    stats = exchange(2)
    stats.start(pack(sum_shift, sum_gain))
    out_pool.wait()
    product(a2, low)
    out_mix = pltpu.make_async_copy(gbuf, term_mix, local.at[4])
    out_mix.start()
    shift_two_grad, gain_two_grad = unpack(stats.finish(combine_sums))

    def grad_middle(r):
        v = work[pl.ds(r, 32), :] + gain_two * scale_two * (
            ext[pl.ds(r, 32), :] - shift_two_grad / total - normed(r) * gain_two_grad / total
        )
        middle_low[pl.ds(r, 32), :] = v.astype(BF)
        return (v,)

    (sum_bias_one,) = row_sums(rows, 32, cout, 1, grad_middle)
    fill = lambda v: jnp.concatenate([v, pad], axis=1)
    vectors[0:8, :] = jnp.concatenate(
        [fill(mean_one), fill(scale_one), fill(gain_one), fill(shift_one), shift_two_grad, gain_two_grad, sum_bias_one, sum_bias_two],
        axis=0,
    )
    own_conv.wait()
    out_mix.wait()
    links.drain()


def run_forward(sizes, features, conv_shard, mix_shard, row_pack, cotangent, scale):
    seq, fsdp = sizes
    rows, cin = features.shape
    cout = conv_shard.shape[1] * fsdp
    deep = conv_shard.shape[0]
    two = mix_shard.shape[0]
    shape = jax.ShapeDtypeStruct
    vmem = pl.BlockSpec(memory_space=pltpu.VMEM)
    hbm = pl.BlockSpec(memory_space=pl.ANY)
    copies = 80
    return pl.pallas_call(
        functools.partial(forward_kernel, sizes),
        out_shape=(
            shape((deep, cout), BF),
            shape((two, cout), BF),
            shape((cout, cout), BF),
            shape((cout, cout), BF),
            shape((rows // 2, cout), BF),
            shape((rows, cin), BF),
            shape((rows, cout), BF),
            shape((8, cout), F32),
        ),
        in_specs=[vmem, hbm, hbm, vmem, vmem, vmem],
        out_specs=(hbm, hbm, hbm, hbm, vmem, vmem, vmem, vmem),
        scratch_shapes=[
            pltpu.VMEM((rows + 16, cout), F32),
            pltpu.VMEM((rows, deep), BF),
            pltpu.VMEM((2, deep, cout // fsdp), BF),
            pltpu.VMEM((two, cout), BF),
            pltpu.VMEM((rows, cout), F32),
            pltpu.VMEM((rows, cout), F32),
            pltpu.VMEM((rows, cout), F32),
            pltpu.VMEM((rows, cout), BF),
            pltpu.VMEM((rows, cout), BF),
            pltpu.VMEM((rows, cout), BF),
            pltpu.VMEM((cout, cout), BF),
            pltpu.VMEM((rows, 128), F32),
            pltpu.VMEM((rows, 128), F32),
            pltpu.VMEM((3, 2, 8, cout // 4), F32),
            pltpu.VMEM((3, seq, 8, cout // 4), F32),
            pltpu.VMEM((3, fsdp, 8, cout // 4), F32),
            pltpu.VMEM((fsdp, 16, cout), BF),
            pltpu.SemaphoreType.DMA((copies,)),
            pltpu.SemaphoreType.DMA((copies,)),
            pltpu.SemaphoreType.DMA((3, seq)),
            pltpu.SemaphoreType.DMA((3, seq)),
            pltpu.SemaphoreType.DMA((3, fsdp)),
            pltpu.SemaphoreType.DMA((3, fsdp)),
            pltpu.SemaphoreType.DMA((5,)),
        ],
        compiler_params=pltpu.CompilerParams(
            collective_id=0, has_side_effects=True, vmem_limit_bytes=62 * 2**20
        ),
    )(features, conv_shard, mix_shard, row_pack, cotangent, scale)


def parameter_pack(owner, features, first, second):
    cout = second[0].shape[0] * lax.axis_size("fsdp")
    out = jnp.zeros((16, cout), BF)
    block = jnp.stack(first)
    out = lax.dynamic_update_slice(out, block, (0, owner * block.shape[1]))
    block = jnp.stack(second)
    out = lax.dynamic_update_slice(out, block, (2, owner * block.shape[1]))
    rows, cin = features.shape
    out = out.at[8:10, :cin].set(features[0:2])
    return out.at[14:16, :cin].set(features[rows - 2 : rows])


def spread_sum(v):
    size = lax.axis_size("seq")
    bit = GROUP
    while bit < size:
        v = v + lax.ppermute(v, "seq", [(i, i ^ bit) for i in range(size)])
        bit *= 2
    return v


def extended(shard, axis, width):
    size, length = lax.axis_size(axis), shard.shape[0]
    up = [(i, (i + 1) % size) for i in range(size - 1)]
    down = [(j, i) for i, j in up]
    before = lax.ppermute(shard[length - width :], axis, up)
    after = lax.ppermute(shard[:width], axis, down)
    return jnp.concatenate([before, shard, after], axis=0)


def on_device(
    features,
    conv_weight,
    mix_weight,
    pool_weight,
    gain_first,
    shift_first,
    gain_second,
    shift_second,
    bias_conv,
    bias_mix,
    cotangent,
    track_counts,
):
    rows, cin = features.shape
    seq, fsdp = lax.axis_size("seq"), lax.axis_size("fsdp")
    total = float(rows * seq * fsdp)
    position = lax.axis_index(("seq", "fsdp"))
    owner = lax.axis_index("fsdp")
    window = position * rows // WIN
    width = conv_weight.shape[2]
    cout = width * fsdp
    taps = conv_weight.shape[0]
    scale = lax.dynamic_slice_in_dim(track_counts, window, 1).astype(F32) / TRACKS
    scale = jnp.broadcast_to(scale[:, None], (1, cout))
    row_pack = parameter_pack(
        owner, features, (gain_first, shift_first), (gain_second, shift_second, bias_conv, bias_mix)
    )
    full_conv, full_mix, term_mix, term_pool, pooled, active_one, middle_low, vectors = run_forward(
        (seq, fsdp),
        features,
        conv_weight.reshape(taps * cin, width),
        jnp.concatenate([mix_weight, pool_weight], axis=0),
        row_pack,
        cotangent,
        scale,
    )
    mean_one, scale_one, gain_one, shift_one = (vectors[i, :cin] for i in range(4))
    shift_two_grad, gain_two_grad, sum_bias_one, sum_bias_two = (vectors[i] for i in range(4, 8))
    normed_one = (features.astype(F32) - mean_one) * scale_one
    before_one = normed_one * gain_one + shift_one

    padded_one = extended(active_one, "fsdp", 2)
    padded_grad = extended(middle_low, "fsdp", 2)
    full_conv = full_conv.reshape(taps, cin, cout)
    term_conv = []
    grad_active = 0.0
    for k in range(taps):
        term_conv.append(
            jnp.einsum("pc,pd->cd", padded_one[k : k + rows], middle_low, preferred_element_type=F32).astype(BF)
        )
        begin = taps - 1 - k
        grad_active = grad_active + jnp.einsum(
            "pd,cd->pc", padded_grad[begin : begin + rows], full_conv[k], preferred_element_type=F32
        )
    def reduced(v):
        out = lax.psum_scatter(v, "fsdp", scatter_dimension=v.ndim - 1, tiled=True)
        out = lax.psum_scatter(out, "seq", scatter_dimension=v.ndim - 2, tiled=True)
        return lax.all_gather(out, "seq", axis=v.ndim - 2, tiled=True).astype(F32)

    grad_conv = reduced(jnp.stack(term_conv))
    grad_mix, grad_pool = reduced(term_mix), reduced(term_pool)
    cdf, slope = normal(before_one)
    grad_before = slope * grad_active
    sums = lax.psum(
        (jnp.sum(grad_before, axis=0), jnp.sum(grad_before * normed_one, axis=0), sum_bias_one, sum_bias_two),
        ("seq", "fsdp"),
    )
    shift_one_grad, gain_one_grad, bias_one_grad, bias_two_grad = sums
    grad_features = (
        gain_one * scale_one * (grad_before - shift_one_grad / total - normed_one * gain_one_grad / total)
    ).astype(BF)

    def share(v, size):
        return lax.dynamic_slice_in_dim(v, owner * size, size)

    first, second = gain_first.shape[0], gain_second.shape[0]
    return (
        pooled,
        grad_features,
        grad_conv,
        grad_mix,
        grad_pool,
        share(gain_one_grad, first),
        share(shift_one_grad, first),
        share(gain_two_grad, second),
        share(shift_two_grad, second),
        share(bias_one_grad, second),
        share(bias_two_grad, second),
    )


def solution(mesh):
    rows = P(("seq", "fsdp"), None)
    vector = P("fsdp")
    in_specs = (rows, P(None, None, "fsdp"), P(None, "fsdp"), P(None, "fsdp")) + (vector,) * 6 + (rows, P())
    out_specs = (rows, rows, P(None, None, "fsdp"), P(None, "fsdp"), P(None, "fsdp")) + (vector,) * 6
    return jax.shard_map(on_device, mesh=mesh, in_specs=in_specs, out_specs=out_specs, check_vma=False)
```

```python
import functools
import math
import jax
import jax.numpy as jnp
from jax import lax
from jax.experimental import pallas as pl
from jax.experimental.pallas import tpu as pltpu
from jax.sharding import PartitionSpec as P

TRACKS = 5313
WIN = 2048
EPSILON = 1e-05
MESH = pl.DeviceIdType.MESH
BF = jnp.bfloat16
F32 = jnp.float32
GROUP = 8


def dot(a, b, ca, cb):
    return lax.dot_general(a, b, (((ca,), (cb,)), ((), ())), preferred_element_type=F32)


def ds(start, size, step):
    return pl.ds(pl.multiple_of(start, step), size)


def fold(v):
    rows, width = v.shape
    return jnp.sum(v.reshape(rows // 8, 8, width), axis=0)


def rows_loop(total, step, body):
    def run(i, carry):
        body(pl.multiple_of(i * step, step))
        return carry

    lax.fori_loop(0, total // step, run, 0)


def row_sums(total, step, width, count, body):
    def run(i, carry):
        parts = body(pl.multiple_of(i * step, step))
        return tuple(c + fold(v) for c, v in zip(carry, parts))

    zero = tuple(jnp.zeros((8, width), F32) for _ in range(count))
    sums = lax.fori_loop(0, total // step, run, zero)
    return [jnp.sum(v, axis=0, keepdims=True) for v in sums]


def normal(b):
    cdf = 0.5 * (1.0 + lax.erf(b * math.sqrt(0.5)))
    pdf = jnp.exp(-0.5 * b * b) * (1.0 / math.sqrt(2.0 * math.pi))
    return cdf, cdf + b * pdf


class Copy:
    def __init__(self, links, src, there, here, device):
        i = links.count
        links.count += 1
        send, recv = links.send.at[i], links.recv.at[i]

        def make(dst):
            return pltpu.make_async_remote_copy(
                src_ref=src,
                dst_ref=dst,
                send_sem=send,
                recv_sem=recv,
                device_id=device,
                device_id_type=MESH,
            )

        self.links = links
        self.out, self.into = functools.partial(make, there), functools.partial(make, here)

    def start(self):
        self.out().start()
        self.links.started.append(self)
        return self

    def wait_recv(self):
        self.into().wait_recv()

    def wait_send(self):
        self.out().wait_send()


class Links:
    def __init__(self, send, recv):
        self.send, self.recv = send, recv
        self.count = 0
        self.started = []

    def copy(self, src, there, here, device):
        return Copy(self, src, there, here, device)

    def drain(self):
        for item in self.started:
            item.wait_send()
        self.started = []


class Place:
    def __init__(self, seq, fsdp):
        self.seq_size, self.fsdp_size = seq, fsdp
        self.s, self.z = lax.axis_index("seq"), lax.axis_index("fsdp")
        self.part = lax.rem(self.s, GROUP)
        self.base = self.s - self.part

    def near(self, mask):
        return (self.base + jnp.bitwise_xor(self.part, mask), self.z)

    def up(self, d):
        return (self.s, lax.rem(self.z + d, self.fsdp_size))

    def barrier(self):
        bar = pltpu.get_barrier_semaphore()

        def greet(i, carry):
            peer = lax.rem(self.s + i, self.seq_size)
            pl.semaphore_signal(bar, inc=1, device_id=(peer, self.z), device_id_type=MESH)
            return carry

        lax.fori_loop(1, self.seq_size, greet, 0)
        for d in range(1, self.fsdp_size):
            pl.semaphore_signal(bar, inc=1, device_id=self.up(d), device_id_type=MESH)
        pl.semaphore_wait(bar, self.seq_size + self.fsdp_size - 2)


class Exchange:
    def __init__(self, place, mine, seq_slots, fsdp_slots, sems):
        self.place, self.mine = place, mine
        self.seq_slots, self.fsdp_slots = seq_slots, fsdp_slots
        self.seq_send, self.seq_recv, self.fsdp_send, self.fsdp_recv = sems

    def _copy(self, i, stage):
        at = self.place
        if stage == 0:
            peer = lax.rem(at.s + i, at.seq_size)
            source = lax.rem(at.s - i + at.seq_size, at.seq_size)
            device, slots, send, recv, me = (peer, at.z), self.seq_slots, self.seq_send, self.seq_recv, at.s
        else:
            peer = lax.rem(at.z + i, at.fsdp_size)
            source = lax.rem(at.z - i + at.fsdp_size, at.fsdp_size)
            device, slots, send, recv, me = (at.s, peer), self.fsdp_slots, self.fsdp_send, self.fsdp_recv, at.z
        make = lambda slot: pltpu.make_async_remote_copy(
            src_ref=self.mine.at[stage],
            dst_ref=slots.at[slot],
            send_sem=send.at[i],
            recv_sem=recv.at[i],
            device_id=device,
            device_id_type=MESH,
        )
        return functools.partial(make, me), functools.partial(make, source)

    def _each(self, stage, what):
        size = self.place.seq_size if stage == 0 else self.place.fsdp_size

        def run(i, carry):
            what(*self._copy(i, stage))
            return carry

        lax.fori_loop(1, size, run, 0)

    def start(self, block):
        self.mine[0] = block
        self.seq_slots[self.place.s] = block
        self._each(0, lambda out, into: out().start())

    def middle(self, combine):
        self._each(0, lambda out, into: into().wait_recv())
        block = combine(self.seq_slots)
        self.mine[1] = block
        self.fsdp_slots[self.place.z] = block
        self._each(1, lambda out, into: out().start())

    def end(self, combine):
        self._each(1, lambda out, into: into().wait_recv())
        block = combine(self.fsdp_slots)
        self._each(0, lambda out, into: out().wait_send())
        self._each(1, lambda out, into: out().wait_send())
        return block

    def finish(self, combine):
        self.middle(combine)
        return self.end(combine)


def pack(*vectors):
    width = vectors[0].shape[1] // 4
    pieces = [v[:, i * width : (i + 1) * width] for v in vectors for i in range(4)]
    return jnp.concatenate(pieces, axis=0)


def unpack(block):
    count = block.shape[0] // 4
    return [jnp.concatenate([block[4 * j + i : 4 * j + i + 1] for i in range(4)], axis=1) for j in range(count)]


def combine_sums(slots):
    return jnp.sum(slots[...], axis=0)


def combine_moments(slots):
    v = slots[...]
    center, spread = v[:, :4], v[:, 4:]
    mean = jnp.mean(center, axis=0)
    rest = jnp.mean(spread + jnp.square(center - mean[None]), axis=0)
    return jnp.concatenate([mean, rest], axis=0)


class Spread:
    def __init__(self, links, at, place, source=None):
        self.links, self.at, self.place, self.source = links, at, place, source
        self.held = {}

    def _send(self, name, mask, of, half=None):
        part = self.at.part
        mine = self.place(jnp.bitwise_xor(part, of), half)
        theirs = self.place(jnp.bitwise_xor(part, of ^ mask), half)
        src = mine if of or self.source is None else self.source
        self.held[name] = self.links.copy(src, mine, theirs, self.at.near(mask)).start()

    def one(self):
        self._send("x", 2, 0)
        self._send("y", 4, 0)
        self._send("c", 1, 0)

    def two(self):
        self.held["x"].wait_recv()
        self._send("xa", 4, 2, 0)
        self._send("xc", 1, 2)
        self.held["y"].wait_recv()
        self._send("yb", 2, 4, 1)
        self._send("yc", 1, 4)

    def three(self):
        self.held["xa"].wait_recv()
        self._send("ac", 1, 6, 0)
        self.held["yb"].wait_recv()
        self._send("bc", 1, 6, 1)

    def four(self):
        for name in ("c", "xc", "yc", "ac", "bc"):
            self.held[name].wait_recv()


class Gather:
    def __init__(self, links, at, shard, full):
        self.links, self.at, self.shard, self.full = links, at, shard, full
        rows, self.width = shard.shape
        self.share = rows // GROUP

    def rows(self, part, half=None):
        start = part * self.share
        if half is None:
            return ds(start, self.share, 16)
        return ds(start + half * (self.share // 2), self.share // 2, 16)

    def columns(self, z):
        return ds(z * self.width, self.width, 128)

    def send(self, d):
        at = self.at
        src = self.shard.at[self.rows(at.part)]
        there = self.full.at[self.rows(at.part), self.columns(at.z)]
        source = lax.rem(at.z - d + at.fsdp_size, at.fsdp_size)
        here = self.full.at[self.rows(at.part), self.columns(source)]
        return self.links.copy(src, there, here, at.up(d)).start()

    def run(self, d, first):
        at = self.at
        z = lax.rem(at.z - d + at.fsdp_size, at.fsdp_size)
        spread = Spread(self.links, at, lambda part, half: self.full.at[self.rows(part, half), self.columns(z)])

        def one():
            first[d].wait_recv()
            spread.one()
            if d + 1 < at.fsdp_size:
                first[d + 1] = self.send(d + 1)

        def four():
            spread.four()
            return z

        return one, spread.two, lambda: None, spread.three, four


def put_blocks(target, half, values, col):
    size = values.shape[0] // 8
    for i in range(8):
        part, side = 4 * half + i // 2, i % 2
        c, x, y = part & 1, part >> 1 & 1, part >> 2
        at = 8 * c + 4 * side + (2 * x + y if side == 0 else 2 * y + x)
        target[at * size : (at + 1) * size, col] = values[i * size : (i + 1) * size].astype(BF)


def forward_kernel(
    sizes,
    features,
    conv_shard,
    mix_shard,
    row_pack,
    cotangent,
    scale,
    full_conv,
    full_mix,
    term_mix,
    term_pool,
    pooled,
    active_out,
    middle_low,
    vectors,
    ext,
    taps,
    wbuf,
    mixw,
    middle,
    deriv,
    work,
    a2,
    low,
    low2,
    gbuf,
    pair_one,
    pair_two,
    mine,
    seq_slots,
    fsdp_slots,
    packs,
    send,
    recv,
    seq_send,
    seq_recv,
    fsdp_send,
    fsdp_recv,
    local,
):
    seq, fsdp = sizes
    at = Place(seq, fsdp)
    links = Links(send, recv)
    rows, cin = features.shape
    cout = full_conv.shape[1]
    width = cout // fsdp
    total = float(rows * seq * fsdp)
    taps_count = conv_shard.shape[0] // cin
    lead = 8

    def exchange(i):
        sems = (seq_send.at[i], seq_recv.at[i], fsdp_send.at[i], fsdp_recv.at[i])
        return Exchange(at, mine.at[i], seq_slots.at[i], fsdp_slots.at[i], sems)

    own_conv = pltpu.make_async_copy(wbuf.at[0], full_conv.at[:, ds(at.z * width, width, 128)], local.at[0])
    own_mix = pltpu.make_async_copy(mix_shard, mixw.at[:, ds(at.z * width, width, 128)], local.at[1])
    own_load = pltpu.make_async_copy(conv_shard, wbuf.at[0], local.at[2])

    at.barrier()
    conv = Gather(links, at, conv_shard, full_conv)
    mix = Gather(links, at, mix_shard, full_mix)
    first_conv, first_mix = {}, {}
    parcels = []
    for d in range(1, fsdp):
        source = lax.rem(at.z - d + fsdp, fsdp)
        parcels.append(links.copy(row_pack, packs.at[at.z], packs.at[source], at.up(d)).start())
    first_conv[1] = conv.send(1)
    own_load.start()
    own_mix.start()
    steps_conv = {d: conv.run(d, first_conv) for d in range(1, fsdp)}
    steps_mix = {d: mix.run(d, first_mix) for d in range(1, fsdp)}

    (sum_one,) = row_sums(rows, 64, cin, 1, lambda r: (features[pl.ds(r, 64), :].astype(F32),))
    mean = sum_one / rows
    (dev_one,) = row_sums(rows, 64, cin, 1, lambda r: (jnp.square(features[pl.ds(r, 64), :].astype(F32) - mean),))
    pad = jnp.zeros((1, cout - cin), F32)
    stats = exchange(0)
    stats.start(pack(jnp.concatenate([mean, pad], axis=1), jnp.concatenate([dev_one / rows, pad], axis=1)))
    packs[at.z] = row_pack[...]
    for parcel in parcels:
        parcel.wait_recv()
    everyone = packs[...].astype(F32)
    params = jnp.sum(everyone[:, :8], axis=0)
    gain_one, shift_one = params[0:1, :cin], params[1:2, :cin]
    gain_two, shift_two, bias_one, bias_two = (params[i : i + 1] for i in range(2, 6))
    mean_one, var_one = unpack(stats.finish(combine_moments))
    mean_one, scale_one = mean_one[:, :cin], lax.rsqrt(var_one[:, :cin] + EPSILON)
    steps_conv[1][0]()

    def active(v):
        b = (v - mean_one) * scale_one * gain_one + shift_one
        return b * (0.5 * (1.0 + lax.erf(b * math.sqrt(0.5))))

    def first_active(r):
        v = active(features[pl.ds(r, 32), :].astype(F32)).astype(BF)
        active_out[pl.ds(r, 32), :] = v
        ext[pl.ds(lead + r, 32), :cin] = v.astype(F32)

    rows_loop(rows, 32, first_active)
    before = packs[lax.rem(at.z + fsdp - 1, fsdp)].astype(F32)[8:16, :cin]
    after = packs[lax.rem(at.z + 1, fsdp)].astype(F32)[8:16, :cin]
    row = lax.broadcasted_iota(jnp.int32, (8, cin), 0)
    ext[0:lead, :cin] = jnp.where((row >= 6) & (at.z > 0), active(before), 0.0)
    ext[lead + rows : lead + rows + 8, :cin] = jnp.where((row < 2) & (at.z < fsdp - 1), active(after), 0.0)
    steps_conv[1][1]()
    steps_conv[1][2]()

    def shifted(k):
        def body(i, carry):
            col = ds(i * 128, 128, 128)
            taps[:, ds(k * cin + i * 128, 128, 128)] = ext[pl.ds(lead - 2 + k, rows), col].astype(BF)
            return carry

        lax.fori_loop(0, cin // 128, body, 0)

    for k in range(taps_count):
        shifted(k)

    def load_block(slot, z):
        copy = pltpu.make_async_copy(full_conv.at[:, ds(z * width, width, 128)], wbuf.at[slot], local.at[3])
        copy.start()
        copy.wait()

    def multiply(slot, z):
        middle[:, ds(z * width, width, 128)] = dot(taps[...], wbuf[slot], 1, 0)

    own_load.wait()
    own_conv.start()
    multiply(0, at.z)
    own_conv.wait()
    order = []
    for d in range(1, fsdp):
        one, two, three, four, five = steps_conv[d]
        if d > 1:
            two()
            three()
        four()
        if d + 1 < fsdp:
            steps_conv[d + 1][0]()
        else:
            first_mix[1] = mix.send(1)
        z = five()
        load_block(d % 2, z)
        multiply(d % 2, z)

    steps_mix[1][0]()

    def plus_bias(r):
        v = middle[pl.ds(r, 32), :] + bias_one
        middle[pl.ds(r, 32), :] = v
        return (v,)

    (sum_two,) = row_sums(rows, 32, cout, 1, plus_bias)
    mean = sum_two / rows
    (dev_two,) = row_sums(rows, 32, cout, 1, lambda r: (jnp.square(middle[pl.ds(r, 32), :] - mean),))
    stats = exchange(1)
    stats.start(pack(mean, dev_two / rows))
    steps_mix[1][1]()
    steps_mix[1][2]()
    mean_two, var_two = unpack(stats.finish(combine_moments))
    scale_two = lax.rsqrt(var_two + EPSILON)
    steps_mix[1][3]()
    steps_mix[2][0]()

    def second_active(r):
        b = (middle[pl.ds(r, 32), :] - mean_two) * scale_two * gain_two + shift_two
        cdf, slope = normal(b)
        a2[pl.ds(r, 32), :] = (b * cdf).astype(BF)
        deriv[pl.ds(r, 32), :] = slope

    rows_loop(rows, 32, second_active)
    steps_mix[1][4]()
    for d in range(2, fsdp):
        steps_mix[d][1]()
        steps_mix[d][2]()
        if d + 1 < fsdp:
            steps_mix[d + 1][0]()
        steps_mix[d][3]()
        steps_mix[d][4]()
    own_mix.wait()
    for d in range(1, fsdp):
        col = ds(lax.rem(at.z + d, fsdp) * width, width, 128)
        load = pltpu.make_async_copy(full_mix.at[:, col], mixw.at[:, col], local.at[3])
        load.start()
        load.wait()

    tile = 512
    tiles = cout // tile

    def column_loop(body):
        def run(i, carry):
            body(ds(i * tile, tile, 128))
            return carry

        lax.fori_loop(0, tiles, run, 0)

    def add_mix(col):
        work[:, col] = dot(a2[...], mixw[0:cout, col], 1, 0)

    column_loop(add_mix)

    def add_residual(r):
        v = middle[pl.ds(r, 32), :] + work[pl.ds(r, 32), :] + bias_two
        ext[pl.ds(r, 32), :] = v
        low[pl.ds(r, 32), :] = v.astype(BF)

    rows_loop(rows, 32, add_residual)

    def add_pool(col):
        work[:, col] = dot(low[...], mixw[cout : 2 * cout, col], 1, 0)

    column_loop(add_pool)

    def pairs(i, carry):
        col = ds(i * 128, 128, 128)
        even, odd = pl.ds(0, rows // 2, 2), pl.ds(1, rows // 2, 2)
        one, two = pair_one, pair_two
        one[...], two[...] = work[:, col], ext[0:rows, col]
        l0, l1 = one[even, :], one[odd, :]
        s0, s1 = two[even, :], two[odd, :]
        top = jnp.maximum(l0, l1)
        e0, e1 = jnp.exp(l0 - top), jnp.exp(l1 - top)
        inverse = 1.0 / (e0 + e1)
        w0, w1 = e0 * inverse, e1 * inverse
        up = cotangent[:, col].astype(F32) * scale[:, col]
        pooled[:, col] = (w0 * s0 + w1 * s1).astype(BF)
        g0, g1 = s0 * up, s1 * up
        both = w0 * g0 + w1 * g1
        one[even, :] = w0 * up
        one[odd, :] = w1 * up
        two[even, :] = w0 * (g0 - both)
        two[odd, :] = w1 * (g1 - both)
        work[:, col] = one[...]
        low2[:, col] = two[...].astype(BF)
        return carry

    lax.fori_loop(0, cout // 128, pairs, 0)

    def product(left, right):
        half = cout // 2
        for i in range(2):
            def body(j, carry):
                col = ds(j * tile, tile, 128)
                put_blocks(gbuf, i, dot(left[:, i * half : (i + 1) * half], right[:, col], 0, 0), col)
                return carry

            lax.fori_loop(0, tiles, body, 0)

    product(low, low2)
    out_pool = pltpu.make_async_copy(gbuf, term_pool, local.at[4])
    out_pool.start()

    def back_pool(col):
        ext[0:rows, col] = dot(low2[...], mixw[ds(cout + col.start, tile, 128), :], 1, 1)

    column_loop(back_pool)

    def grad_summed(r):
        v = work[pl.ds(r, 32), :] + ext[pl.ds(r, 32), :]
        work[pl.ds(r, 32), :] = v
        low[pl.ds(r, 32), :] = v.astype(BF)
        return (v,)

    (sum_bias_two,) = row_sums(rows, 32, cout, 1, grad_summed)

    def back_mix(col):
        ext[0:rows, col] = dot(low[...], mixw[ds(col.start, tile, 128), :], 1, 1)

    column_loop(back_mix)

    def normed(r):
        return (middle[pl.ds(r, 32), :] - mean_two) * scale_two

    def grad_before(r):
        v = ext[pl.ds(r, 32), :] * deriv[pl.ds(r, 32), :]
        ext[pl.ds(r, 32), :] = v
        return v, v * normed(r)

    sum_shift, sum_gain = row_sums(rows, 32, cout, 2, grad_before)
    stats = exchange(2)
    stats.start(pack(sum_shift, sum_gain))
    out_pool.wait()
    product(a2, low)
    out_mix = pltpu.make_async_copy(gbuf, term_mix, local.at[4])
    out_mix.start()
    shift_two_grad, gain_two_grad = unpack(stats.finish(combine_sums))

    def grad_middle(r):
        v = work[pl.ds(r, 32), :] + gain_two * scale_two * (
            ext[pl.ds(r, 32), :] - shift_two_grad / total - normed(r) * gain_two_grad / total
        )
        middle_low[pl.ds(r, 32), :] = v.astype(BF)
        return (v,)

    (sum_bias_one,) = row_sums(rows, 32, cout, 1, grad_middle)
    fill = lambda v: jnp.concatenate([v, pad], axis=1)
    vectors[0:8, :] = jnp.concatenate(
        [fill(mean_one), fill(scale_one), fill(gain_one), fill(shift_one), shift_two_grad, gain_two_grad, sum_bias_one, sum_bias_two],
        axis=0,
    )
    out_mix.wait()
    links.drain()


def run_forward(sizes, features, conv_shard, mix_shard, row_pack, cotangent, scale):
    seq, fsdp = sizes
    rows, cin = features.shape
    cout = conv_shard.shape[1] * fsdp
    deep = conv_shard.shape[0]
    two = mix_shard.shape[0]
    shape = jax.ShapeDtypeStruct
    vmem = pl.BlockSpec(memory_space=pltpu.VMEM)
    hbm = pl.BlockSpec(memory_space=pl.ANY)
    copies = 80
    return pl.pallas_call(
        functools.partial(forward_kernel, sizes),
        out_shape=(
            shape((deep, cout), BF),
            shape((two, cout), BF),
            shape((cout, cout), BF),
            shape((cout, cout), BF),
            shape((rows // 2, cout), BF),
            shape((rows, cin), BF),
            shape((rows, cout), BF),
            shape((8, cout), F32),
        ),
        in_specs=[vmem, hbm, hbm, vmem, vmem, vmem],
        out_specs=(hbm, hbm, hbm, hbm, vmem, vmem, vmem, vmem),
        scratch_shapes=[
            pltpu.VMEM((rows + 16, cout), F32),
            pltpu.VMEM((rows, deep), BF),
            pltpu.VMEM((2, deep, cout // fsdp), BF),
            pltpu.VMEM((two, cout), BF),
            pltpu.VMEM((rows, cout), F32),
            pltpu.VMEM((rows, cout), F32),
            pltpu.VMEM((rows, cout), F32),
            pltpu.VMEM((rows, cout), BF),
            pltpu.VMEM((rows, cout), BF),
            pltpu.VMEM((rows, cout), BF),
            pltpu.VMEM((cout, cout), BF),
            pltpu.VMEM((rows, 128), F32),
            pltpu.VMEM((rows, 128), F32),
            pltpu.VMEM((3, 2, 8, cout // 4), F32),
            pltpu.VMEM((3, seq, 8, cout // 4), F32),
            pltpu.VMEM((3, fsdp, 8, cout // 4), F32),
            pltpu.VMEM((fsdp, 16, cout), BF),
            pltpu.SemaphoreType.DMA((copies,)),
            pltpu.SemaphoreType.DMA((copies,)),
            pltpu.SemaphoreType.DMA((3, seq)),
            pltpu.SemaphoreType.DMA((3, seq)),
            pltpu.SemaphoreType.DMA((3, fsdp)),
            pltpu.SemaphoreType.DMA((3, fsdp)),
            pltpu.SemaphoreType.DMA((5,)),
        ],
        compiler_params=pltpu.CompilerParams(
            collective_id=0, has_side_effects=True, vmem_limit_bytes=62 * 2**20
        ),
    )(features, conv_shard, mix_shard, row_pack, cotangent, scale)


class Reduce:
    def __init__(self, links, at, unit, first, slot, buffers, core_slot, credit):
        self.links, self.at, self.unit, self.slot = links, at, unit, slot
        self.core_slot, self.credit = core_slot, credit
        self.from_x, self.from_y, self.from_yx, self.from_xy, self.own, self.from_z, self.total = (
            buffers[0].at[pl.ds(2 * first, 2 * unit)],
            buffers[1].at[pl.ds(2 * first, 2 * unit)],
            buffers[2].at[pl.ds(first, unit)],
            buffers[3].at[pl.ds(first, unit)],
            buffers[4].at[pl.ds(2 * first, 2 * unit)],
            buffers[5].at[:, pl.ds(2 * first, 2 * unit)],
            buffers[6].at[pl.ds(2 * first, 2 * unit)],
        )
        part = at.part
        self.c, self.x, self.y = part & 1, (part >> 1) & 1, part >> 2
        self.sent = []

    def _rows(self, start, count):
        return self.slot.at[ds(start * self.unit, count * self.unit, 16)]

    def _send(self, src, dst, device):
        copy = self.links.copy(src, dst, dst, device).start()
        self.links.started.remove(copy)
        self.sent.append(copy)
        return copy

    def core(self, wait_credit):
        if wait_credit:
            pl.semaphore_wait(self.credit, 1)
        dst = self.core_slot.at[pl.ds(0, 8 * self.unit)]
        self.by_core = self._send(self._rows((1 - self.c) * 8, 8), dst, self.at.near(1))

    def _add(self, start, other, count, out=None):
        step = 16
        mine = self._rows(start, count)
        out = mine if out is None else out

        def body(r):
            v = mine[pl.ds(r, step), :].astype(F32) + other[pl.ds(r, step), :].astype(F32)
            out[pl.ds(r, step), :] = v.astype(BF)

        rows_loop(count * self.unit, step, body)

    def plane(self, give_credit):
        self.by_core.wait_recv()
        self._add(self.c * 8, self.core_slot, 8)
        if give_credit:
            pl.semaphore_signal(self.credit, inc=1, device_id=self.at.near(1), device_id_type=MESH)
        self.a, self.b = self.c * 8, self.c * 8 + 4
        self.by_x = self._send(self._rows(self.a + (1 - self.x) * 2, 2), self.from_x, self.at.near(2))
        self.by_y = self._send(self._rows(self.b + (1 - self.y) * 2, 2), self.from_y, self.at.near(4))

    def cross(self):
        a, b = self.a + self.x * 2, self.b + self.y * 2
        self.by_x.wait_recv()
        self._add(a, self.from_x, 2)
        self.by_yx = self._send(self._rows(a + 1 - self.y, 1), self.from_yx, self.at.near(4))
        self.by_y.wait_recv()
        self._add(b, self.from_y, 2)
        self.by_xy = self._send(self._rows(b + 1 - self.x, 1), self.from_xy, self.at.near(2))
        self.a, self.b = a + self.y, b + self.x

    def depth(self):
        self.by_yx.wait_recv()
        self._add(self.a, self.from_yx, 1, self.own.at[pl.ds(0, self.unit)])
        self.by_xy.wait_recv()
        self._add(self.b, self.from_xy, 1, self.own.at[pl.ds(self.unit, self.unit)])
        width = self.total.shape[1]
        at = self.at
        self.by_z = []
        for d in range(1, at.fsdp_size):
            col = ds(lax.rem(at.z + d, at.fsdp_size) * width, width, 128)
            dst = self.from_z.at[d - 1]
            self.by_z.append(self.links.copy(self.own.at[:, col], dst, dst, at.up(d)).start())

    def finish(self):
        width = self.total.shape[1]
        col = ds(self.at.z * width, width, 128)
        for copy in self.by_z:
            copy.wait_recv()

        def body(r):
            v = self.own[pl.ds(r, 16), col].astype(F32)
            for d in range(self.at.fsdp_size - 1):
                v = v + self.from_z[d, pl.ds(r, 16), :].astype(F32)
            self.total[pl.ds(r, 16), :] = v.astype(BF)

        rows_loop(2 * self.unit, 16, body)

    def free(self):
        for copy in self.sent:
            copy.wait_send()
        self.sent = []


def backward_kernel(
    sizes,
    features,
    active_one,
    middle_low,
    vectors,
    full_conv,
    term_mix,
    term_pool,
    gathered,
    grad_features,
    sums_out,
    ext,
    shifted,
    weight,
    grad_active,
    slots,
    core_slots,
    from_x,
    from_y,
    from_yx,
    from_xy,
    own,
    from_z,
    total,
    edges,
    mine,
    seq_slots,
    fsdp_slots,
    send,
    recv,
    seq_send,
    seq_recv,
    fsdp_send,
    fsdp_recv,
    credits,
    local,
):
    seq, fsdp = sizes
    at = Place(seq, fsdp)
    links = Links(send, recv)
    rows, cin = features.shape
    cout = full_conv.shape[1]
    taps = full_conv.shape[0] // cin
    all_rows = float(rows * seq * fsdp)
    lead = 8
    buffers = (from_x, from_y, from_yx, from_xy, own, from_z, total)
    heights = [cout, cout] + [cin] * taps
    chunks, first = [], 0
    for i, height in enumerate(heights):
        unit = height // 16
        chunks.append(
            Reduce(links, at, unit, first, slots.at[i % 3], buffers, core_slots.at[i % 2], credits.at[i % 2])
        )
        first += unit
    share = 2 * first
    count = len(chunks)

    def load_weight(k):
        return pltpu.make_async_copy(full_conv.at[pl.ds(k * cin, cin)], weight.at[k % 2], local.at[k % 2])

    load_weight(0).start()
    loads = []
    for i, term in enumerate((term_pool, term_mix)):
        loads.append(pltpu.make_async_copy(term, slots.at[i], local.at[2 + i]))
        loads[i].start()
    at.barrier()
    below = links.copy(middle_low.at[pl.ds(0, 16)], edges.at[1], edges.at[1], at.up(fsdp - 1)).start()
    above = links.copy(middle_low.at[pl.ds(rows - 16, 16)], edges.at[0], edges.at[0], at.up(1)).start()

    def core(i):
        chunks[i].core(i >= 2)

    def plane(i):
        chunks[i].plane(i + 2 < count)

    for i in range(2):
        loads[i].wait()
        core(i)

    def widen(r):
        ext[pl.ds(lead + r, 32), :] = middle_low[pl.ds(r, 32), :].astype(F32)

    rows_loop(rows, 32, widen)
    below.wait_recv()
    above.wait_recv()
    ext[0:lead, :] = jnp.where(at.z > 0, edges[0].astype(F32)[8:16], 0.0)
    ext[lead + rows : lead + rows + 8, :] = jnp.where(at.z < fsdp - 1, edges[1].astype(F32)[0:8], 0.0)
    half_width = (taps - 1) // 2
    tile = 512

    def shift(k):
        start = lead + half_width - k

        def body(i, carry):
            col = ds(i * 128, 128, 128)
            shifted[:, col] = ext[pl.ds(start, rows), col].astype(BF)
            return carry

        lax.fori_loop(0, cout // 128, body, 0)

    def product(slot):
        half = cin // 2
        for i in range(2):

            def body(j, carry):
                col = ds(j * tile, tile, 128)
                put_blocks(slot, i, dot(active_one[:, i * half : (i + 1) * half], shifted[:, col], 0, 0), col)
                return carry

            lax.fori_loop(0, cout // tile, body, 0)

    def back(k):
        load_weight(k).wait()
        if k + 1 < taps:
            load_weight(k + 1).start()

        def body(j, carry):
            col = ds(j * 256, 256, 128)
            v = dot(shifted[...], weight[k % 2, col, :], 1, 1)
            grad_active[:, col] = v if k == 0 else grad_active[:, col] + v
            return carry

        lax.fori_loop(0, cin // 256, body, 0)

    groups = {}

    def spread(lo, hi):
        start = 2 * sum(c.unit for c in chunks[:lo])
        size = 2 * sum(c.unit for c in chunks[lo:hi])

        def place(part, half):
            if half is None:
                return gathered.at[ds(part * share + start, size, 16)]
            return gathered.at[ds(part * share + start + half * (size // 2), size // 2, 16)]

        groups[lo] = Spread(links, at, place, total.at[pl.ds(start, size)])
        groups[lo].one()

    plane(0)
    for k in range(taps):
        i = k + 2
        shift(k)
        if i >= 3:
            chunks[i - 3].depth()
            chunks[i - 3].free()
        product(slots.at[i % 3])
        core(i)
        plane(i - 1)
        chunks[i - 2].cross()
        back(k)
        if i >= 4:
            chunks[i - 4].finish()
        if i == 5:
            spread(0, 2)

    mean_one, scale_one, gain_one, shift_one = (vectors[i : i + 1, :cin] for i in range(4))

    def grad_before(r):
        normed = (features[pl.ds(r, 32), :].astype(F32) - mean_one) * scale_one
        v = normal(normed * gain_one + shift_one)[1] * grad_active[pl.ds(r, 32), :]
        grad_active[pl.ds(r, 32), :] = v
        return v, v * normed

    sum_shift, sum_gain = row_sums(rows, 32, cin, 2, grad_before)
    pad = jnp.zeros((1, cout - cin), F32)
    wide = lambda v: jnp.concatenate([v, pad], axis=1)
    sems = (seq_send, seq_recv, fsdp_send, fsdp_recv)
    stats = Exchange(at, mine, seq_slots, fsdp_slots, sems)
    stats.start(pack(wide(sum_shift), wide(sum_gain), vectors[6:7, :], vectors[7:8, :]))
    plane(count - 1)
    chunks[count - 2].cross()
    stats.middle(combine_sums)
    groups[0].two()
    chunks[count - 3].depth()
    chunks[count - 4].finish()
    chunks[count - 1].cross()
    spread(2, count - 3)
    groups[0].three()
    chunks[count - 2].depth()
    chunks[count - 3].finish()
    everyone = unpack(stats.end(combine_sums))
    shift_grad, gain_grad = everyone[0][:, :cin], everyone[1][:, :cin]

    def store(r):
        normed = (features[pl.ds(r, 32), :].astype(F32) - mean_one) * scale_one
        v = grad_active[pl.ds(r, 32), :] - shift_grad / all_rows - normed * gain_grad / all_rows
        grad_features[pl.ds(r, 32), :] = (gain_one * scale_one * v).astype(BF)

    rows_loop(rows, 32, store)
    sums_out[0:4, :] = jnp.concatenate(everyone, axis=0)
    chunks[count - 1].depth()
    groups[2].two()
    chunks[count - 2].finish()
    groups[2].three()
    chunks[count - 1].finish()
    spread(count - 3, count)
    keep = pltpu.make_async_copy(total, gathered.at[ds(at.part * share, share, 16)], local.at[4])
    keep.start()
    groups[0].four()
    groups[2].four()
    groups[count - 3].two()
    groups[count - 3].three()
    groups[count - 3].four()
    keep.wait()
    for chunk in chunks:
        chunk.free()
    links.drain()


def run_backward(sizes, features, active_one, middle_low, vectors, full_conv, term_mix, term_pool):
    seq, fsdp = sizes
    rows, cin = features.shape
    deep, cout = full_conv.shape
    width = cout // fsdp
    share = (deep + 2 * cout) // GROUP
    shape = jax.ShapeDtypeStruct
    vmem = pl.BlockSpec(memory_space=pltpu.VMEM)
    hbm = pl.BlockSpec(memory_space=pl.ANY)
    copies = 160
    return pl.pallas_call(
        functools.partial(backward_kernel, sizes),
        out_shape=(shape((GROUP * share, width), BF), shape((rows, cin), BF), shape((8, cout), F32)),
        in_specs=[vmem, vmem, vmem, vmem, hbm, hbm, hbm],
        out_specs=(hbm, vmem, vmem),
        scratch_shapes=[
            pltpu.VMEM((rows + 16, cout), F32),
            pltpu.VMEM((rows, cout), BF),
            pltpu.VMEM((2, cin, cout), BF),
            pltpu.VMEM((rows, cin), F32),
            pltpu.VMEM((3, cout, cout), BF),
            pltpu.VMEM((2, cout // 2, cout), BF),
            pltpu.VMEM((share, cout), BF),
            pltpu.VMEM((share, cout), BF),
            pltpu.VMEM((share // 2, cout), BF),
            pltpu.VMEM((share // 2, cout), BF),
            pltpu.VMEM((share, cout), BF),
            pltpu.VMEM((fsdp - 1, share, width), BF),
            pltpu.VMEM((share, width), BF),
            pltpu.VMEM((2, 16, cout), BF),
            pltpu.VMEM((2, 16, cout // 4), F32),
            pltpu.VMEM((seq, 16, cout // 4), F32),
            pltpu.VMEM((fsdp, 16, cout // 4), F32),
            pltpu.SemaphoreType.DMA((copies,)),
            pltpu.SemaphoreType.DMA((copies,)),
            pltpu.SemaphoreType.DMA((seq,)),
            pltpu.SemaphoreType.DMA((seq,)),
            pltpu.SemaphoreType.DMA((fsdp,)),
            pltpu.SemaphoreType.DMA((fsdp,)),
            pltpu.SemaphoreType.REGULAR((2,)),
            pltpu.SemaphoreType.DMA((5,)),
        ],
        compiler_params=pltpu.CompilerParams(
            collective_id=1, has_side_effects=True, vmem_limit_bytes=62 * 2**20
        ),
    )(features, active_one, middle_low, vectors, full_conv, term_mix, term_pool)


def parameter_pack(owner, features, first, second):
    cout = second[0].shape[0] * lax.axis_size("fsdp")
    out = jnp.zeros((16, cout), BF)
    block = jnp.stack(first)
    out = lax.dynamic_update_slice(out, block, (0, owner * block.shape[1]))
    block = jnp.stack(second)
    out = lax.dynamic_update_slice(out, block, (2, owner * block.shape[1]))
    rows, cin = features.shape
    out = out.at[8:10, :cin].set(features[0:2])
    return out.at[14:16, :cin].set(features[rows - 2 : rows])


def spread_sum(v):
    size = lax.axis_size("seq")
    bit = GROUP
    while bit < size:
        v = v + lax.ppermute(v, "seq", [(i, i ^ bit) for i in range(size)])
        bit *= 2
    return v


def on_device(
    features,
    conv_weight,
    mix_weight,
    pool_weight,
    gain_first,
    shift_first,
    gain_second,
    shift_second,
    bias_conv,
    bias_mix,
    cotangent,
    track_counts,
):
    rows, cin = features.shape
    seq, fsdp = lax.axis_size("seq"), lax.axis_size("fsdp")
    position = lax.axis_index(("seq", "fsdp"))
    owner = lax.axis_index("fsdp")
    window = position * rows // WIN
    width = conv_weight.shape[2]
    cout = width * fsdp
    taps = conv_weight.shape[0]
    scale = lax.dynamic_slice_in_dim(track_counts, window, 1).astype(F32) / TRACKS
    scale = jnp.broadcast_to(scale[:, None], (1, cout))
    row_pack = parameter_pack(
        owner, features, (gain_first, shift_first), (gain_second, shift_second, bias_conv, bias_mix)
    )
    full_conv, full_mix, term_mix, term_pool, pooled, active_one, middle_low, vectors = run_forward(
        (seq, fsdp),
        features,
        conv_weight.reshape(taps * cin, width),
        jnp.concatenate([mix_weight, pool_weight], axis=0),
        row_pack,
        cotangent,
        scale,
    )
    gathered, grad_features, sums = run_backward(
        (seq, fsdp), features, active_one, middle_low, vectors, full_conv, term_mix, term_pool
    )
    parts = spread_sum(gathered.reshape(GROUP, -1, width).astype(F32))
    taken = 0
    products = []
    for height in [cout, cout] + [cin] * taps:
        size = height // GROUP
        products.append(parts[:, taken : taken + size].reshape(height, width))
        taken += size
    grad_pool, grad_mix = products[:2]
    grad_conv = jnp.stack(products[2:])
    shift_two_grad, gain_two_grad = vectors[4], vectors[5]
    shift_one_grad, gain_one_grad, bias_one_grad, bias_two_grad = sums[0], sums[1], sums[2], sums[3]

    def share(v, size):
        return lax.dynamic_slice_in_dim(v, owner * size, size)

    first, second = gain_first.shape[0], gain_second.shape[0]
    return (
        pooled,
        grad_features,
        grad_conv,
        grad_mix,
        grad_pool,
        share(gain_one_grad, first),
        share(shift_one_grad, first),
        share(gain_two_grad, second),
        share(shift_two_grad, second),
        share(bias_one_grad, second),
        share(bias_two_grad, second),
    )


def solution(mesh):
    rows = P(("seq", "fsdp"), None)
    vector = P("fsdp")
    in_specs = (rows, P(None, None, "fsdp"), P(None, "fsdp"), P(None, "fsdp")) + (vector,) * 6 + (rows, P())
    out_specs = (rows, rows, P(None, None, "fsdp"), P(None, "fsdp"), P(None, "fsdp")) + (vector,) * 6
    return jax.shard_map(on_device, mesh=mesh, in_specs=in_specs, out_specs=out_specs, check_vma=False)
```

```python
import functools
import math
import jax
import jax.numpy as jnp
from jax import lax
from jax.experimental import pallas as pl
from jax.experimental.pallas import tpu as pltpu
from jax.sharding import PartitionSpec as P

TRACKS = 5313
WIN = 2048
EPSILON = 1e-05
MESH = pl.DeviceIdType.MESH
BF = jnp.bfloat16
F32 = jnp.float32
GROUP = 8


def dot(a, b, ca, cb):
    return lax.dot_general(a, b, (((ca,), (cb,)), ((), ())), preferred_element_type=F32)


def ds(start, size, step):
    return pl.ds(pl.multiple_of(start, step), size)


def fold(v):
    rows, width = v.shape
    return jnp.sum(v.reshape(rows // 8, 8, width), axis=0)


def rows_loop(total, step, body):
    def run(i, carry):
        body(pl.multiple_of(i * step, step))
        return carry

    lax.fori_loop(0, total // step, run, 0)


def row_sums(total, step, width, count, body):
    def run(i, carry):
        parts = body(pl.multiple_of(i * step, step))
        return tuple(c + fold(v) for c, v in zip(carry, parts))

    zero = tuple(jnp.zeros((8, width), F32) for _ in range(count))
    sums = lax.fori_loop(0, total // step, run, zero)
    return [jnp.sum(v, axis=0, keepdims=True) for v in sums]


def normal(b):
    cdf = 0.5 * (1.0 + lax.erf(b * math.sqrt(0.5)))
    pdf = jnp.exp(-0.5 * b * b) * (1.0 / math.sqrt(2.0 * math.pi))
    return cdf, cdf + b * pdf


class Copy:
    def __init__(self, links, src, there, here, device):
        i = links.count
        links.count += 1
        send, recv = links.send.at[i], links.recv.at[i]

        def make(dst):
            return pltpu.make_async_remote_copy(
                src_ref=src,
                dst_ref=dst,
                send_sem=send,
                recv_sem=recv,
                device_id=device,
                device_id_type=MESH,
            )

        self.links = links
        self.out, self.into = functools.partial(make, there), functools.partial(make, here)

    def start(self):
        self.out().start()
        self.links.started.append(self)
        return self

    def wait_recv(self):
        self.into().wait_recv()

    def wait_send(self):
        self.out().wait_send()


class Links:
    def __init__(self, send, recv):
        self.send, self.recv = send, recv
        self.count = 0
        self.started = []

    def copy(self, src, there, here, device):
        return Copy(self, src, there, here, device)

    def drain(self):
        for item in self.started:
            item.wait_send()
        self.started = []


class Place:
    def __init__(self, seq, fsdp):
        self.seq_size, self.fsdp_size = seq, fsdp
        self.s, self.z = lax.axis_index("seq"), lax.axis_index("fsdp")
        self.part = lax.rem(self.s, GROUP)
        self.base = self.s - self.part
        self.c, self.x, self.y = self.part & 1, (self.part >> 1) & 1, self.part >> 2

    def near(self, mask):
        return (self.base + jnp.bitwise_xor(self.part, mask), self.z)

    def up(self, d):
        return (self.s, lax.rem(self.z + d, self.fsdp_size))

    def barrier(self):
        bar = pltpu.get_barrier_semaphore()

        def greet(i, carry):
            peer = lax.rem(self.s + i, self.seq_size)
            pl.semaphore_signal(bar, inc=1, device_id=(peer, self.z), device_id_type=MESH)
            return carry

        lax.fori_loop(1, self.seq_size, greet, 0)
        for d in range(1, self.fsdp_size):
            pl.semaphore_signal(bar, inc=1, device_id=self.up(d), device_id_type=MESH)
        pl.semaphore_wait(bar, self.seq_size + self.fsdp_size - 2)


class Exchange:
    def __init__(self, place, mine, seq_slots, fsdp_slots, sems):
        self.place, self.mine = place, mine
        self.seq_slots, self.fsdp_slots = seq_slots, fsdp_slots
        self.seq_send, self.seq_recv, self.fsdp_send, self.fsdp_recv = sems

    def _copy(self, i, stage):
        at = self.place
        if stage == 0:
            peer = lax.rem(at.s + i, at.seq_size)
            source = lax.rem(at.s - i + at.seq_size, at.seq_size)
            device, slots, send, recv, me = (peer, at.z), self.seq_slots, self.seq_send, self.seq_recv, at.s
        else:
            peer = lax.rem(at.z + i, at.fsdp_size)
            source = lax.rem(at.z - i + at.fsdp_size, at.fsdp_size)
            device, slots, send, recv, me = (at.s, peer), self.fsdp_slots, self.fsdp_send, self.fsdp_recv, at.z
        make = lambda slot: pltpu.make_async_remote_copy(
            src_ref=self.mine.at[stage],
            dst_ref=slots.at[slot],
            send_sem=send.at[i],
            recv_sem=recv.at[i],
            device_id=device,
            device_id_type=MESH,
        )
        return functools.partial(make, me), functools.partial(make, source)

    def _each(self, stage, what):
        size = self.place.seq_size if stage == 0 else self.place.fsdp_size

        def run(i, carry):
            what(*self._copy(i, stage))
            return carry

        lax.fori_loop(1, size, run, 0)

    def start(self, block):
        self.mine[0] = block
        self.seq_slots[self.place.s] = block
        self._each(0, lambda out, into: out().start())

    def middle(self, combine):
        self._each(0, lambda out, into: into().wait_recv())
        block = combine(self.seq_slots)
        self.mine[1] = block
        self.fsdp_slots[self.place.z] = block
        self._each(1, lambda out, into: out().start())

    def end(self, combine):
        self._each(1, lambda out, into: into().wait_recv())
        block = combine(self.fsdp_slots)
        self._each(0, lambda out, into: out().wait_send())
        self._each(1, lambda out, into: out().wait_send())
        return block

    def finish(self, combine):
        self.middle(combine)
        return self.end(combine)


def pack(*vectors):
    width = vectors[0].shape[1] // 4
    pieces = [v[:, i * width : (i + 1) * width] for v in vectors for i in range(4)]
    return jnp.concatenate(pieces, axis=0)


def unpack(block):
    count = block.shape[0] // 4
    return [jnp.concatenate([block[4 * j + i : 4 * j + i + 1] for i in range(4)], axis=1) for j in range(count)]


def combine_sums(slots):
    return jnp.sum(slots[...], axis=0)


def combine_moments(slots):
    v = slots[...]
    center, spread = v[:, :4], v[:, 4:]
    mean = jnp.mean(center, axis=0)
    rest = jnp.mean(spread + jnp.square(center - mean[None]), axis=0)
    return jnp.concatenate([mean, rest], axis=0)


class Spread:
    def __init__(self, links, at, place, source=None):
        self.links, self.at, self.place, self.source = links, at, place, source
        self.held = {}

    def _send(self, name, mask, of, half=None):
        part = self.at.part
        mine = self.place(jnp.bitwise_xor(part, of), half)
        theirs = self.place(jnp.bitwise_xor(part, of ^ mask), half)
        src = mine if of or self.source is None else self.source
        self.held[name] = self.links.copy(src, mine, theirs, self.at.near(mask)).start()

    def one(self):
        self._send("x", 2, 0)
        self._send("y", 4, 0)
        self._send("c", 1, 0)

    def two(self):
        self.held["x"].wait_recv()
        self._send("xa", 4, 2, 0)
        self._send("xc", 1, 2)
        self.held["y"].wait_recv()
        self._send("yb", 2, 4, 1)
        self._send("yc", 1, 4)

    def three(self):
        self.held["xa"].wait_recv()
        self._send("ac", 1, 6, 0)
        self.held["yb"].wait_recv()
        self._send("bc", 1, 6, 1)

    def four(self):
        for name in ("c", "xc", "yc", "ac", "bc"):
            self.held[name].wait_recv()


class Gather:
    def __init__(self, links, at, shard, full):
        self.links, self.at, self.shard, self.full = links, at, shard, full
        rows, self.width = shard.shape
        self.share = rows // GROUP

    def rows(self, part, half=None):
        start = part * self.share
        if half is None:
            return ds(start, self.share, 16)
        return ds(start + half * (self.share // 2), self.share // 2, 16)

    def columns(self, z):
        return ds(z * self.width, self.width, 128)

    def send(self, d):
        at = self.at
        src = self.shard.at[self.rows(at.part)]
        there = self.full.at[self.rows(at.part), self.columns(at.z)]
        source = lax.rem(at.z - d + at.fsdp_size, at.fsdp_size)
        here = self.full.at[self.rows(at.part), self.columns(source)]
        return self.links.copy(src, there, here, at.up(d)).start()

    def run(self, d, first):
        at = self.at
        z = lax.rem(at.z - d + at.fsdp_size, at.fsdp_size)
        spread = Spread(self.links, at, lambda part, half: self.full.at[self.rows(part, half), self.columns(z)])

        def one():
            first[d].wait_recv()
            spread.one()
            if d + 1 < at.fsdp_size:
                first[d + 1] = self.send(d + 1)

        def four():
            spread.four()
            return z

        return one, spread.two, lambda: None, spread.three, four


def put_blocks(target, half, values, col):
    size = values.shape[0] // 8
    for i in range(8):
        part, side = 4 * half + i // 2, i % 2
        c, x, y = part & 1, part >> 1 & 1, part >> 2
        at = 8 * c + 4 * side + (2 * x + y if side == 0 else 2 * y + x)
        target[at * size : (at + 1) * size, col] = values[i * size : (i + 1) * size].astype(BF)


def forward_kernel(
    sizes,
    features,
    conv_shard,
    mix_shard,
    row_pack,
    cotangent,
    scale,
    full_conv,
    full_mix,
    term_mix,
    active_x,
    active_y,
    pool_total,
    pooled,
    active_out,
    middle_low,
    vectors,
    ext,
    taps,
    wbuf,
    mixw,
    middle,
    deriv,
    work,
    a2,
    low,
    low2,
    gbuf,
    pair_one,
    pair_two,
    pool_core,
    pool_x,
    pool_y,
    pool_yx,
    pool_xy,
    pool_own,
    pool_z,
    mine,
    seq_slots,
    fsdp_slots,
    packs,
    send,
    recv,
    seq_send,
    seq_recv,
    fsdp_send,
    fsdp_recv,
    local,
):
    seq, fsdp = sizes
    at = Place(seq, fsdp)
    links = Links(send, recv)
    rows, cin = features.shape
    cout = full_conv.shape[1]
    width = cout // fsdp
    total = float(rows * seq * fsdp)
    taps_count = conv_shard.shape[0] // cin
    lead = 8

    def exchange(i):
        sems = (seq_send.at[i], seq_recv.at[i], fsdp_send.at[i], fsdp_recv.at[i])
        return Exchange(at, mine.at[i], seq_slots.at[i], fsdp_slots.at[i], sems)

    own_conv = pltpu.make_async_copy(wbuf.at[0], full_conv.at[:, ds(at.z * width, width, 128)], local.at[0])
    own_mix = pltpu.make_async_copy(mix_shard, mixw.at[:, ds(at.z * width, width, 128)], local.at[1])
    own_load = pltpu.make_async_copy(conv_shard, wbuf.at[0], local.at[2])

    at.barrier()
    conv = Gather(links, at, conv_shard, full_conv)
    mix = Gather(links, at, mix_shard, full_mix)
    first_conv, first_mix = {}, {}
    parcels = []
    for d in range(1, fsdp):
        source = lax.rem(at.z - d + fsdp, fsdp)
        parcels.append(links.copy(row_pack, packs.at[at.z], packs.at[source], at.up(d)).start())
    first_conv[1] = conv.send(1)
    own_load.start()
    own_mix.start()
    steps_conv = {d: conv.run(d, first_conv) for d in range(1, fsdp)}
    steps_mix = {d: mix.run(d, first_mix) for d in range(1, fsdp)}

    (sum_one,) = row_sums(rows, 64, cin, 1, lambda r: (features[pl.ds(r, 64), :].astype(F32),))
    mean = sum_one / rows
    (dev_one,) = row_sums(rows, 64, cin, 1, lambda r: (jnp.square(features[pl.ds(r, 64), :].astype(F32) - mean),))
    pad = jnp.zeros((1, cout - cin), F32)
    stats = exchange(0)
    stats.start(pack(jnp.concatenate([mean, pad], axis=1), jnp.concatenate([dev_one / rows, pad], axis=1)))
    packs[at.z] = row_pack[...]
    for parcel in parcels:
        parcel.wait_recv()
    everyone = packs[...].astype(F32)
    params = jnp.sum(everyone[:, :8], axis=0)
    gain_one, shift_one = params[0:1, :cin], params[1:2, :cin]
    gain_two, shift_two, bias_one, bias_two = (params[i : i + 1] for i in range(2, 6))
    mean_one, var_one = unpack(stats.finish(combine_moments))
    mean_one, scale_one = mean_one[:, :cin], lax.rsqrt(var_one[:, :cin] + EPSILON)
    steps_conv[1][0]()

    def active(v):
        b = (v - mean_one) * scale_one * gain_one + shift_one
        return b * (0.5 * (1.0 + lax.erf(b * math.sqrt(0.5))))

    def first_active(r):
        v = active(features[pl.ds(r, 32), :].astype(F32)).astype(BF)
        active_out[pl.ds(r, 32), :] = v
        ext[pl.ds(lead + r, 32), :cin] = v.astype(F32)

    rows_loop(rows, 32, first_active)
    before = packs[lax.rem(at.z + fsdp - 1, fsdp)].astype(F32)[8:16, :cin]
    after = packs[lax.rem(at.z + 1, fsdp)].astype(F32)[8:16, :cin]
    row = lax.broadcasted_iota(jnp.int32, (8, cin), 0)
    ext[0:lead, :cin] = jnp.where((row >= 6) & (at.z > 0), active(before), 0.0)
    ext[lead + rows : lead + rows + 8, :cin] = jnp.where((row < 2) & (at.z < fsdp - 1), active(after), 0.0)
    steps_conv[1][1]()
    steps_conv[1][2]()

    def shifted(k):
        def body(i, carry):
            col = ds(i * 128, 128, 128)
            taps[:, ds(k * cin + i * 128, 128, 128)] = ext[pl.ds(lead - 2 + k, rows), col].astype(BF)
            return carry

        lax.fori_loop(0, cin // 128, body, 0)

    for k in range(taps_count):
        shifted(k)

    def load_block(slot, z):
        copy = pltpu.make_async_copy(full_conv.at[:, ds(z * width, width, 128)], wbuf.at[slot], local.at[3])
        copy.start()
        copy.wait()

    def multiply(slot, z):
        middle[:, ds(z * width, width, 128)] = dot(taps[...], wbuf[slot], 1, 0)

    own_load.wait()
    own_conv.start()
    multiply(0, at.z)
    own_conv.wait()
    order = []
    for d in range(1, fsdp):
        one, two, three, four, five = steps_conv[d]
        if d > 1:
            two()
            three()
        four()
        if d + 1 < fsdp:
            steps_conv[d + 1][0]()
        else:
            first_mix[1] = mix.send(1)
        z = five()
        load_block(d % 2, z)
        multiply(d % 2, z)

    steps_mix[1][0]()

    def plus_bias(r):
        v = middle[pl.ds(r, 32), :] + bias_one
        middle[pl.ds(r, 32), :] = v
        return (v,)

    (sum_two,) = row_sums(rows, 32, cout, 1, plus_bias)
    mean = sum_two / rows
    (dev_two,) = row_sums(rows, 32, cout, 1, lambda r: (jnp.square(middle[pl.ds(r, 32), :] - mean),))
    stats = exchange(1)
    stats.start(pack(mean, dev_two / rows))
    steps_mix[1][1]()
    steps_mix[1][2]()
    mean_two, var_two = unpack(stats.finish(combine_moments))
    scale_two = lax.rsqrt(var_two + EPSILON)
    steps_mix[1][3]()
    steps_mix[2][0]()

    def second_active(r):
        b = (middle[pl.ds(r, 32), :] - mean_two) * scale_two * gain_two + shift_two
        cdf, slope = normal(b)
        a2[pl.ds(r, 32), :] = (b * cdf).astype(BF)
        deriv[pl.ds(r, 32), :] = slope

    rows_loop(rows, 32, second_active)
    steps_mix[1][4]()
    for d in range(2, fsdp):
        steps_mix[d][1]()
        steps_mix[d][2]()
        if d + 1 < fsdp:
            steps_mix[d + 1][0]()
        steps_mix[d][3]()
        steps_mix[d][4]()
    own_mix.wait()
    for d in range(1, fsdp):
        col = ds(lax.rem(at.z + d, fsdp) * width, width, 128)
        load = pltpu.make_async_copy(full_mix.at[:, col], mixw.at[:, col], local.at[3])
        load.start()
        load.wait()

    tile = 512
    tiles = cout // tile

    def column_loop(body):
        def run(i, carry):
            body(ds(i * tile, tile, 128))
            return carry

        lax.fori_loop(0, tiles, run, 0)

    def add_mix(col):
        work[:, col] = dot(a2[...], mixw[0:cout, col], 1, 0)

    half = cin // 2
    links.copy(active_out.at[:, ds((1 - at.x) * half, half, 128)], active_x, active_x, at.near(2)).start()
    links.copy(active_out.at[:, ds((1 - at.y) * half, half, 128)], active_y, active_y, at.near(4)).start()
    actives = links.started[-2:]
    column_loop(add_mix)

    def add_residual(r):
        v = middle[pl.ds(r, 32), :] + work[pl.ds(r, 32), :] + bias_two
        ext[pl.ds(r, 32), :] = v
        low[pl.ds(r, 32), :] = v.astype(BF)

    rows_loop(rows, 32, add_residual)

    def add_pool(col):
        work[:, col] = dot(low[...], mixw[cout : 2 * cout, col], 1, 0)

    column_loop(add_pool)

    def pairs(i, carry):
        col = ds(i * 128, 128, 128)
        even, odd = pl.ds(0, rows // 2, 2), pl.ds(1, rows // 2, 2)
        one, two = pair_one, pair_two
        one[...], two[...] = work[:, col], ext[0:rows, col]
        l0, l1 = one[even, :], one[odd, :]
        s0, s1 = two[even, :], two[odd, :]
        top = jnp.maximum(l0, l1)
        e0, e1 = jnp.exp(l0 - top), jnp.exp(l1 - top)
        inverse = 1.0 / (e0 + e1)
        w0, w1 = e0 * inverse, e1 * inverse
        up = cotangent[:, col].astype(F32) * scale[:, col]
        pooled[:, col] = (w0 * s0 + w1 * s1).astype(BF)
        g0, g1 = s0 * up, s1 * up
        both = w0 * g0 + w1 * g1
        one[even, :] = w0 * up
        one[odd, :] = w1 * up
        two[even, :] = w0 * (g0 - both)
        two[odd, :] = w1 * (g1 - both)
        work[:, col] = one[...]
        low2[:, col] = two[...].astype(BF)
        return carry

    lax.fori_loop(0, cout // 128, pairs, 0)

    def product(left, right, gbuf):
        half = cout // 2
        for i in range(2):
            def body(j, carry):
                col = ds(j * tile, tile, 128)
                put_blocks(gbuf, i, dot(left[:, i * half : (i + 1) * half], right[:, col], 0, 0), col)
                return carry

            lax.fori_loop(0, tiles, body, 0)

    product(low, low2, gbuf)
    pool_buffers = (pool_core, pool_x, pool_y, pool_yx, pool_xy, pool_own, pool_z, pool_total)
    pool = Reduce(links, at, gbuf, pool_buffers)
    pool.core()

    def back_pool(col):
        ext[0:rows, col] = dot(low2[...], mixw[ds(cout + col.start, tile, 128), :], 1, 1)

    column_loop(back_pool)

    def grad_summed(r):
        v = work[pl.ds(r, 32), :] + ext[pl.ds(r, 32), :]
        work[pl.ds(r, 32), :] = v
        low[pl.ds(r, 32), :] = v.astype(BF)
        return (v,)

    pool.plane()
    (sum_bias_two,) = row_sums(rows, 32, cout, 1, grad_summed)

    def back_mix(col):
        ext[0:rows, col] = dot(low[...], mixw[ds(col.start, tile, 128), :], 1, 1)

    column_loop(back_mix)

    def normed(r):
        return (middle[pl.ds(r, 32), :] - mean_two) * scale_two

    def grad_before(r):
        v = ext[pl.ds(r, 32), :] * deriv[pl.ds(r, 32), :]
        ext[pl.ds(r, 32), :] = v
        return v, v * normed(r)

    sum_shift, sum_gain = row_sums(rows, 32, cout, 2, grad_before)
    stats = exchange(2)
    stats.start(pack(sum_shift, sum_gain))
    product(a2, low, mixw.at[pl.ds(cout, cout)])
    out_mix = pltpu.make_async_copy(mixw.at[pl.ds(cout, cout)], term_mix, local.at[4])
    out_mix.start()
    pool.cross()
    shift_two_grad, gain_two_grad = unpack(stats.finish(combine_sums))

    def grad_middle(r):
        v = work[pl.ds(r, 32), :] + gain_two * scale_two * (
            ext[pl.ds(r, 32), :] - shift_two_grad / total - normed(r) * gain_two_grad / total
        )
        middle_low[pl.ds(r, 32), :] = v.astype(BF)
        return (v,)

    (sum_bias_one,) = row_sums(rows, 32, cout, 1, grad_middle)
    fill = lambda v: jnp.concatenate([v, pad], axis=1)
    vectors[0:8, :] = jnp.concatenate(
        [fill(mean_one), fill(scale_one), fill(gain_one), fill(shift_one), shift_two_grad, gain_two_grad, sum_bias_one, sum_bias_two],
        axis=0,
    )
    pool.depth()
    for copy in actives:
        copy.wait_recv()
    out_mix.wait()
    pool.finish()
    links.drain()


def run_forward(sizes, features, conv_shard, mix_shard, row_pack, cotangent, scale):
    seq, fsdp = sizes
    rows, cin = features.shape
    cout = conv_shard.shape[1] * fsdp
    deep = conv_shard.shape[0]
    two = mix_shard.shape[0]
    shape = jax.ShapeDtypeStruct
    vmem = pl.BlockSpec(memory_space=pltpu.VMEM)
    hbm = pl.BlockSpec(memory_space=pl.ANY)
    copies = 100
    half = (rows, cin // 2)
    pool = Reduce.scratch(cout, cout, fsdp)
    return pl.pallas_call(
        functools.partial(forward_kernel, sizes),
        out_shape=(
            shape((deep, cout), BF),
            shape((two, cout), BF),
            shape((cout, cout), BF),
            shape(half, BF),
            shape(half, BF),
            shape((cout // GROUP, cout // fsdp), BF),
            shape((rows // 2, cout), BF),
            shape((rows, cin), BF),
            shape((rows, cout), BF),
            shape((8, cout), F32),
        ),
        in_specs=[vmem, hbm, hbm, vmem, vmem, vmem],
        out_specs=(hbm, hbm, hbm, hbm, hbm, vmem, vmem, vmem, vmem, vmem),
        scratch_shapes=[
            pltpu.VMEM((rows + 16, cout), F32),
            pltpu.VMEM((rows, deep), BF),
            pltpu.VMEM((2, deep, cout // fsdp), BF),
            pltpu.VMEM((two, cout), BF),
            pltpu.VMEM((rows, cout), F32),
            pltpu.VMEM((rows, cout), F32),
            pltpu.VMEM((rows, cout), F32),
            pltpu.VMEM((rows, cout), BF),
            pltpu.VMEM((rows, cout), BF),
            pltpu.VMEM((rows, cout), BF),
            pltpu.VMEM((cout, cout), BF),
            pltpu.VMEM((rows, 128), F32),
            pltpu.VMEM((rows, 128), F32),
            *pool,
            pltpu.VMEM((3, 2, 8, cout // 4), F32),
            pltpu.VMEM((3, seq, 8, cout // 4), F32),
            pltpu.VMEM((3, fsdp, 8, cout // 4), F32),
            pltpu.VMEM((fsdp, 16, cout), BF),
            pltpu.SemaphoreType.DMA((copies,)),
            pltpu.SemaphoreType.DMA((copies,)),
            pltpu.SemaphoreType.DMA((3, seq)),
            pltpu.SemaphoreType.DMA((3, seq)),
            pltpu.SemaphoreType.DMA((3, fsdp)),
            pltpu.SemaphoreType.DMA((3, fsdp)),
            pltpu.SemaphoreType.DMA((5,)),
        ],
        compiler_params=pltpu.CompilerParams(
            collective_id=0, has_side_effects=True, vmem_limit_bytes=62 * 2**20
        ),
    )(features, conv_shard, mix_shard, row_pack, cotangent, scale)


class Reduce:
    def __init__(self, links, at, slot, buffers):
        self.links, self.at, self.slot = links, at, slot
        self.unit = slot.shape[0] // 16
        self.core_slot, self.from_x, self.from_y, self.from_yx, self.from_xy, self.own, self.from_z, self.total = buffers

    @staticmethod
    def scratch(height, width, parts):
        unit = height // 16
        rows = (8 * unit, 2 * unit, 2 * unit, unit, unit, 2 * unit)
        return [pltpu.VMEM((r, width), BF) for r in rows] + [pltpu.VMEM((parts - 1, 2 * unit, width // parts), BF)]

    def _rows(self, start, count):
        return self.slot.at[ds(start * self.unit, count * self.unit, 16)]

    def _send(self, src, dst, device):
        return self.links.copy(src, dst, dst, device).start()

    def core(self):
        self.by_core = self._send(self._rows((1 - self.at.c) * 8, 8), self.core_slot, self.at.near(1))

    def _add(self, start, other, count, out=None):
        step = 16
        mine = self._rows(start, count)
        out = mine if out is None else out

        def body(r):
            v = mine[pl.ds(r, step), :].astype(F32) + other[pl.ds(r, step), :].astype(F32)
            out[pl.ds(r, step), :] = v.astype(BF)

        rows_loop(count * self.unit, step, body)

    def plane(self):
        at = self.at
        self.by_core.wait_recv()
        self._add(at.c * 8, self.core_slot, 8)
        self.a, self.b = at.c * 8, at.c * 8 + 4
        self.by_x = self._send(self._rows(self.a + (1 - at.x) * 2, 2), self.from_x, at.near(2))
        self.by_y = self._send(self._rows(self.b + (1 - at.y) * 2, 2), self.from_y, at.near(4))

    def cross(self):
        x, y = self.at.x, self.at.y
        a, b = self.a + x * 2, self.b + y * 2
        self.by_x.wait_recv()
        self._add(a, self.from_x, 2)
        self.by_yx = self._send(self._rows(a + 1 - y, 1), self.from_yx, self.at.near(4))
        self.by_y.wait_recv()
        self._add(b, self.from_y, 2)
        self.by_xy = self._send(self._rows(b + 1 - x, 1), self.from_xy, self.at.near(2))
        self.a, self.b = a + y, b + x

    def depth(self):
        self.by_yx.wait_recv()
        self._add(self.a, self.from_yx, 1, self.own.at[pl.ds(0, self.unit)])
        self.by_xy.wait_recv()
        self._add(self.b, self.from_xy, 1, self.own.at[pl.ds(self.unit, self.unit)])
        self.along = Along(self.links, self.at, self.own, self.from_z, self.total)

    def finish(self):
        self.along.finish()


class Along:
    def __init__(self, links, at, own, from_z, total):
        self.at, self.own, self.from_z, self.total = at, own, from_z, total
        self.width = total.shape[1]
        self.copies = []
        for d in range(1, at.fsdp_size):
            col = ds(lax.rem(at.z + d, at.fsdp_size) * self.width, self.width, 128)
            dst = from_z.at[d - 1]
            self.copies.append(links.copy(own.at[:, col], dst, dst, at.up(d)).start())

    def finish(self):
        col = ds(self.at.z * self.width, self.width, 128)
        for copy in self.copies:
            copy.wait_recv()

        def body(r):
            v = self.own[pl.ds(r, 16), col].astype(F32)
            for d in range(self.at.fsdp_size - 1):
                v = v + self.from_z[d, pl.ds(r, 16), :].astype(F32)
            self.total[pl.ds(r, 16), :] = v.astype(BF)

        rows_loop(self.own.shape[0], 16, body)


class Tap:
    def __init__(self, links, at, slot, buffers):
        self.links, self.at, self.slot = links, at, slot
        self.core_slot, self.from_x, self.from_y, self.own, self.from_z, self.total = buffers
        self.size = slot.shape[0] // 4
        self.half = slot.shape[1] // 2

    def core(self):
        at = self.at
        src = self.slot.at[ds((1 - at.c) * 2 * self.size, 2 * self.size, 16)]
        self.by_core = self.links.copy(src, self.core_slot, self.core_slot, at.near(1)).start()

    def plane(self):
        at, size, half = self.at, self.size, self.half
        self.by_core.wait_recv()
        start = at.c * 2 * size

        def body(r):
            row = ds(start + r, 16, 16)
            v = self.slot[row, :].astype(F32) + self.core_slot[pl.ds(r, 16), :].astype(F32)
            self.slot[row, :] = v.astype(BF)

        rows_loop(2 * size, 16, body)
        low = self.slot.at[ds(start + (1 - at.y) * size, size, 16), 0:half]
        high = self.slot.at[ds(start + (1 - at.x) * size, size, 16), half : 2 * half]
        self.by_y = self.links.copy(low, self.from_y, self.from_y, at.near(4)).start()
        self.by_x = self.links.copy(high, self.from_x, self.from_x, at.near(2)).start()

    def depth(self):
        at, size, half = self.at, self.size, self.half
        start = at.c * 2 * size
        for copy, mine, other, col in (
            (self.by_y, at.y, self.from_y, slice(0, half)),
            (self.by_x, at.x, self.from_x, slice(half, 2 * half)),
        ):
            copy.wait_recv()

            def body(r):
                v = self.slot[ds(start + mine * size + r, 16, 16), col].astype(F32) + other[pl.ds(r, 16), :].astype(F32)
                self.own[pl.ds(r, 16), col] = v.astype(BF)

            rows_loop(size, 16, body)
        self.along = Along(self.links, at, self.own, self.from_z, self.total)

    def finish(self):
        self.along.finish()


def backward_kernel(
    sizes,
    features,
    active_one,
    active_x,
    active_y,
    vectors,
    pool_total,
    middle_low,
    full_conv,
    term_mix,
    gathered,
    grad_features,
    sums_out,
    edged,
    edged_x,
    edged_y,
    ext,
    shifted,
    shifted_two,
    weight,
    grad_active,
    slots,
    core_slots,
    from_x,
    from_y,
    own,
    from_z,
    total,
    mix_slot,
    mix_core,
    mix_x,
    mix_y,
    mix_yx,
    mix_xy,
    mix_own,
    mix_z,
    mix_total,
    mine,
    seq_slots,
    fsdp_slots,
    send,
    recv,
    seq_send,
    seq_recv,
    fsdp_send,
    fsdp_recv,
    local,
):
    seq, fsdp = sizes
    at = Place(seq, fsdp)
    links = Links(send, recv)
    rows, cin = features.shape
    cout = full_conv.shape[1]
    taps = full_conv.shape[0] // cin
    all_rows = float(rows * seq * fsdp)
    lead = 16
    half_in, half_out = cin // 2, cout // 2
    pool_share, tap_share = cout // GROUP, cin // GROUP
    start_tap = 2 * pool_share
    share = start_tap + taps * tap_share

    def load_weight(i):
        return pltpu.make_async_copy(full_conv.at[pl.ds(i * half_in, half_in)], weight.at[i % 2], local.at[i % 2])

    load_weight(0).start()
    load_weight(1).start()
    load_mix = pltpu.make_async_copy(term_mix, mix_slot, local.at[2])
    load_middle = pltpu.make_async_copy(middle_low, edged.at[pl.ds(lead, rows)], local.at[3])
    load_middle.start()
    load_mix.start()
    at.barrier()
    top, bottom = pl.ds(0, lead), pl.ds(lead + rows, lead)
    below = links.copy(middle_low.at[top], edged.at[bottom], edged.at[bottom], at.up(fsdp - 1)).start()
    above = links.copy(middle_low.at[pl.ds(rows - lead, lead)], edged.at[top], edged.at[top], at.up(1)).start()

    def spread(block, start, order):
        size = block.shape[0]

        def place(part, half):
            first = order(part) * share + start
            if half is None:
                return gathered.at[ds(first, size, 16)]
            return gathered.at[ds(first + half * (size // 2), size // 2, 16)]

        keep = pltpu.make_async_copy(block, place(at.part, None), local.at[4 + len(groups)])
        groups.append((Spread(links, at, place, block), keep))
        groups[-1][0].one()
        keep.start()

    groups = []

    def tap_order(part):
        c, x, y = part & 1, (part >> 1) & 1, part >> 2
        low = at.z < fsdp // 2
        return jnp.where(low, x, y) * 4 + c * 2 + jnp.where(low, y, x)

    load_middle.wait()
    below.wait_recv()
    above.wait_recv()
    edged[top, :] = jnp.where(at.z > 0, edged[top, :], jnp.zeros((lead, cout), BF))
    edged[bottom, :] = jnp.where(at.z < fsdp - 1, edged[bottom, :], jnp.zeros((lead, cout), BF))
    to_x = links.copy(edged.at[:, 0:half_out], edged_x, edged_x, at.near(2)).start()
    to_y = links.copy(edged.at[:, half_out:cout], edged_y, edged_y, at.near(4)).start()
    mix = Reduce(links, at, mix_slot, (mix_core, mix_x, mix_y, mix_yx, mix_xy, mix_own, mix_z, mix_total))
    load_mix.wait()
    mix.core()

    def widen(r):
        ext[pl.ds(r, 32), :] = edged[pl.ds(r, 32), :].astype(F32)

    rows_loop(rows + 2 * lead, 32, widen)
    half_width = (taps - 1) // 2

    def shift(target, k):
        start = lead + half_width - k

        def body(i, carry):
            col = ds(i * 128, 128, 128)
            target[:, col] = ext[pl.ds(start, rows), col].astype(BF)
            return carry

        lax.fori_loop(0, cout // 128, body, 0)

    def back(k):
        for i in (2 * k, 2 * k + 1):
            load_weight(i).wait()

            for j in range(2):
                at_row = j * (half_in // 2)
                col = slice((i % 2) * half_in + at_row, (i % 2) * half_in + at_row + half_in // 2)
                v = dot(shifted[k], weight[i % 2, at_row : at_row + half_in // 2, :], 1, 1)
                grad_active[:, col] = v if k == 0 else grad_active[:, col] + v
            if i + 2 < 2 * taps:
                load_weight(i + 2).start()

    for k in range(taps):
        shift(shifted.at[k], k)
        back(k)
        if k == 0:
            mix.plane()
            spread(pool_total, 0, lambda part: part)

    mean_one, scale_one, gain_one, shift_one = (vectors[i : i + 1, :cin] for i in range(4))

    def grad_before(r):
        normed = (features[pl.ds(r, 32), :].astype(F32) - mean_one) * scale_one
        v = normal(normed * gain_one + shift_one)[1] * grad_active[pl.ds(r, 32), :]
        grad_active[pl.ds(r, 32), :] = v
        return v, v * normed

    sum_shift, sum_gain = row_sums(rows, 32, cin, 2, grad_before)
    pad = jnp.zeros((1, cout - cin), F32)
    wide = lambda v: jnp.concatenate([v, pad], axis=1)
    sems = (seq_send, seq_recv, fsdp_send, fsdp_recv)
    stats = Exchange(at, mine, seq_slots, fsdp_slots, sems)
    stats.start(pack(wide(sum_shift), wide(sum_gain), vectors[6:7, :], vectors[7:8, :]))

    to_x.wait_recv()
    to_y.wait_recv()

    def widen_two(r):
        ext[pl.ds(r, 32), 0:half_out] = edged_x[pl.ds(r, 32), :].astype(F32)
        ext[pl.ds(r, 32), half_out:cout] = edged_y[pl.ds(r, 32), :].astype(F32)

    rows_loop(rows + 2 * lead, 32, widen_two)
    columns = (ds(at.x * half_in, half_in, 128), ds(at.y * half_in, half_in, 128))
    tile = 256

    def product(k):
        for i, other in enumerate((active_x, active_y)):

            def body(j, carry):
                col = ds(i * half_out + j * tile, tile, 128)
                v = dot(active_one[:, columns[i]], shifted[k, :, col], 0, 0)
                v = v + dot(other[...], shifted_two[:, col], 0, 0)
                slots[k, :, col] = v.astype(BF)
                return carry

            lax.fori_loop(0, half_out // tile, body, 0)

    steps = []
    for k in range(taps):
        mine_rows = pl.ds(k * tap_share, tap_share)
        steps.append(
            Tap(
                links,
                at,
                slots.at[k],
                (
                    core_slots.at[k],
                    from_x.at[mine_rows],
                    from_y.at[mine_rows],
                    own.at[mine_rows],
                    from_z.at[:, mine_rows],
                    total.at[mine_rows],
                ),
            )
        )

    def finish(k):
        steps[k].finish()
        spread(steps[k].total, start_tap + k * tap_share, tap_order)

    for k in range(taps):
        shift(shifted_two, k)
        product(k)
        steps[k].core()
        if k == 0:
            mix.cross()
            groups[0][0].two()
        if k == 1:
            stats.middle(combine_sums)
            groups[0][0].three()
        if k >= 1:
            steps[k - 1].plane()
        if k == 2:
            mix.depth()
            everyone = unpack(stats.end(combine_sums))
        if k >= 2:
            steps[k - 2].depth()
    steps[taps - 1].plane()
    mix.finish()
    spread(mix_total, pool_share, lambda part: part)
    steps[taps - 2].depth()
    finish(0)
    shift_grad, gain_grad = everyone[0][:, :cin], everyone[1][:, :cin]

    def store(r):
        normed = (features[pl.ds(r, 32), :].astype(F32) - mean_one) * scale_one
        v = grad_active[pl.ds(r, 32), :] - shift_grad / all_rows - normed * gain_grad / all_rows
        grad_features[pl.ds(r, 32), :] = (gain_one * scale_one * v).astype(BF)

    rows_loop(rows, 32, store)
    sums_out[0:4, :] = jnp.concatenate(everyone, axis=0)
    steps[taps - 1].depth()
    groups[1][0].two()
    for k in range(1, taps):
        finish(k)
        groups[k][0].three()
        groups[k + 1][0].two()
    groups[taps][0].three()
    groups[taps + 1][0].two()
    groups[taps + 1][0].three()
    for group, keep in groups:
        group.four()
        keep.wait()
    links.drain()


def run_backward(sizes, features, active_one, active_x, active_y, vectors, pool_total, middle_low, full_conv, term_mix):
    seq, fsdp = sizes
    rows, cin = features.shape
    deep, cout = full_conv.shape
    taps = deep // cin
    width = cout // fsdp
    share = (deep + 2 * cout) // GROUP
    tap_share = cin // GROUP
    shape = jax.ShapeDtypeStruct
    vmem = pl.BlockSpec(memory_space=pltpu.VMEM)
    hbm = pl.BlockSpec(memory_space=pl.ANY)
    copies = 160
    return pl.pallas_call(
        functools.partial(backward_kernel, sizes),
        out_shape=(shape((GROUP * share, width), BF), shape((rows, cin), BF), shape((8, cout), F32)),
        in_specs=[vmem, vmem, vmem, vmem, vmem, vmem, hbm, hbm, hbm],
        out_specs=(hbm, vmem, vmem),
        scratch_shapes=[
            pltpu.VMEM((rows + 32, cout), BF),
            pltpu.VMEM((rows + 32, cout // 2), BF),
            pltpu.VMEM((rows + 32, cout // 2), BF),
            pltpu.VMEM((rows + 32, cout), F32),
            pltpu.VMEM((taps, rows, cout), BF),
            pltpu.VMEM((rows, cout), BF),
            pltpu.VMEM((2, cin // 2, cout), BF),
            pltpu.VMEM((rows, cin), F32),
            pltpu.VMEM((taps, cin // 2, cout), BF),
            pltpu.VMEM((taps, cin // 4, cout), BF),
            pltpu.VMEM((taps * tap_share, cout // 2), BF),
            pltpu.VMEM((taps * tap_share, cout // 2), BF),
            pltpu.VMEM((taps * tap_share, cout), BF),
            pltpu.VMEM((fsdp - 1, taps * tap_share, width), BF),
            pltpu.VMEM((taps * tap_share, width), BF),
            pltpu.VMEM((cout, cout), BF),
            *Reduce.scratch(cout, cout, fsdp),
            pltpu.VMEM((cout // GROUP, width), BF),
            pltpu.VMEM((2, 16, cout // 4), F32),
            pltpu.VMEM((seq, 16, cout // 4), F32),
            pltpu.VMEM((fsdp, 16, cout // 4), F32),
            pltpu.SemaphoreType.DMA((copies,)),
            pltpu.SemaphoreType.DMA((copies,)),
            pltpu.SemaphoreType.DMA((seq,)),
            pltpu.SemaphoreType.DMA((seq,)),
            pltpu.SemaphoreType.DMA((fsdp,)),
            pltpu.SemaphoreType.DMA((fsdp,)),
            pltpu.SemaphoreType.DMA((6 + taps,)),
        ],
        compiler_params=pltpu.CompilerParams(
            collective_id=1, has_side_effects=True, vmem_limit_bytes=62 * 2**20
        ),
    )(features, active_one, active_x, active_y, vectors, pool_total, middle_low, full_conv, term_mix)


def parameter_pack(owner, features, first, second):
    cout = second[0].shape[0] * lax.axis_size("fsdp")
    out = jnp.zeros((16, cout), BF)
    block = jnp.stack(first)
    out = lax.dynamic_update_slice(out, block, (0, owner * block.shape[1]))
    block = jnp.stack(second)
    out = lax.dynamic_update_slice(out, block, (2, owner * block.shape[1]))
    rows, cin = features.shape
    out = out.at[8:10, :cin].set(features[0:2])
    return out.at[14:16, :cin].set(features[rows - 2 : rows])


def spread_sum(v):
    size = lax.axis_size("seq")
    bit = GROUP
    while bit < size:
        v = v + lax.ppermute(v, "seq", [(i, i ^ bit) for i in range(size)])
        bit *= 2
    return v


def on_device(
    features,
    conv_weight,
    mix_weight,
    pool_weight,
    gain_first,
    shift_first,
    gain_second,
    shift_second,
    bias_conv,
    bias_mix,
    cotangent,
    track_counts,
):
    rows, cin = features.shape
    seq, fsdp = lax.axis_size("seq"), lax.axis_size("fsdp")
    position = lax.axis_index(("seq", "fsdp"))
    owner = lax.axis_index("fsdp")
    window = position * rows // WIN
    width = conv_weight.shape[2]
    cout = width * fsdp
    taps = conv_weight.shape[0]
    scale = lax.dynamic_slice_in_dim(track_counts, window, 1).astype(F32) / TRACKS
    scale = jnp.broadcast_to(scale[:, None], (1, cout))
    row_pack = parameter_pack(
        owner, features, (gain_first, shift_first), (gain_second, shift_second, bias_conv, bias_mix)
    )
    full_conv, _, term_mix, active_x, active_y, pool_total, pooled, active_one, middle_low, vectors = run_forward(
        (seq, fsdp),
        features,
        conv_weight.reshape(taps * cin, width),
        jnp.concatenate([mix_weight, pool_weight], axis=0),
        row_pack,
        cotangent,
        scale,
    )
    gathered, grad_features, sums = run_backward(
        (seq, fsdp), features, active_one, active_x, active_y, vectors, pool_total, middle_low, full_conv, term_mix
    )
    parts = spread_sum(gathered.reshape(GROUP, -1, width).astype(F32))
    taken = 0
    products = []
    for height in [cout, cout] + [cin] * taps:
        size = height // GROUP
        products.append(parts[:, taken : taken + size].reshape(height, width))
        taken += size
    grad_pool, grad_mix = products[:2]
    grad_conv = jnp.stack(products[2:])
    shift_two_grad, gain_two_grad = vectors[4], vectors[5]
    shift_one_grad, gain_one_grad, bias_one_grad, bias_two_grad = sums[0], sums[1], sums[2], sums[3]

    def share(v, size):
        return lax.dynamic_slice_in_dim(v, owner * size, size)

    first, second = gain_first.shape[0], gain_second.shape[0]
    return (
        pooled,
        grad_features,
        grad_conv,
        grad_mix,
        grad_pool,
        share(gain_one_grad, first),
        share(shift_one_grad, first),
        share(gain_two_grad, second),
        share(shift_two_grad, second),
        share(bias_one_grad, second),
        share(bias_two_grad, second),
    )


def solution(mesh):
    rows = P(("seq", "fsdp"), None)
    vector = P("fsdp")
    in_specs = (rows, P(None, None, "fsdp"), P(None, "fsdp"), P(None, "fsdp")) + (vector,) * 6 + (rows, P())
    out_specs = (rows, rows, P(None, None, "fsdp"), P(None, "fsdp"), P(None, "fsdp")) + (vector,) * 6
    return jax.shard_map(on_device, mesh=mesh, in_specs=in_specs, out_specs=out_specs, check_vma=False)
```

```python
import functools
import math
import jax
import jax.numpy as jnp
from jax import lax
from jax.experimental import pallas as pl
from jax.experimental.pallas import tpu as pltpu
from jax.sharding import PartitionSpec as P

TRACKS = 5313
WIN = 2048
EPSILON = 1e-05
MESH = pl.DeviceIdType.MESH
BF = jnp.bfloat16
F32 = jnp.float32
GROUP = 8


def dot(a, b, ca, cb):
    return lax.dot_general(a, b, (((ca,), (cb,)), ((), ())), preferred_element_type=F32)


def ds(start, size, step):
    return pl.ds(pl.multiple_of(start, step), size)


def fold(v):
    rows, width = v.shape
    return jnp.sum(v.reshape(rows // 8, 8, width), axis=0)


def rows_loop(total, step, body):
    def run(i, carry):
        body(pl.multiple_of(i * step, step))
        return carry

    lax.fori_loop(0, total // step, run, 0)


def row_sums(total, step, width, count, body):
    def run(i, carry):
        parts = body(pl.multiple_of(i * step, step))
        return tuple(c + fold(v) for c, v in zip(carry, parts))

    zero = tuple(jnp.zeros((8, width), F32) for _ in range(count))
    sums = lax.fori_loop(0, total // step, run, zero)
    return [jnp.sum(v, axis=0, keepdims=True) for v in sums]


def normal(b):
    cdf = 0.5 * (1.0 + lax.erf(b * math.sqrt(0.5)))
    pdf = jnp.exp(-0.5 * b * b) * (1.0 / math.sqrt(2.0 * math.pi))
    return cdf, cdf + b * pdf


class Copy:
    def __init__(self, links, src, there, here, device):
        i = links.count
        links.count += 1
        send, recv = links.send.at[i], links.recv.at[i]

        def make(dst):
            return pltpu.make_async_remote_copy(
                src_ref=src,
                dst_ref=dst,
                send_sem=send,
                recv_sem=recv,
                device_id=device,
                device_id_type=MESH,
            )

        self.links = links
        self.out, self.into = functools.partial(make, there), functools.partial(make, here)

    def start(self):
        self.out().start()
        self.links.started.append(self)
        return self

    def wait_recv(self):
        self.into().wait_recv()

    def wait_send(self):
        self.out().wait_send()


class Links:
    def __init__(self, send, recv):
        self.send, self.recv = send, recv
        self.count = 0
        self.started = []

    def copy(self, src, there, here, device):
        return Copy(self, src, there, here, device)

    def drain(self):
        for item in self.started:
            item.wait_send()
        self.started = []


class Place:
    def __init__(self, seq, fsdp):
        self.seq_size, self.fsdp_size = seq, fsdp
        self.s, self.z = lax.axis_index("seq"), lax.axis_index("fsdp")
        self.part = lax.rem(self.s, GROUP)
        self.base = self.s - self.part
        self.c, self.x, self.y = self.part & 1, (self.part >> 1) & 1, self.part >> 2

    def near(self, mask):
        return (self.base + jnp.bitwise_xor(self.part, mask), self.z)

    def up(self, d):
        return (self.s, lax.rem(self.z + d, self.fsdp_size))

    def barrier(self):
        bar = pltpu.get_barrier_semaphore()

        def greet(i, carry):
            peer = lax.rem(self.s + i, self.seq_size)
            pl.semaphore_signal(bar, inc=1, device_id=(peer, self.z), device_id_type=MESH)
            return carry

        lax.fori_loop(1, self.seq_size, greet, 0)
        for d in range(1, self.fsdp_size):
            pl.semaphore_signal(bar, inc=1, device_id=self.up(d), device_id_type=MESH)
        pl.semaphore_wait(bar, self.seq_size + self.fsdp_size - 2)


class Exchange:
    def __init__(self, place, mine, seq_slots, fsdp_slots, sems):
        self.place, self.mine = place, mine
        self.seq_slots, self.fsdp_slots = seq_slots, fsdp_slots
        self.seq_send, self.seq_recv, self.fsdp_send, self.fsdp_recv = sems

    def _copy(self, i, stage):
        at = self.place
        if stage == 0:
            peer = lax.rem(at.s + i, at.seq_size)
            source = lax.rem(at.s - i + at.seq_size, at.seq_size)
            device, slots, send, recv, me = (peer, at.z), self.seq_slots, self.seq_send, self.seq_recv, at.s
        else:
            peer = lax.rem(at.z + i, at.fsdp_size)
            source = lax.rem(at.z - i + at.fsdp_size, at.fsdp_size)
            device, slots, send, recv, me = (at.s, peer), self.fsdp_slots, self.fsdp_send, self.fsdp_recv, at.z
        make = lambda slot: pltpu.make_async_remote_copy(
            src_ref=self.mine.at[stage],
            dst_ref=slots.at[slot],
            send_sem=send.at[i],
            recv_sem=recv.at[i],
            device_id=device,
            device_id_type=MESH,
        )
        return functools.partial(make, me), functools.partial(make, source)

    def _each(self, stage, what):
        size = self.place.seq_size if stage == 0 else self.place.fsdp_size

        def run(i, carry):
            what(*self._copy(i, stage))
            return carry

        lax.fori_loop(1, size, run, 0)

    def start(self, block):
        self.mine[0] = block
        self.seq_slots[self.place.s] = block
        self._each(0, lambda out, into: out().start())

    def middle(self, combine):
        self._each(0, lambda out, into: into().wait_recv())
        block = combine(self.seq_slots)
        self.mine[1] = block
        self.fsdp_slots[self.place.z] = block
        self._each(1, lambda out, into: out().start())

    def end(self, combine):
        self._each(1, lambda out, into: into().wait_recv())
        block = combine(self.fsdp_slots)
        self._each(0, lambda out, into: out().wait_send())
        self._each(1, lambda out, into: out().wait_send())
        return block

    def finish(self, combine):
        self.middle(combine)
        return self.end(combine)


def pack(*vectors):
    width = vectors[0].shape[1] // 4
    pieces = [v[:, i * width : (i + 1) * width] for v in vectors for i in range(4)]
    return jnp.concatenate(pieces, axis=0)


def unpack(block):
    count = block.shape[0] // 4
    return [jnp.concatenate([block[4 * j + i : 4 * j + i + 1] for i in range(4)], axis=1) for j in range(count)]


def combine_sums(slots):
    return jnp.sum(slots[...], axis=0)


def combine_moments(slots):
    v = slots[...]
    center, spread = v[:, :4], v[:, 4:]
    mean = jnp.mean(center, axis=0)
    rest = jnp.mean(spread + jnp.square(center - mean[None]), axis=0)
    return jnp.concatenate([mean, rest], axis=0)


class Spread:
    def __init__(self, links, at, place, source=None):
        self.links, self.at, self.place, self.source = links, at, place, source
        self.held = {}

    def _send(self, name, mask, of, half=None):
        part = self.at.part
        mine = self.place(jnp.bitwise_xor(part, of), half)
        theirs = self.place(jnp.bitwise_xor(part, of ^ mask), half)
        src = mine if of or self.source is None else self.source
        self.held[name] = self.links.copy(src, mine, theirs, self.at.near(mask)).start()

    def one(self):
        self._send("x", 2, 0)
        self._send("y", 4, 0)
        self._send("c", 1, 0)

    def two(self):
        self.held["x"].wait_recv()
        self._send("xa", 4, 2, 0)
        self._send("xc", 1, 2)
        self.held["y"].wait_recv()
        self._send("yb", 2, 4, 1)
        self._send("yc", 1, 4)

    def three(self):
        self.held["xa"].wait_recv()
        self._send("ac", 1, 6, 0)
        self.held["yb"].wait_recv()
        self._send("bc", 1, 6, 1)

    def four(self):
        for name in ("c", "xc", "yc", "ac", "bc"):
            self.held[name].wait_recv()


class Gather:
    def __init__(self, links, at, shard, full, d, lo, size):
        self.links, self.at, self.shard, self.full, self.d = links, at, shard, full, d
        self.lo, self.size = lo, size
        self.share, self.width = shard.shape[0] // GROUP, shard.shape[1]
        self.z = lax.rem(at.z - d + at.fsdp_size, at.fsdp_size)
        spread = Spread(links, at, lambda part, half: self.full.at[self._rows(part, half), self._columns(self.z)])
        self.spread, self.two, self.three, self.four = spread, spread.two, spread.three, spread.four

    def _rows(self, part, half=None):
        start = part * self.share + self.lo
        if half is None:
            return ds(start, self.size, 16)
        return ds(start + half * (self.size // 2), self.size // 2, 16)

    def _columns(self, z):
        return ds(z * self.width, self.width, 128)

    def send(self):
        at = self.at
        rows = self._rows(at.part)
        passed = self._columns(lax.rem(self.z + 1, at.fsdp_size))
        there = self.full.at[rows, passed]
        here = self.full.at[rows, self._columns(self.z)]
        src = self.shard.at[rows] if self.d == 1 else there
        self.along = self.links.copy(src, there, here, at.up(1)).start()

    def one(self):
        self.along.wait_recv()
        self.spread.one()


def put_blocks(target, half, values, col):
    size = values.shape[0] // 8
    for i in range(8):
        part, side = 4 * half + i // 2, i % 2
        c, x, y = part & 1, part >> 1 & 1, part >> 2
        at = 8 * c + 4 * side + (2 * x + y if side == 0 else 2 * y + x)
        target[at * size : (at + 1) * size, col] = values[i * size : (i + 1) * size].astype(BF)


def forward_kernel(
    sizes,
    features,
    conv_shard,
    mix_shard,
    vectors_in,
    cotangent,
    scale,
    full_conv,
    full_mix,
    term_mix,
    active_x,
    active_y,
    pool_own,
    pooled,
    active_out,
    middle_low,
    vectors,
    ext,
    taps,
    wbuf,
    mixw,
    middle,
    deriv,
    work,
    a2,
    low,
    low2,
    gbuf,
    pair_one,
    pair_two,
    pool_core,
    pool_x,
    pool_y,
    pool_yx,
    pool_xy,
    mine,
    seq_slots,
    fsdp_slots,
    packs,
    edges,
    send,
    recv,
    seq_send,
    seq_recv,
    fsdp_send,
    fsdp_recv,
    local,
):
    seq, fsdp = sizes
    at = Place(seq, fsdp)
    links = Links(send, recv)
    rows, cin = features.shape
    cout = full_conv.shape[1]
    width = cout // fsdp
    total = float(rows * seq * fsdp)
    taps_count = conv_shard.shape[0] // cin
    lead = 8

    def exchange(i):
        sems = (seq_send.at[i], seq_recv.at[i], fsdp_send.at[i], fsdp_recv.at[i])
        return Exchange(at, mine.at[i], seq_slots.at[i], fsdp_slots.at[i], sems)

    own_conv = pltpu.make_async_copy(wbuf.at[0], full_conv.at[:, ds(at.z * width, width, 128)], local.at[0])
    own_mix = pltpu.make_async_copy(mix_shard, mixw.at[:, ds(at.z * width, width, 128)], local.at[1])
    own_load = pltpu.make_async_copy(conv_shard, wbuf.at[0], local.at[2])

    at.barrier()
    near = range(1, fsdp)
    share = conv_shard.shape[0] // GROUP
    cut = share * 3 // 5 // 32 * 32
    conv = [Gather(links, at, conv_shard, full_conv, d, *piece) for d in near for piece in ((0, cut), (cut, share - cut))]
    mix = [Gather(links, at, mix_shard, full_mix, d, 0, mix_shard.shape[0] // GROUP) for d in near]
    parcels = []
    for d in near:
        source = lax.rem(at.z - d + fsdp, fsdp)
        parcels.append(links.copy(vectors_in, packs.at[at.z], packs.at[source], at.up(d)).start())
    parcels.append(links.copy(features.at[pl.ds(0, 16)], edges.at[1], edges.at[1], at.up(fsdp - 1)).start())
    parcels.append(links.copy(features.at[pl.ds(rows - 16, 16)], edges.at[0], edges.at[0], at.up(1)).start())
    conv[0].send()
    own_load.start()
    own_mix.start()

    (sum_one,) = row_sums(rows, 64, cin, 1, lambda r: (features[pl.ds(r, 64), :].astype(F32),))
    mean = sum_one / rows
    (dev_one,) = row_sums(rows, 64, cin, 1, lambda r: (jnp.square(features[pl.ds(r, 64), :].astype(F32) - mean),))
    pad = jnp.zeros((1, cout - cin), F32)
    stats = exchange(0)
    stats.start(pack(jnp.concatenate([mean, pad], axis=1), jnp.concatenate([dev_one / rows, pad], axis=1)))
    packs[at.z] = vectors_in[...]
    stats.middle(combine_moments)
    conv[0].one()
    for parcel in parcels:
        parcel.wait_recv()
    everyone = packs[...]
    share_in = cin // fsdp
    gain_one, shift_one = (jnp.concatenate([everyone[z, i : i + 1, :share_in] for z in range(fsdp)], axis=1) for i in range(2))
    gain_two, shift_two, bias_one, bias_two = (
        jnp.concatenate([everyone[z, i : i + 1] for z in range(fsdp)], axis=1) for i in range(2, 6)
    )
    mean_one, var_one = unpack(stats.end(combine_moments))
    conv[1].send()
    conv[2].send()
    mean_one, scale_one = mean_one[:, :cin], lax.rsqrt(var_one[:, :cin] + EPSILON)

    def active(v):
        b = (v - mean_one) * scale_one * gain_one + shift_one
        return b * (0.5 * (1.0 + lax.erf(b * math.sqrt(0.5))))

    def first_active(r):
        v = active(features[pl.ds(r, 32), :].astype(F32)).astype(BF)
        active_out[pl.ds(r, 32), :] = v
        ext[pl.ds(lead + r, 32), :cin] = v.astype(F32)

    rows_loop(rows, 32, first_active)
    conv[1].one()
    conv[3].send()
    conv[0].two()
    row = lax.broadcasted_iota(jnp.int32, (8, cin), 0)
    before, after = edges[0].astype(F32)[8:16], edges[1].astype(F32)[0:8]
    ext[0:lead, :cin] = jnp.where((row >= 6) & (at.z > 0), active(before), 0.0)
    ext[lead + rows : lead + rows + 8, :cin] = jnp.where((row < 2) & (at.z < fsdp - 1), active(after), 0.0)
    def shifted(k):
        def body(i, carry):
            col = ds(i * 128, 128, 128)
            taps[:, ds(k * cin + i * 128, 128, 128)] = ext[pl.ds(lead - 2 + k, rows), col].astype(BF)
            return carry

        lax.fori_loop(0, cin // 128, body, 0)

    for k in range(taps_count):
        shifted(k)
    conv[2].one()
    conv[4].send()
    conv[1].two()
    conv[0].three()

    def load_block(slot, z):
        copy = pltpu.make_async_copy(full_conv.at[:, ds(z * width, width, 128)], wbuf.at[slot], local.at[3])
        copy.start()
        return copy

    def multiply(slot, z, half):
        row = pl.ds(half * (rows // 2), rows // 2)
        middle[row, ds(z * width, width, 128)] = dot(taps[row, :], wbuf[slot], 1, 0)

    def load_mix(i):
        col = ds(mix[i].z * width, width, 128)
        copy = pltpu.make_async_copy(full_mix.at[:, col], mixw.at[:, col], local.at[5 + i])
        copy.start()
        return copy

    own_load.wait()
    own_conv.start()
    multiply(0, at.z, 0)
    conv[3].one()
    conv[5].send()
    conv[2].two()
    conv[1].three()
    conv[0].four()
    multiply(0, at.z, 1)
    own_conv.wait()
    conv[4].one()
    mix[0].send()
    conv[3].two()
    conv[2].three()
    conv[1].four()
    block = load_block(1, conv[0].z)
    conv[5].one()
    conv[4].two()
    conv[3].three()
    conv[2].four()
    block.wait()
    multiply(1, conv[0].z, 0)
    mix[0].one()
    mix[1].send()
    conv[5].two()
    conv[4].three()
    conv[3].four()
    block = load_block(0, conv[2].z)
    multiply(1, conv[0].z, 1)
    block.wait()
    multiply(0, conv[2].z, 0)
    mix[1].one()
    mix[2].send()
    conv[5].three()
    conv[4].four()
    multiply(0, conv[2].z, 1)
    mix[0].two()
    conv[5].four()
    block = load_block(1, conv[4].z)
    mix[1].two()
    mix[0].three()
    block.wait()
    multiply(1, conv[4].z, 0)
    mix[0].four()
    mix[1].three()
    multiply(1, conv[4].z, 1)

    def plus_bias(r):
        v = middle[pl.ds(r, 32), :] + bias_one
        middle[pl.ds(r, 32), :] = v
        return (v,)

    (sum_two,) = row_sums(rows, 32, cout, 1, plus_bias)
    mean = sum_two / rows
    (dev_two,) = row_sums(rows, 32, cout, 1, lambda r: (jnp.square(middle[pl.ds(r, 32), :] - mean),))
    stats = exchange(1)
    stats.start(pack(mean, dev_two / rows))
    loads = [load_mix(0)]
    stats.middle(combine_moments)
    mix[2].one()
    mix[1].four()
    loads.append(load_mix(1))
    mean_two, var_two = unpack(stats.end(combine_moments))
    scale_two = lax.rsqrt(var_two + EPSILON)

    def second_active(r):
        b = (middle[pl.ds(r, 32), :] - mean_two) * scale_two * gain_two + shift_two
        cdf, slope = normal(b)
        a2[pl.ds(r, 32), :] = (b * cdf).astype(BF)
        deriv[pl.ds(r, 32), :] = slope

    rows_loop(rows // 2, 32, second_active)
    mix[2].two()
    rows_loop(rows // 2, 32, lambda r: second_active(rows // 2 + r))
    mix[2].three()
    mix[2].four()
    loads.append(load_mix(2))
    own_mix.wait()
    half = cin // 2
    actives = [
        links.copy(active_out.at[:, ds((1 - at.x) * half, half, 128)], active_x, active_x, at.near(2)).start(),
        links.copy(active_out.at[:, ds((1 - at.y) * half, half, 128)], active_y, active_y, at.near(4)).start(),
    ]
    for load in loads:
        load.wait()

    tile = 512
    tiles = cout // tile

    def column_loop(body):
        def run(i, carry):
            body(ds(i * tile, tile, 128))
            return carry

        lax.fori_loop(0, tiles, run, 0)

    def add_mix(col):
        work[:, col] = dot(a2[...], mixw[0:cout, col], 1, 0)

    column_loop(add_mix)

    def add_residual(r):
        v = middle[pl.ds(r, 32), :] + work[pl.ds(r, 32), :] + bias_two
        ext[pl.ds(r, 32), :] = v
        low[pl.ds(r, 32), :] = v.astype(BF)

    rows_loop(rows, 32, add_residual)

    def add_pool(col):
        work[:, col] = dot(low[...], mixw[cout : 2 * cout, col], 1, 0)

    column_loop(add_pool)

    def pairs(i, carry):
        col = ds(i * 128, 128, 128)
        even, odd = pl.ds(0, rows // 2, 2), pl.ds(1, rows // 2, 2)
        one, two = pair_one, pair_two
        one[...], two[...] = work[:, col], ext[0:rows, col]
        l0, l1 = one[even, :], one[odd, :]
        s0, s1 = two[even, :], two[odd, :]
        top = jnp.maximum(l0, l1)
        e0, e1 = jnp.exp(l0 - top), jnp.exp(l1 - top)
        inverse = 1.0 / (e0 + e1)
        w0, w1 = e0 * inverse, e1 * inverse
        up = cotangent[:, col].astype(F32) * scale[:, col]
        pooled[:, col] = (w0 * s0 + w1 * s1).astype(BF)
        g0, g1 = s0 * up, s1 * up
        both = w0 * g0 + w1 * g1
        one[even, :] = w0 * up
        one[odd, :] = w1 * up
        two[even, :] = w0 * (g0 - both)
        two[odd, :] = w1 * (g1 - both)
        work[:, col] = one[...]
        low2[:, col] = two[...].astype(BF)
        return carry

    lax.fori_loop(0, cout // 128, pairs, 0)

    def product(left, right, gbuf):
        half = cout // 2
        for i in range(2):
            def body(j, carry):
                col = ds(j * tile, tile, 128)
                put_blocks(gbuf, i, dot(left[:, i * half : (i + 1) * half], right[:, col], 0, 0), col)
                return carry

            lax.fori_loop(0, tiles, body, 0)

    product(low, low2, gbuf)
    pool_buffers = (pool_core, pool_x, pool_y, pool_yx, pool_xy, pool_own)
    pool = Reduce(links, at, gbuf, pool_buffers)
    pool.core()

    def back_pool(col):
        ext[0:rows, col] = dot(low2[...], mixw[ds(cout + col.start, tile, 128), :], 1, 1)

    column_loop(back_pool)

    def grad_summed(r):
        v = work[pl.ds(r, 32), :] + ext[pl.ds(r, 32), :]
        work[pl.ds(r, 32), :] = v
        low[pl.ds(r, 32), :] = v.astype(BF)
        return (v,)

    pool.plane()
    (sum_bias_two,) = row_sums(rows, 32, cout, 1, grad_summed)

    def back_mix(col):
        ext[0:rows, col] = dot(low[...], mixw[ds(col.start, tile, 128), :], 1, 1)

    column_loop(back_mix)

    def normed(r):
        return (middle[pl.ds(r, 32), :] - mean_two) * scale_two

    def grad_before(r):
        v = ext[pl.ds(r, 32), :] * deriv[pl.ds(r, 32), :]
        ext[pl.ds(r, 32), :] = v
        return v, v * normed(r)

    sum_shift, sum_gain = row_sums(rows, 32, cout, 2, grad_before)
    stats = exchange(2)
    stats.start(pack(sum_shift, sum_gain))
    product(a2, low, mixw.at[pl.ds(cout, cout)])
    out_mix = pltpu.make_async_copy(mixw.at[pl.ds(cout, cout)], term_mix, local.at[4])
    out_mix.start()
    stats.middle(combine_sums)
    pool.cross()
    shift_two_grad, gain_two_grad = unpack(stats.end(combine_sums))

    def grad_middle(r):
        v = work[pl.ds(r, 32), :] + gain_two * scale_two * (
            ext[pl.ds(r, 32), :] - shift_two_grad / total - normed(r) * gain_two_grad / total
        )
        middle_low[pl.ds(r, 32), :] = v.astype(BF)
        return (v,)

    (sum_bias_one,) = row_sums(rows, 32, cout, 1, grad_middle)
    fill = lambda v: jnp.concatenate([v, pad], axis=1)
    vectors[0:8, :] = jnp.concatenate(
        [fill(mean_one), fill(scale_one), fill(gain_one), fill(shift_one), shift_two_grad, gain_two_grad, sum_bias_one, sum_bias_two],
        axis=0,
    )
    pool.depth()
    for copy in actives:
        copy.wait_recv()
    out_mix.wait()
    links.drain()


def run_forward(sizes, features, conv_shard, mix_shard, vectors_in, cotangent, scale):
    seq, fsdp = sizes
    rows, cin = features.shape
    cout = conv_shard.shape[1] * fsdp
    deep = conv_shard.shape[0]
    two = mix_shard.shape[0]
    shape = jax.ShapeDtypeStruct
    vmem = pl.BlockSpec(memory_space=pltpu.VMEM)
    hbm = pl.BlockSpec(memory_space=pl.ANY)
    copies = 120
    half = (rows, cin // 2)
    pool = Reduce.scratch(cout, cout)
    return pl.pallas_call(
        functools.partial(forward_kernel, sizes),
        out_shape=(
            shape((deep, cout), BF),
            shape((two, cout), BF),
            shape((cout, cout), BF),
            shape(half, BF),
            shape(half, BF),
            shape((cout // GROUP, cout), BF),
            shape((rows // 2, cout), BF),
            shape((rows, cin), BF),
            shape((rows, cout), BF),
            shape((8, cout), F32),
        ),
        in_specs=[vmem, hbm, hbm, vmem, vmem, vmem],
        out_specs=(hbm, hbm, hbm, hbm, hbm, vmem, vmem, vmem, vmem, vmem),
        scratch_shapes=[
            pltpu.VMEM((rows + 16, cout), F32),
            pltpu.VMEM((rows, deep), BF),
            pltpu.VMEM((2, deep, cout // fsdp), BF),
            pltpu.VMEM((two, cout), BF),
            pltpu.VMEM((rows, cout), F32),
            pltpu.VMEM((rows, cout), F32),
            pltpu.VMEM((rows, cout), F32),
            pltpu.VMEM((rows, cout), BF),
            pltpu.VMEM((rows, cout), BF),
            pltpu.VMEM((rows, cout), BF),
            pltpu.VMEM((cout, cout), BF),
            pltpu.VMEM((rows, 128), F32),
            pltpu.VMEM((rows, 128), F32),
            *pool,
            pltpu.VMEM((3, 2, 8, cout // 4), F32),
            pltpu.VMEM((3, seq, 8, cout // 4), F32),
            pltpu.VMEM((3, fsdp, 8, cout // 4), F32),
            pltpu.VMEM((fsdp, 8, cout // fsdp), F32),
            pltpu.VMEM((2, 16, cin), BF),
            pltpu.SemaphoreType.DMA((copies,)),
            pltpu.SemaphoreType.DMA((copies,)),
            pltpu.SemaphoreType.DMA((3, seq)),
            pltpu.SemaphoreType.DMA((3, seq)),
            pltpu.SemaphoreType.DMA((3, fsdp)),
            pltpu.SemaphoreType.DMA((3, fsdp)),
            pltpu.SemaphoreType.DMA((4 + fsdp,)),
        ],
        compiler_params=pltpu.CompilerParams(
            collective_id=0, has_side_effects=True, vmem_limit_bytes=62 * 2**20
        ),
    )(features, conv_shard, mix_shard, vectors_in, cotangent, scale)


class Reduce:
    def __init__(self, links, at, slot, buffers):
        self.links, self.at, self.slot = links, at, slot
        self.unit = slot.shape[0] // 16
        self.core_slot, self.from_x, self.from_y, self.from_yx, self.from_xy, self.own = buffers

    @staticmethod
    def scratch(height, width):
        unit = height // 16
        return [pltpu.VMEM((r, width), BF) for r in (8 * unit, 2 * unit, 2 * unit, unit, unit)]

    def _rows(self, start, count):
        return self.slot.at[ds(start * self.unit, count * self.unit, 16)]

    def _send(self, src, dst, device):
        return self.links.copy(src, dst, dst, device).start()

    def core(self):
        self.by_core = self._send(self._rows((1 - self.at.c) * 8, 8), self.core_slot, self.at.near(1))

    def _add(self, start, other, count, out=None):
        step = 16
        mine = self._rows(start, count)
        out = mine if out is None else out

        def body(r):
            v = mine[pl.ds(r, step), :].astype(F32) + other[pl.ds(r, step), :].astype(F32)
            out[pl.ds(r, step), :] = v.astype(BF)

        rows_loop(count * self.unit, step, body)

    def plane(self):
        at = self.at
        self.by_core.wait_recv()
        self._add(at.c * 8, self.core_slot, 8)
        self.a, self.b = at.c * 8, at.c * 8 + 4
        self.by_x = self._send(self._rows(self.a + (1 - at.x) * 2, 2), self.from_x, at.near(2))
        self.by_y = self._send(self._rows(self.b + (1 - at.y) * 2, 2), self.from_y, at.near(4))

    def cross(self):
        x, y = self.at.x, self.at.y
        a, b = self.a + x * 2, self.b + y * 2
        self.by_x.wait_recv()
        self._add(a, self.from_x, 2)
        self.by_yx = self._send(self._rows(a + 1 - y, 1), self.from_yx, self.at.near(4))
        self.by_y.wait_recv()
        self._add(b, self.from_y, 2)
        self.by_xy = self._send(self._rows(b + 1 - x, 1), self.from_xy, self.at.near(2))
        self.a, self.b = a + y, b + x

    def depth(self):
        self.by_yx.wait_recv()
        self._add(self.a, self.from_yx, 1, self.own.at[pl.ds(0, self.unit)])
        self.by_xy.wait_recv()
        self._add(self.b, self.from_xy, 1, self.own.at[pl.ds(self.unit, self.unit)])


class Along:
    def __init__(self, links, at, own, from_z, total):
        self.at, self.own, self.from_z, self.total = at, own, from_z, total
        self.width = total.shape[1]
        self.copies = []
        for d in range(1, at.fsdp_size):
            col = ds(lax.rem(at.z + d, at.fsdp_size) * self.width, self.width, 128)
            dst = from_z.at[d - 1]
            self.copies.append(links.copy(own.at[:, col], dst, dst, at.up(d)).start())

    def finish(self):
        col = ds(self.at.z * self.width, self.width, 128)
        for copy in self.copies:
            copy.wait_recv()

        def body(r):
            v = self.own[pl.ds(r, 16), col].astype(F32)
            for d in range(self.at.fsdp_size - 1):
                v = v + self.from_z[d, pl.ds(r, 16), :].astype(F32)
            self.total[pl.ds(r, 16), :] = v.astype(BF)

        rows_loop(self.own.shape[0], 16, body)


class Tap:
    def __init__(self, links, at, slot, buffers):
        self.links, self.at, self.slot = links, at, slot
        self.core_slot, self.from_x, self.from_y, self.own, self.from_z, self.total = buffers
        self.size = slot.shape[0] // 4
        self.half = slot.shape[1] // 2

    def core(self):
        at = self.at
        src = self.slot.at[ds((1 - at.c) * 2 * self.size, 2 * self.size, 16)]
        self.by_core = self.links.copy(src, self.core_slot, self.core_slot, at.near(1)).start()

    def plane(self):
        at, size, half = self.at, self.size, self.half
        self.by_core.wait_recv()
        start = at.c * 2 * size

        def body(r):
            row = ds(start + r, 16, 16)
            v = self.slot[row, :].astype(F32) + self.core_slot[pl.ds(r, 16), :].astype(F32)
            self.slot[row, :] = v.astype(BF)

        rows_loop(2 * size, 16, body)
        low = self.slot.at[ds(start + (1 - at.y) * size, size, 16), 0:half]
        high = self.slot.at[ds(start + (1 - at.x) * size, size, 16), half : 2 * half]
        self.by_y = self.links.copy(low, self.from_y, self.from_y, at.near(4)).start()
        self.by_x = self.links.copy(high, self.from_x, self.from_x, at.near(2)).start()

    def depth(self):
        at, size, half = self.at, self.size, self.half
        start = at.c * 2 * size
        for copy, mine, other, col in (
            (self.by_y, at.y, self.from_y, slice(0, half)),
            (self.by_x, at.x, self.from_x, slice(half, 2 * half)),
        ):
            copy.wait_recv()

            def body(r):
                v = self.slot[ds(start + mine * size + r, 16, 16), col].astype(F32) + other[pl.ds(r, 16), :].astype(F32)
                self.own[pl.ds(r, 16), col] = v.astype(BF)

            rows_loop(size, 16, body)
        self.along = Along(self.links, at, self.own, self.from_z, self.total)

    def finish(self):
        self.along.finish()


def backward_kernel(
    sizes,
    features,
    active_one,
    active_x,
    active_y,
    vectors,
    pool_own,
    middle_low,
    full_conv,
    term_mix,
    gathered,
    grad_features,
    sums_out,
    edged,
    edged_x,
    edged_y,
    ext,
    shifted,
    shifted_two,
    weight,
    grad_active,
    slots,
    core_slots,
    from_x,
    from_y,
    own,
    from_z,
    total,
    mix_slot,
    mix_core,
    mix_x,
    mix_y,
    mix_yx,
    mix_xy,
    mix_own,
    mix_z,
    mix_total,
    pool_z,
    pool_total,
    mine,
    seq_slots,
    fsdp_slots,
    send,
    recv,
    seq_send,
    seq_recv,
    fsdp_send,
    fsdp_recv,
    local,
):
    seq, fsdp = sizes
    at = Place(seq, fsdp)
    links = Links(send, recv)
    rows, cin = features.shape
    cout = full_conv.shape[1]
    taps = full_conv.shape[0] // cin
    all_rows = float(rows * seq * fsdp)
    lead = 16
    half_in, half_out = cin // 2, cout // 2
    pool_share, tap_share = cout // GROUP, cin // GROUP
    start_tap = 2 * pool_share
    share = start_tap + taps * tap_share

    def load_weight(i):
        return pltpu.make_async_copy(full_conv.at[pl.ds(i * half_in, half_in)], weight.at[i % 2], local.at[i % 2])

    load_weight(0).start()
    load_weight(1).start()
    load_mix = pltpu.make_async_copy(term_mix, mix_slot, local.at[2])
    load_middle = pltpu.make_async_copy(middle_low, edged.at[pl.ds(lead, rows)], local.at[3])
    load_middle.start()
    load_mix.start()
    at.barrier()
    top, bottom = pl.ds(0, lead), pl.ds(lead + rows, lead)
    below = links.copy(middle_low.at[top], edged.at[bottom], edged.at[bottom], at.up(fsdp - 1)).start()
    above = links.copy(middle_low.at[pl.ds(rows - lead, lead)], edged.at[top], edged.at[top], at.up(1)).start()

    def spread(block, start, order):
        size = block.shape[0]

        def place(part, half):
            first = order(part) * share + start
            if half is None:
                return gathered.at[ds(first, size, 16)]
            return gathered.at[ds(first + half * (size // 2), size // 2, 16)]

        keep = pltpu.make_async_copy(block, place(at.part, None), local.at[4 + len(groups)])
        groups.append((Spread(links, at, place, block), keep))
        groups[-1][0].one()
        keep.start()

    groups = []

    def tap_order(part):
        c, x, y = part & 1, (part >> 1) & 1, part >> 2
        low = at.z < fsdp // 2
        return jnp.where(low, x, y) * 4 + c * 2 + jnp.where(low, y, x)

    load_middle.wait()
    below.wait_recv()
    above.wait_recv()
    edged[top, :] = jnp.where(at.z > 0, edged[top, :], jnp.zeros((lead, cout), BF))
    edged[bottom, :] = jnp.where(at.z < fsdp - 1, edged[bottom, :], jnp.zeros((lead, cout), BF))
    to_x = links.copy(edged.at[:, 0:half_out], edged_x, edged_x, at.near(2)).start()
    to_y = links.copy(edged.at[:, half_out:cout], edged_y, edged_y, at.near(4)).start()
    pool = Along(links, at, pool_own, pool_z, pool_total)
    mix = Reduce(links, at, mix_slot, (mix_core, mix_x, mix_y, mix_yx, mix_xy, mix_own))
    load_mix.wait()
    mix.core()

    def widen(r):
        ext[pl.ds(r, 32), :] = edged[pl.ds(r, 32), :].astype(F32)

    rows_loop(rows + 2 * lead, 32, widen)
    half_width = (taps - 1) // 2

    def shift(target, k):
        start = lead + half_width - k

        def body(i, carry):
            col = ds(i * 128, 128, 128)
            target[:, col] = ext[pl.ds(start, rows), col].astype(BF)
            return carry

        lax.fori_loop(0, cout // 128, body, 0)

    def back(k):
        for i in (2 * k, 2 * k + 1):
            load_weight(i).wait()

            for j in range(2):
                at_row = j * (half_in // 2)
                col = slice((i % 2) * half_in + at_row, (i % 2) * half_in + at_row + half_in // 2)
                v = dot(shifted[k], weight[i % 2, at_row : at_row + half_in // 2, :], 1, 1)
                grad_active[:, col] = v if k == 0 else grad_active[:, col] + v
            if i + 2 < 2 * taps:
                load_weight(i + 2).start()

    for k in range(taps):
        shift(shifted.at[k], k)
        back(k)
        if k == 0:
            mix.plane()
        if k == 2:
            pool.finish()
            spread(pool_total, 0, lambda part: part)

    mean_one, scale_one, gain_one, shift_one = (vectors[i : i + 1, :cin] for i in range(4))

    def grad_before(r):
        normed = (features[pl.ds(r, 32), :].astype(F32) - mean_one) * scale_one
        v = normal(normed * gain_one + shift_one)[1] * grad_active[pl.ds(r, 32), :]
        grad_active[pl.ds(r, 32), :] = v
        return v, v * normed

    sum_shift, sum_gain = row_sums(rows, 32, cin, 2, grad_before)
    pad = jnp.zeros((1, cout - cin), F32)
    wide = lambda v: jnp.concatenate([v, pad], axis=1)
    sems = (seq_send, seq_recv, fsdp_send, fsdp_recv)
    stats = Exchange(at, mine, seq_slots, fsdp_slots, sems)
    stats.start(pack(wide(sum_shift), wide(sum_gain), vectors[6:7, :], vectors[7:8, :]))

    to_x.wait_recv()
    to_y.wait_recv()

    def widen_two(r):
        ext[pl.ds(r, 32), 0:half_out] = edged_x[pl.ds(r, 32), :].astype(F32)
        ext[pl.ds(r, 32), half_out:cout] = edged_y[pl.ds(r, 32), :].astype(F32)

    rows_loop(rows + 2 * lead, 32, widen_two)
    columns = (ds(at.x * half_in, half_in, 128), ds(at.y * half_in, half_in, 128))
    tile = 256

    def product(k):
        for i, other in enumerate((active_x, active_y)):

            def body(j, carry):
                col = ds(i * half_out + j * tile, tile, 128)
                v = dot(active_one[:, columns[i]], shifted[k, :, col], 0, 0)
                v = v + dot(other[...], shifted_two[:, col], 0, 0)
                slots[k, :, col] = v.astype(BF)
                return carry

            lax.fori_loop(0, half_out // tile, body, 0)

    steps = []
    for k in range(taps):
        mine_rows = pl.ds(k * tap_share, tap_share)
        steps.append(
            Tap(
                links,
                at,
                slots.at[k],
                (
                    core_slots.at[k],
                    from_x.at[mine_rows],
                    from_y.at[mine_rows],
                    own.at[mine_rows],
                    from_z.at[:, mine_rows],
                    total.at[mine_rows],
                ),
            )
        )

    def finish(k):
        steps[k].finish()
        spread(steps[k].total, start_tap + k * tap_share, tap_order)

    for k in range(taps):
        shift(shifted_two, k)
        product(k)
        steps[k].core()
        if k == 0:
            mix.cross()
            groups[0][0].two()
        if k == 1:
            stats.middle(combine_sums)
            groups[0][0].three()
        if k >= 1:
            steps[k - 1].plane()
        if k == 2:
            mix.depth()
            mix_along = Along(links, at, mix_own, mix_z, mix_total)
            everyone = unpack(stats.end(combine_sums))
        if k >= 2:
            steps[k - 2].depth()
    steps[taps - 1].plane()
    mix_along.finish()
    spread(mix_total, pool_share, lambda part: part)
    steps[taps - 2].depth()
    finish(0)
    shift_grad, gain_grad = everyone[0][:, :cin], everyone[1][:, :cin]

    def store(r):
        normed = (features[pl.ds(r, 32), :].astype(F32) - mean_one) * scale_one
        v = grad_active[pl.ds(r, 32), :] - shift_grad / all_rows - normed * gain_grad / all_rows
        grad_features[pl.ds(r, 32), :] = (gain_one * scale_one * v).astype(BF)

    rows_loop(rows, 32, store)
    sums_out[0:4, :] = jnp.concatenate(everyone, axis=0)
    steps[taps - 1].depth()
    groups[1][0].two()
    for k in range(1, taps):
        finish(k)
        groups[k][0].three()
        groups[k + 1][0].two()
    groups[taps][0].three()
    groups[taps + 1][0].two()
    groups[taps + 1][0].three()
    for group, keep in groups:
        group.four()
        keep.wait()
    links.drain()


def run_backward(sizes, features, active_one, active_x, active_y, vectors, pool_own, middle_low, full_conv, term_mix):
    seq, fsdp = sizes
    rows, cin = features.shape
    deep, cout = full_conv.shape
    taps = deep // cin
    width = cout // fsdp
    share = (deep + 2 * cout) // GROUP
    tap_share = cin // GROUP
    shape = jax.ShapeDtypeStruct
    vmem = pl.BlockSpec(memory_space=pltpu.VMEM)
    hbm = pl.BlockSpec(memory_space=pl.ANY)
    copies = 160
    return pl.pallas_call(
        functools.partial(backward_kernel, sizes),
        out_shape=(shape((GROUP * share, width), BF), shape((rows, cin), BF), shape((8, cout), F32)),
        in_specs=[vmem, vmem, vmem, vmem, vmem, vmem, hbm, hbm, hbm],
        out_specs=(hbm, vmem, vmem),
        scratch_shapes=[
            pltpu.VMEM((rows + 32, cout), BF),
            pltpu.VMEM((rows + 32, cout // 2), BF),
            pltpu.VMEM((rows + 32, cout // 2), BF),
            pltpu.VMEM((rows + 32, cout), F32),
            pltpu.VMEM((taps, rows, cout), BF),
            pltpu.VMEM((rows, cout), BF),
            pltpu.VMEM((2, cin // 2, cout), BF),
            pltpu.VMEM((rows, cin), F32),
            pltpu.VMEM((taps, cin // 2, cout), BF),
            pltpu.VMEM((taps, cin // 4, cout), BF),
            pltpu.VMEM((taps * tap_share, cout // 2), BF),
            pltpu.VMEM((taps * tap_share, cout // 2), BF),
            pltpu.VMEM((taps * tap_share, cout), BF),
            pltpu.VMEM((fsdp - 1, taps * tap_share, width), BF),
            pltpu.VMEM((taps * tap_share, width), BF),
            pltpu.VMEM((cout, cout), BF),
            *Reduce.scratch(cout, cout),
            pltpu.VMEM((cout // GROUP, cout), BF),
            pltpu.VMEM((fsdp - 1, cout // GROUP, width), BF),
            pltpu.VMEM((cout // GROUP, width), BF),
            pltpu.VMEM((fsdp - 1, cout // GROUP, width), BF),
            pltpu.VMEM((cout // GROUP, width), BF),
            pltpu.VMEM((2, 16, cout // 4), F32),
            pltpu.VMEM((seq, 16, cout // 4), F32),
            pltpu.VMEM((fsdp, 16, cout // 4), F32),
            pltpu.SemaphoreType.DMA((copies,)),
            pltpu.SemaphoreType.DMA((copies,)),
            pltpu.SemaphoreType.DMA((seq,)),
            pltpu.SemaphoreType.DMA((seq,)),
            pltpu.SemaphoreType.DMA((fsdp,)),
            pltpu.SemaphoreType.DMA((fsdp,)),
            pltpu.SemaphoreType.DMA((6 + taps,)),
        ],
        compiler_params=pltpu.CompilerParams(
            collective_id=1, has_side_effects=True, vmem_limit_bytes=62 * 2**20
        ),
    )(features, active_one, active_x, active_y, vectors, pool_own, middle_low, full_conv, term_mix)


def spread_sum(v):
    size = lax.axis_size("seq")
    bit = GROUP
    while bit < size:
        v = v + lax.ppermute(v, "seq", [(i, i ^ bit) for i in range(size)])
        bit *= 2
    return v


def on_device(
    features,
    conv_weight,
    mix_weight,
    pool_weight,
    gain_first,
    shift_first,
    gain_second,
    shift_second,
    bias_conv,
    bias_mix,
    cotangent,
    track_counts,
):
    rows, cin = features.shape
    seq, fsdp = lax.axis_size("seq"), lax.axis_size("fsdp")
    position = lax.axis_index(("seq", "fsdp"))
    owner = lax.axis_index("fsdp")
    window = position * rows // WIN
    width = conv_weight.shape[2]
    cout = width * fsdp
    taps = conv_weight.shape[0]
    scale = lax.dynamic_slice_in_dim(track_counts, window, 1).astype(F32) / TRACKS
    scale = jnp.broadcast_to(scale[:, None], (1, cout))
    rest = ((0, width - gain_first.shape[0]),)
    own_vectors = [jnp.pad(gain_first, rest), jnp.pad(shift_first, rest), gain_second, shift_second, bias_conv, bias_mix]
    own_vectors = jnp.stack(own_vectors + [jnp.zeros_like(bias_mix)] * 2).astype(F32)
    full_conv, _, term_mix, active_x, active_y, pool_own, pooled, active_one, middle_low, vectors = run_forward(
        (seq, fsdp),
        features,
        conv_weight.reshape(taps * cin, width),
        jnp.concatenate([mix_weight, pool_weight], axis=0),
        own_vectors,
        cotangent,
        scale,
    )
    gathered, grad_features, sums = run_backward(
        (seq, fsdp), features, active_one, active_x, active_y, vectors, pool_own, middle_low, full_conv, term_mix
    )
    parts = spread_sum(gathered.reshape(GROUP, -1, width).astype(F32))
    taken = 0
    products = []
    for height in [cout, cout] + [cin] * taps:
        size = height // GROUP
        products.append(parts[:, taken : taken + size].reshape(height, width))
        taken += size
    grad_pool, grad_mix = products[:2]
    grad_conv = jnp.stack(products[2:])
    shift_two_grad, gain_two_grad = vectors[4], vectors[5]
    shift_one_grad, gain_one_grad, bias_one_grad, bias_two_grad = sums[0], sums[1], sums[2], sums[3]

    def share(v, size):
        return lax.dynamic_slice_in_dim(v, owner * size, size)

    first, second = gain_first.shape[0], gain_second.shape[0]
    return (
        pooled,
        grad_features,
        grad_conv,
        grad_mix,
        grad_pool,
        share(gain_one_grad, first),
        share(shift_one_grad, first),
        share(gain_two_grad, second),
        share(shift_two_grad, second),
        share(bias_one_grad, second),
        share(bias_two_grad, second),
    )


def solution(mesh):
    rows = P(("seq", "fsdp"), None)
    vector = P("fsdp")
    in_specs = (rows, P(None, None, "fsdp"), P(None, "fsdp"), P(None, "fsdp")) + (vector,) * 6 + (rows, P())
    out_specs = (rows, rows, P(None, None, "fsdp"), P(None, "fsdp"), P(None, "fsdp")) + (vector,) * 6
    return jax.shard_map(on_device, mesh=mesh, in_specs=in_specs, out_specs=out_specs, check_vma=False)
```

```python
import functools
import math
import jax
import jax.numpy as jnp
from jax import lax
from jax.experimental import pallas as pl
from jax.experimental.pallas import tpu as pltpu
from jax.sharding import PartitionSpec as P

TRACKS = 5313
WIN = 2048
EPSILON = 1e-05
MESH = pl.DeviceIdType.MESH
BF = jnp.bfloat16
F32 = jnp.float32
GROUP = 8


def dot(a, b, ca, cb):
    return lax.dot_general(a, b, (((ca,), (cb,)), ((), ())), preferred_element_type=F32)


def ds(start, size, step):
    return pl.ds(pl.multiple_of(start, step), size)


def fold(v):
    rows, width = v.shape
    return jnp.sum(v.reshape(rows // 8, 8, width), axis=0)


def rows_loop(total, step, body):
    def run(i, carry):
        body(pl.multiple_of(i * step, step))
        return carry

    lax.fori_loop(0, total // step, run, 0)


def row_sums(total, step, width, count, body):
    def run(i, carry):
        parts = body(pl.multiple_of(i * step, step))
        return tuple(c + fold(v) for c, v in zip(carry, parts))

    zero = tuple(jnp.zeros((8, width), F32) for _ in range(count))
    sums = lax.fori_loop(0, total // step, run, zero)
    return [jnp.sum(v, axis=0, keepdims=True) for v in sums]


def normal(b):
    cdf = 0.5 * (1.0 + lax.erf(b * math.sqrt(0.5)))
    pdf = jnp.exp(-0.5 * b * b) * (1.0 / math.sqrt(2.0 * math.pi))
    return cdf, cdf + b * pdf


class Copy:
    def __init__(self, links, src, there, here, device):
        i = links.count
        links.count += 1
        send, recv = links.send.at[i], links.recv.at[i]

        def make(dst):
            return pltpu.make_async_remote_copy(
                src_ref=src,
                dst_ref=dst,
                send_sem=send,
                recv_sem=recv,
                device_id=device,
                device_id_type=MESH,
            )

        self.links = links
        self.out, self.into = functools.partial(make, there), functools.partial(make, here)

    def start(self):
        self.out().start()
        self.links.started.append(self)
        return self

    def wait_recv(self):
        self.into().wait_recv()

    def wait_send(self):
        self.out().wait_send()


class Links:
    def __init__(self, send, recv):
        self.send, self.recv = send, recv
        self.count = 0
        self.started = []

    def copy(self, src, there, here, device):
        return Copy(self, src, there, here, device)

    def drain(self):
        for item in self.started:
            item.wait_send()
        self.started = []


class Place:
    def __init__(self, seq, fsdp):
        self.seq_size, self.fsdp_size = seq, fsdp
        self.s, self.z = lax.axis_index("seq"), lax.axis_index("fsdp")
        self.part = lax.rem(self.s, GROUP)
        self.base = self.s - self.part
        self.c, self.x, self.y = self.part & 1, (self.part >> 1) & 1, self.part >> 2

    def near(self, mask):
        return (self.base + jnp.bitwise_xor(self.part, mask), self.z)

    def up(self, d):
        return (self.s, lax.rem(self.z + d, self.fsdp_size))

    def barrier(self):
        bar = pltpu.get_barrier_semaphore()

        def greet(i, carry):
            peer = lax.rem(self.s + i, self.seq_size)
            pl.semaphore_signal(bar, inc=1, device_id=(peer, self.z), device_id_type=MESH)
            return carry

        lax.fori_loop(1, self.seq_size, greet, 0)
        for d in range(1, self.fsdp_size):
            pl.semaphore_signal(bar, inc=1, device_id=self.up(d), device_id_type=MESH)
        pl.semaphore_wait(bar, self.seq_size + self.fsdp_size - 2)


class Exchange:
    def __init__(self, place, mine, seq_slots, fsdp_slots, sems):
        self.place, self.mine = place, mine
        self.seq_slots, self.fsdp_slots = seq_slots, fsdp_slots
        self.seq_send, self.seq_recv, self.fsdp_send, self.fsdp_recv = sems

    def _copy(self, i, stage):
        at = self.place
        if stage == 0:
            peer = lax.rem(at.s + i, at.seq_size)
            source = lax.rem(at.s - i + at.seq_size, at.seq_size)
            device, slots, send, recv, me = (peer, at.z), self.seq_slots, self.seq_send, self.seq_recv, at.s
        else:
            peer = lax.rem(at.z + i, at.fsdp_size)
            source = lax.rem(at.z - i + at.fsdp_size, at.fsdp_size)
            device, slots, send, recv, me = (at.s, peer), self.fsdp_slots, self.fsdp_send, self.fsdp_recv, at.z
        make = lambda slot: pltpu.make_async_remote_copy(
            src_ref=self.mine.at[stage],
            dst_ref=slots.at[slot],
            send_sem=send.at[i],
            recv_sem=recv.at[i],
            device_id=device,
            device_id_type=MESH,
        )
        return functools.partial(make, me), functools.partial(make, source)

    def _each(self, stage, what):
        size = self.place.seq_size if stage == 0 else self.place.fsdp_size

        def run(i, carry):
            what(*self._copy(i, stage))
            return carry

        lax.fori_loop(1, size, run, 0)

    def start(self, block):
        self.mine[0] = block
        self.seq_slots[self.place.s] = block
        self._each(0, lambda out, into: out().start())

    def middle(self, combine):
        self._each(0, lambda out, into: into().wait_recv())
        block = combine(self.seq_slots)
        self.mine[1] = block
        self.fsdp_slots[self.place.z] = block
        self._each(1, lambda out, into: out().start())

    def end(self, combine):
        self._each(1, lambda out, into: into().wait_recv())
        block = combine(self.fsdp_slots)
        self._each(0, lambda out, into: out().wait_send())
        self._each(1, lambda out, into: out().wait_send())
        return block

    def finish(self, combine):
        self.middle(combine)
        return self.end(combine)


def pack(*vectors):
    width = vectors[0].shape[1] // 4
    pieces = [v[:, i * width : (i + 1) * width] for v in vectors for i in range(4)]
    return jnp.concatenate(pieces, axis=0)


def unpack(block):
    count = block.shape[0] // 4
    return [jnp.concatenate([block[4 * j + i : 4 * j + i + 1] for i in range(4)], axis=1) for j in range(count)]


def combine_sums(slots):
    return jnp.sum(slots[...], axis=0)


def combine_moments(slots):
    v = slots[...]
    center, spread = v[:, :4], v[:, 4:]
    mean = jnp.mean(center, axis=0)
    rest = jnp.mean(spread + jnp.square(center - mean[None]), axis=0)
    return jnp.concatenate([mean, rest], axis=0)


class Spread:
    def __init__(self, links, at, place, source=None):
        self.links, self.at, self.place, self.source = links, at, place, source
        self.held = {}

    def _send(self, name, mask, of, half=None):
        part = self.at.part
        mine = self.place(jnp.bitwise_xor(part, of), half)
        theirs = self.place(jnp.bitwise_xor(part, of ^ mask), half)
        src = mine if of or self.source is None else self.source
        self.held[name] = self.links.copy(src, mine, theirs, self.at.near(mask)).start()

    def one(self):
        self._send("x", 2, 0)
        self._send("y", 4, 0)
        self._send("c", 1, 0)

    def two(self):
        self.held["x"].wait_recv()
        self._send("xa", 4, 2, 0)
        self._send("xc", 1, 2)
        self.held["y"].wait_recv()
        self._send("yb", 2, 4, 1)
        self._send("yc", 1, 4)

    def three(self):
        self.held["xa"].wait_recv()
        self._send("ac", 1, 6, 0)
        self.held["yb"].wait_recv()
        self._send("bc", 1, 6, 1)

    def four(self):
        for name in ("c", "xc", "yc", "ac", "bc"):
            self.held[name].wait_recv()


class Gather:
    def __init__(self, links, at, shard, full, d, lo, size):
        self.links, self.at, self.shard, self.full, self.d = links, at, shard, full, d
        self.lo, self.size = lo, size
        self.share, self.width = shard.shape[0] // GROUP, shard.shape[1]
        self.z = lax.rem(at.z - d + at.fsdp_size, at.fsdp_size)
        spread = Spread(links, at, lambda part, half: self.full.at[self._rows(part, half), self._columns(self.z)])
        self.spread, self.two, self.three, self.four = spread, spread.two, spread.three, spread.four

    def _rows(self, part, half=None):
        start = part * self.share + self.lo
        if half is None:
            return ds(start, self.size, 16)
        return ds(start + half * (self.size // 2), self.size // 2, 16)

    def _columns(self, z):
        return ds(z * self.width, self.width, 128)

    def send(self):
        at = self.at
        rows = self._rows(at.part)
        passed = self._columns(lax.rem(self.z + 1, at.fsdp_size))
        there = self.full.at[rows, passed]
        here = self.full.at[rows, self._columns(self.z)]
        src = self.shard.at[rows] if self.d == 1 else there
        self.along = self.links.copy(src, there, here, at.up(1)).start()

    def arrive(self):
        self.along.wait_recv()

    def one(self):
        self.arrive()
        self.spread.one()


def put_blocks(target, half, values, col):
    size = values.shape[0] // 8
    for i in range(8):
        part, side = 4 * half + i // 2, i % 2
        c, x, y = part & 1, part >> 1 & 1, part >> 2
        at = 8 * c + 4 * side + (2 * x + y if side == 0 else 2 * y + x)
        target[at * size : (at + 1) * size, col] = values[i * size : (i + 1) * size].astype(BF)


def forward_kernel(
    sizes,
    features,
    conv_shard,
    mix_shard,
    pool_shard,
    vectors_in,
    cotangent,
    scale,
    full_conv,
    full_mix,
    full_pool,
    term_mix,
    active_x,
    active_y,
    pool_own,
    pooled,
    active_out,
    middle_low,
    vectors,
    ext,
    taps,
    wbuf,
    mixw,
    middle,
    deriv,
    work,
    a2,
    low,
    low2,
    gbuf,
    pair_one,
    pair_two,
    pool_core,
    pool_x,
    pool_y,
    pool_yx,
    pool_xy,
    mine,
    seq_slots,
    fsdp_slots,
    packs,
    edges,
    send,
    recv,
    seq_send,
    seq_recv,
    fsdp_send,
    fsdp_recv,
    local,
):
    seq, fsdp = sizes
    at = Place(seq, fsdp)
    links = Links(send, recv)
    rows, cin = features.shape
    cout = full_conv.shape[1]
    width = cout // fsdp
    total = float(rows * seq * fsdp)
    taps_count = conv_shard.shape[0] // cin
    lead = 8

    def exchange(i):
        sems = (seq_send.at[i], seq_recv.at[i], fsdp_send.at[i], fsdp_recv.at[i])
        return Exchange(at, mine.at[i], seq_slots.at[i], fsdp_slots.at[i], sems)

    own_conv = pltpu.make_async_copy(wbuf.at[0], full_conv.at[:, ds(at.z * width, width, 128)], local.at[0])
    mixing, pooling = pl.ds(0, cout), pl.ds(cout, cout)
    own_mix = pltpu.make_async_copy(mix_shard, mixw.at[mixing, ds(at.z * width, width, 128)], local.at[1])
    own_pool = pltpu.make_async_copy(pool_shard, mixw.at[pooling, ds(at.z * width, width, 128)], local.at[4])
    own_load = pltpu.make_async_copy(conv_shard, wbuf.at[0], local.at[2])

    at.barrier()
    near = range(1, fsdp)
    share = conv_shard.shape[0] // GROUP
    cut = share * 3 // 5 // 32 * 32
    conv = [Gather(links, at, conv_shard, full_conv, d, *piece) for d in near for piece in ((0, cut), (cut, share - cut))]
    mix, poolw = (
        [Gather(links, at, shard, full, d, 0, cout // GROUP) for d in near]
        for shard, full in ((mix_shard, full_mix), (pool_shard, full_pool))
    )
    parcels = []
    for d in near:
        source = lax.rem(at.z - d + fsdp, fsdp)
        parcels.append(links.copy(vectors_in, packs.at[at.z], packs.at[source], at.up(d)).start())
    parcels.append(links.copy(features.at[pl.ds(0, 16)], edges.at[1], edges.at[1], at.up(fsdp - 1)).start())
    parcels.append(links.copy(features.at[pl.ds(rows - 16, 16)], edges.at[0], edges.at[0], at.up(1)).start())
    conv[0].send()
    own_load.start()
    own_mix.start()
    own_pool.start()

    (sum_one,) = row_sums(rows, 64, cin, 1, lambda r: (features[pl.ds(r, 64), :].astype(F32),))
    mean = sum_one / rows
    (dev_one,) = row_sums(rows, 64, cin, 1, lambda r: (jnp.square(features[pl.ds(r, 64), :].astype(F32) - mean),))
    pad = jnp.zeros((1, cout - cin), F32)
    stats = exchange(0)
    stats.start(pack(jnp.concatenate([mean, pad], axis=1), jnp.concatenate([dev_one / rows, pad], axis=1)))
    packs[at.z] = vectors_in[...]
    stats.middle(combine_moments)
    conv[0].one()
    for parcel in parcels:
        parcel.wait_recv()
    everyone = packs[...]
    share_in = cin // fsdp
    gain_one, shift_one = (jnp.concatenate([everyone[z, i : i + 1, :share_in] for z in range(fsdp)], axis=1) for i in range(2))
    gain_two, shift_two, bias_one, bias_two = (
        jnp.concatenate([everyone[z, i : i + 1] for z in range(fsdp)], axis=1) for i in range(2, 6)
    )
    mean_one, var_one = unpack(stats.end(combine_moments))
    conv[1].send()
    conv[2].send()
    mean_one, scale_one = mean_one[:, :cin], lax.rsqrt(var_one[:, :cin] + EPSILON)

    def active(v):
        b = (v - mean_one) * scale_one * gain_one + shift_one
        return b * (0.5 * (1.0 + lax.erf(b * math.sqrt(0.5))))

    def first_active(r):
        v = active(features[pl.ds(r, 32), :].astype(F32)).astype(BF)
        active_out[pl.ds(r, 32), :] = v
        ext[pl.ds(lead + r, 32), :cin] = v.astype(F32)

    rows_loop(rows, 32, first_active)
    conv[1].one()
    conv[3].send()
    conv[0].two()
    row = lax.broadcasted_iota(jnp.int32, (8, cin), 0)
    before, after = edges[0].astype(F32)[8:16], edges[1].astype(F32)[0:8]
    ext[0:lead, :cin] = jnp.where((row >= 6) & (at.z > 0), active(before), 0.0)
    ext[lead + rows : lead + rows + 8, :cin] = jnp.where((row < 2) & (at.z < fsdp - 1), active(after), 0.0)
    def shifted(k):
        def body(i, carry):
            col = ds(i * 128, 128, 128)
            taps[:, ds(k * cin + i * 128, 128, 128)] = ext[pl.ds(lead - 2 + k, rows), col].astype(BF)
            return carry

        lax.fori_loop(0, cin // 128, body, 0)

    for k in range(taps_count):
        shifted(k)
    conv[2].one()
    conv[4].send()
    conv[1].two()
    conv[0].three()

    def load_block(slot, z):
        copy = pltpu.make_async_copy(full_conv.at[:, ds(z * width, width, 128)], wbuf.at[slot], local.at[3])
        copy.start()
        return copy

    def multiply(slot, z, half):
        row = pl.ds(half * (rows // 2), rows // 2)
        middle[row, ds(z * width, width, 128)] = dot(taps[row, :], wbuf[slot], 1, 0)

    def load_later(part, i, target):
        col = ds(part[i].z * width, width, 128)
        copy = pltpu.make_async_copy(part[i].full.at[:, col], mixw.at[target, col], local.at[5 + i])
        copy.start()
        return copy

    own_load.wait()
    own_conv.start()
    multiply(0, at.z, 0)
    conv[3].one()
    conv[5].send()
    conv[2].two()
    conv[1].three()
    conv[0].four()
    multiply(0, at.z, 1)
    own_conv.wait()
    conv[4].one()
    mix[0].send()
    conv[3].two()
    conv[2].three()
    conv[1].four()
    block = load_block(1, conv[0].z)
    conv[5].one()
    poolw[0].send()
    conv[4].two()
    conv[3].three()
    conv[2].four()
    block.wait()
    multiply(1, conv[0].z, 0)
    mix[0].one()
    mix[1].send()
    conv[5].two()
    conv[4].three()
    conv[3].four()
    block = load_block(0, conv[2].z)
    multiply(1, conv[0].z, 1)
    mix[1].one()
    mix[2].send()
    block.wait()
    multiply(0, conv[2].z, 0)
    conv[5].three()
    conv[4].four()
    multiply(0, conv[2].z, 1)
    mix[0].two()
    mix[2].one()
    poolw[0].arrive()
    poolw[1].send()
    conv[5].four()
    block = load_block(1, conv[4].z)
    mix[1].two()
    mix[0].three()
    poolw[0].spread.one()
    block.wait()
    multiply(1, conv[4].z, 0)
    mix[1].three()
    mix[2].two()
    poolw[1].arrive()
    poolw[2].send()
    multiply(1, conv[4].z, 1)
    poolw[0].two()
    mix[2].three()

    def plus_bias(r):
        v = middle[pl.ds(r, 32), :] + bias_one
        middle[pl.ds(r, 32), :] = v
        return (v,)

    (sum_two,) = row_sums(rows, 32, cout, 1, plus_bias)
    mean = sum_two / rows
    (dev_two,) = row_sums(rows, 32, cout, 1, lambda r: (jnp.square(middle[pl.ds(r, 32), :] - mean),))
    stats = exchange(1)
    stats.start(pack(mean, dev_two / rows))
    for part in mix:
        part.four()
    loads = [load_later(mix, i, mixing) for i in range(fsdp - 1)]
    stats.middle(combine_moments)
    poolw[1].spread.one()
    poolw[2].one()
    mean_two, var_two = unpack(stats.end(combine_moments))
    scale_two = lax.rsqrt(var_two + EPSILON)

    def second_active(r):
        b = (middle[pl.ds(r, 32), :] - mean_two) * scale_two * gain_two + shift_two
        cdf, slope = normal(b)
        a2[pl.ds(r, 32), :] = (b * cdf).astype(BF)
        deriv[pl.ds(r, 32), :] = slope

    rows_loop(rows // 2, 32, second_active)
    poolw[0].three()
    poolw[1].two()
    rows_loop(rows // 2, 32, lambda r: second_active(rows // 2 + r))
    poolw[2].two()
    poolw[1].three()
    own_mix.wait()
    for load in loads:
        load.wait()

    tile = 512
    tiles = cout // tile

    def column_loop(body):
        def run(i, carry):
            body(ds(i * tile, tile, 128))
            return carry

        lax.fori_loop(0, tiles, run, 0)

    def add_mix(col):
        work[:, col] = dot(a2[...], mixw[0:cout, col], 1, 0)

    column_loop(add_mix)
    poolw[2].three()

    def add_residual(r):
        v = middle[pl.ds(r, 32), :] + work[pl.ds(r, 32), :] + bias_two
        ext[pl.ds(r, 32), :] = v
        low[pl.ds(r, 32), :] = v.astype(BF)

    rows_loop(rows, 32, add_residual)

    def add_pool(col):
        work[:, col] = dot(low[...], mixw[cout : 2 * cout, col], 1, 0)

    for part in poolw:
        part.four()
    loads = [load_later(poolw, i, pooling) for i in range(fsdp - 1)]
    half = cin // 2
    actives = [
        links.copy(active_out.at[:, ds((1 - at.x) * half, half, 128)], active_x, active_x, at.near(2)).start(),
        links.copy(active_out.at[:, ds((1 - at.y) * half, half, 128)], active_y, active_y, at.near(4)).start(),
    ]
    own_pool.wait()
    for load in loads:
        load.wait()
    column_loop(add_pool)

    def pairs(i, carry):
        col = ds(i * 128, 128, 128)
        even, odd = pl.ds(0, rows // 2, 2), pl.ds(1, rows // 2, 2)
        one, two = pair_one, pair_two
        one[...], two[...] = work[:, col], ext[0:rows, col]
        l0, l1 = one[even, :], one[odd, :]
        s0, s1 = two[even, :], two[odd, :]
        top = jnp.maximum(l0, l1)
        e0, e1 = jnp.exp(l0 - top), jnp.exp(l1 - top)
        inverse = 1.0 / (e0 + e1)
        w0, w1 = e0 * inverse, e1 * inverse
        up = cotangent[:, col].astype(F32) * scale[:, col]
        pooled[:, col] = (w0 * s0 + w1 * s1).astype(BF)
        g0, g1 = s0 * up, s1 * up
        both = w0 * g0 + w1 * g1
        one[even, :] = w0 * up
        one[odd, :] = w1 * up
        two[even, :] = w0 * (g0 - both)
        two[odd, :] = w1 * (g1 - both)
        work[:, col] = one[...]
        low2[:, col] = two[...].astype(BF)
        return carry

    lax.fori_loop(0, cout // 128, pairs, 0)

    def product(left, right, gbuf):
        half = cout // 2
        for i in range(2):
            def body(j, carry):
                col = ds(j * tile, tile, 128)
                put_blocks(gbuf, i, dot(left[:, i * half : (i + 1) * half], right[:, col], 0, 0), col)
                return carry

            lax.fori_loop(0, tiles, body, 0)

    product(low, low2, gbuf)
    pool_buffers = (pool_core, pool_x, pool_y, pool_yx, pool_xy, pool_own)
    pool = Reduce(links, at, gbuf, pool_buffers)
    pool.core()

    def back_pool(col):
        ext[0:rows, col] = dot(low2[...], mixw[ds(cout + col.start, tile, 128), :], 1, 1)

    column_loop(back_pool)

    def grad_summed(r):
        v = work[pl.ds(r, 32), :] + ext[pl.ds(r, 32), :]
        work[pl.ds(r, 32), :] = v
        low[pl.ds(r, 32), :] = v.astype(BF)
        return (v,)

    pool.plane()
    (sum_bias_two,) = row_sums(rows, 32, cout, 1, grad_summed)

    def back_mix(col):
        ext[0:rows, col] = dot(low[...], mixw[ds(col.start, tile, 128), :], 1, 1)

    column_loop(back_mix)

    def normed(r):
        return (middle[pl.ds(r, 32), :] - mean_two) * scale_two

    def grad_before(r):
        v = ext[pl.ds(r, 32), :] * deriv[pl.ds(r, 32), :]
        ext[pl.ds(r, 32), :] = v
        return v, v * normed(r)

    sum_shift, sum_gain = row_sums(rows, 32, cout, 2, grad_before)
    stats = exchange(2)
    stats.start(pack(sum_shift, sum_gain))
    product(a2, low, mixw.at[pooling])
    out_mix = pltpu.make_async_copy(mixw.at[pooling], term_mix, local.at[4])
    out_mix.start()
    stats.middle(combine_sums)
    pool.cross()
    shift_two_grad, gain_two_grad = unpack(stats.end(combine_sums))

    def grad_middle(r):
        v = work[pl.ds(r, 32), :] + gain_two * scale_two * (
            ext[pl.ds(r, 32), :] - shift_two_grad / total - normed(r) * gain_two_grad / total
        )
        middle_low[pl.ds(r, 32), :] = v.astype(BF)
        return (v,)

    (sum_bias_one,) = row_sums(rows, 32, cout, 1, grad_middle)
    fill = lambda v: jnp.concatenate([v, pad], axis=1)
    vectors[0:8, :] = jnp.concatenate(
        [fill(mean_one), fill(scale_one), fill(gain_one), fill(shift_one), shift_two_grad, gain_two_grad, sum_bias_one, sum_bias_two],
        axis=0,
    )
    pool.depth()
    for copy in actives:
        copy.wait_recv()
    out_mix.wait()
    links.drain()


def run_forward(sizes, features, conv_shard, mix_shard, pool_shard, vectors_in, cotangent, scale):
    seq, fsdp = sizes
    rows, cin = features.shape
    cout = conv_shard.shape[1] * fsdp
    deep = conv_shard.shape[0]
    two = 2 * cout
    shape = jax.ShapeDtypeStruct
    vmem = pl.BlockSpec(memory_space=pltpu.VMEM)
    hbm = pl.BlockSpec(memory_space=pl.ANY)
    copies = 140
    half = (rows, cin // 2)
    pool = Reduce.scratch(cout, cout)
    return pl.pallas_call(
        functools.partial(forward_kernel, sizes),
        out_shape=(
            shape((deep, cout), BF),
            shape((cout, cout), BF),
            shape((cout, cout), BF),
            shape((cout, cout), BF),
            shape(half, BF),
            shape(half, BF),
            shape((cout // GROUP, cout), BF),
            shape((rows // 2, cout), BF),
            shape((rows, cin), BF),
            shape((rows, cout), BF),
            shape((8, cout), F32),
        ),
        in_specs=[vmem, hbm, hbm, hbm, vmem, vmem, vmem],
        out_specs=(hbm, hbm, hbm, hbm, hbm, hbm, vmem, vmem, vmem, vmem, vmem),
        scratch_shapes=[
            pltpu.VMEM((rows + 16, cout), F32),
            pltpu.VMEM((rows, deep), BF),
            pltpu.VMEM((2, deep, cout // fsdp), BF),
            pltpu.VMEM((two, cout), BF),
            pltpu.VMEM((rows, cout), F32),
            pltpu.VMEM((rows, cout), F32),
            pltpu.VMEM((rows, cout), F32),
            pltpu.VMEM((rows, cout), BF),
            pltpu.VMEM((rows, cout), BF),
            pltpu.VMEM((rows, cout), BF),
            pltpu.VMEM((cout, cout), BF),
            pltpu.VMEM((rows, 128), F32),
            pltpu.VMEM((rows, 128), F32),
            *pool,
            pltpu.VMEM((3, 2, 8, cout // 4), F32),
            pltpu.VMEM((3, seq, 8, cout // 4), F32),
            pltpu.VMEM((3, fsdp, 8, cout // 4), F32),
            pltpu.VMEM((fsdp, 8, cout // fsdp), F32),
            pltpu.VMEM((2, 16, cin), BF),
            pltpu.SemaphoreType.DMA((copies,)),
            pltpu.SemaphoreType.DMA((copies,)),
            pltpu.SemaphoreType.DMA((3, seq)),
            pltpu.SemaphoreType.DMA((3, seq)),
            pltpu.SemaphoreType.DMA((3, fsdp)),
            pltpu.SemaphoreType.DMA((3, fsdp)),
            pltpu.SemaphoreType.DMA((4 + fsdp,)),
        ],
        compiler_params=pltpu.CompilerParams(
            collective_id=0, has_side_effects=True, vmem_limit_bytes=62 * 2**20
        ),
    )(features, conv_shard, mix_shard, pool_shard, vectors_in, cotangent, scale)


class Reduce:
    def __init__(self, links, at, slot, buffers):
        self.links, self.at, self.slot = links, at, slot
        self.unit = slot.shape[0] // 16
        self.core_slot, self.from_x, self.from_y, self.from_yx, self.from_xy, self.own = buffers

    @staticmethod
    def scratch(height, width):
        unit = height // 16
        return [pltpu.VMEM((r, width), BF) for r in (8 * unit, 2 * unit, 2 * unit, unit, unit)]

    def _rows(self, start, count):
        return self.slot.at[ds(start * self.unit, count * self.unit, 16)]

    def _send(self, src, dst, device):
        return self.links.copy(src, dst, dst, device).start()

    def core(self):
        self.by_core = self._send(self._rows((1 - self.at.c) * 8, 8), self.core_slot, self.at.near(1))

    def _add(self, start, other, count, out=None):
        step = 16
        mine = self._rows(start, count)
        out = mine if out is None else out

        def body(r):
            v = mine[pl.ds(r, step), :].astype(F32) + other[pl.ds(r, step), :].astype(F32)
            out[pl.ds(r, step), :] = v.astype(BF)

        rows_loop(count * self.unit, step, body)

    def plane(self):
        at = self.at
        self.by_core.wait_recv()
        self._add(at.c * 8, self.core_slot, 8)
        self.a, self.b = at.c * 8, at.c * 8 + 4
        self.by_x = self._send(self._rows(self.a + (1 - at.x) * 2, 2), self.from_x, at.near(2))
        self.by_y = self._send(self._rows(self.b + (1 - at.y) * 2, 2), self.from_y, at.near(4))

    def cross(self):
        x, y = self.at.x, self.at.y
        a, b = self.a + x * 2, self.b + y * 2
        self.by_x.wait_recv()
        self._add(a, self.from_x, 2)
        self.by_yx = self._send(self._rows(a + 1 - y, 1), self.from_yx, self.at.near(4))
        self.by_y.wait_recv()
        self._add(b, self.from_y, 2)
        self.by_xy = self._send(self._rows(b + 1 - x, 1), self.from_xy, self.at.near(2))
        self.a, self.b = a + y, b + x

    def depth(self):
        self.by_yx.wait_recv()
        self._add(self.a, self.from_yx, 1, self.own.at[pl.ds(0, self.unit)])
        self.by_xy.wait_recv()
        self._add(self.b, self.from_xy, 1, self.own.at[pl.ds(self.unit, self.unit)])


class Along:
    def __init__(self, links, at, own, from_z, total):
        self.links, self.at, self.own, self.from_z, self.total = links, at, own, from_z, total
        self.width = total.shape[1]
        self.last = at.fsdp_size - 2

    def _column(self, back):
        at = self.at
        return ds(lax.rem(at.z - back + at.fsdp_size, at.fsdp_size) * self.width, self.width, 128)

    def _send(self, src, i):
        dst = self.from_z.at[i]
        self.copy = self.links.copy(src, dst, dst, self.at.up(1)).start()

    def _add(self, i, back, out):
        self.copy.wait_recv()
        col = self._column(back)

        def body(r):
            v = self.own[pl.ds(r, 16), col].astype(F32) + self.from_z[i, pl.ds(r, 16), :].astype(F32)
            out[pl.ds(r, 16), :] = v.astype(BF)

        rows_loop(self.own.shape[0], 16, body)

    def start(self):
        self._send(self.own.at[:, self._column(1)], 0)
        return self

    def hop(self, i):
        self._add(i, i + 2, self.from_z.at[i])
        self._send(self.from_z.at[i], i + 1)

    def finish(self):
        self._add(self.last, 0, self.total)


class Tap:
    def __init__(self, links, at, slot, buffers):
        self.links, self.at, self.slot = links, at, slot
        self.core_slot, self.from_x, self.from_y, self.own, self.from_z, self.total = buffers
        self.size = slot.shape[0] // 4
        self.half = slot.shape[1] // 2

    def core(self):
        at = self.at
        src = self.slot.at[ds((1 - at.c) * 2 * self.size, 2 * self.size, 16)]
        self.by_core = self.links.copy(src, self.core_slot, self.core_slot, at.near(1)).start()

    def plane(self):
        at, size, half = self.at, self.size, self.half
        self.by_core.wait_recv()
        start = at.c * 2 * size

        def body(r):
            row = ds(start + r, 16, 16)
            v = self.slot[row, :].astype(F32) + self.core_slot[pl.ds(r, 16), :].astype(F32)
            self.slot[row, :] = v.astype(BF)

        rows_loop(2 * size, 16, body)
        low = self.slot.at[ds(start + (1 - at.y) * size, size, 16), 0:half]
        high = self.slot.at[ds(start + (1 - at.x) * size, size, 16), half : 2 * half]
        self.by_y = self.links.copy(low, self.from_y, self.from_y, at.near(4)).start()
        self.by_x = self.links.copy(high, self.from_x, self.from_x, at.near(2)).start()

    def depth(self):
        at, size, half = self.at, self.size, self.half
        start = at.c * 2 * size
        for copy, mine, other, col in (
            (self.by_y, at.y, self.from_y, slice(0, half)),
            (self.by_x, at.x, self.from_x, slice(half, 2 * half)),
        ):
            copy.wait_recv()

            def body(r):
                v = self.slot[ds(start + mine * size + r, 16, 16), col].astype(F32) + other[pl.ds(r, 16), :].astype(F32)
                self.own[pl.ds(r, 16), col] = v.astype(BF)

            rows_loop(size, 16, body)
        self.along = Along(self.links, at, self.own, self.from_z, self.total).start()

    def hop(self, i):
        self.along.hop(i)

    def finish(self):
        self.along.finish()


ORDER = (
    "mc", "halo", "widen", "s4", "s3", "s1", "ph0", "mp", "s2", "s0", "b0", "ph1", "b1", "w2", "t0", "u0", "t1",
    "u1", "pl0", "t2", "u2", "pl1", "t3", "d0", "u3", "pl2", "t4", "h0", "d1", "u4", "mx", "pf", "pl3", "d2",
    "g0", "b2", "h1", "pl4", "h2", "b3", "md", "f0", "p2", "g1", "b4", "g2", "sums", "mh0", "d3", "f1", "d4",
    "f2", "q0", "p3", "mh1", "e1", "h3", "q1", "h4", "q2", "r0", "r1", "mf", "store", "r2", "g3", "m2", "g4",
    "f3", "m3", "f4", "q3", "q4", "r3", "r4",
)


def backward_kernel(
    sizes,
    features,
    active_one,
    active_x,
    active_y,
    vectors,
    pool_own,
    middle_low,
    full_conv,
    term_mix,
    grad_conv,
    grad_mix,
    grad_pool,
    grad_features,
    sums_out,
    edged,
    edged_x,
    edged_y,
    ext,
    shifted,
    shifted_two,
    weight,
    grad_active,
    slots,
    core_slots,
    from_x,
    from_y,
    own,
    from_z,
    total,
    mix_slot,
    mix_core,
    mix_x,
    mix_y,
    mix_yx,
    mix_xy,
    mix_own,
    mix_z,
    mix_total,
    pool_z,
    pool_total,
    mine,
    seq_slots,
    fsdp_slots,
    send,
    recv,
    seq_send,
    seq_recv,
    fsdp_send,
    fsdp_recv,
    local,
):
    seq, fsdp = sizes
    at = Place(seq, fsdp)
    links = Links(send, recv)
    rows, cin = features.shape
    cout = full_conv.shape[1]
    taps = full_conv.shape[0] // cin
    all_rows = float(rows * seq * fsdp)
    lead = 16
    half_in, half_out = cin // 2, cout // 2
    tap_share = cin // GROUP

    def load_weight(i):
        return pltpu.make_async_copy(full_conv.at[pl.ds(i * half_in, half_in)], weight.at[i % 2], local.at[i % 2])

    top, bottom, inner = pl.ds(0, lead), pl.ds(lead + rows, lead), pl.ds(lead, rows)
    load_middle = pltpu.make_async_copy(middle_low, edged.at[inner], local.at[3])
    load_middle.start()
    load_mix = pltpu.make_async_copy(term_mix, mix_slot, local.at[2])
    load_mix.start()
    load_weight(0).start()
    load_weight(1).start()
    at.barrier()
    below = links.copy(middle_low.at[pl.ds(0, lead)], edged.at[bottom], edged.at[bottom], at.up(fsdp - 1)).start()
    above = links.copy(middle_low.at[pl.ds(rows - lead, lead)], edged.at[top], edged.at[top], at.up(1)).start()
    pairs = ((edged_x, 2, slice(0, half_out)), (edged_y, 4, slice(half_out, cout)))
    exchanged = [
        links.copy(middle_low.at[:, col], target.at[inner], target.at[inner], at.near(mask)).start()
        for target, mask, col in pairs
    ]
    pool = Along(links, at, pool_own, pool_z, pool_total).start()
    groups = []

    def spread(block, target, start, order):
        size = block.shape[0]

        def place(part, half):
            first = start + order(part) * size
            if half is None:
                return target.at[ds(first, size, 16)]
            return target.at[ds(first + half * (size // 2), size // 2, 16)]

        keep = pltpu.make_async_copy(block, place(at.part, None), local.at[4 + len(groups)])
        group = Spread(links, at, place, block)
        groups.append((group, keep))
        group.one()
        keep.start()
        return group

    def tap_order(part):
        c, x, y = part & 1, (part >> 1) & 1, part >> 2
        low = at.z < fsdp // 2
        return jnp.where(low, x, y) * 4 + c * 2 + jnp.where(low, y, x)

    def natural_order(part):
        return part

    mix = Reduce(links, at, mix_slot, (mix_core, mix_x, mix_y, mix_yx, mix_xy, mix_own))
    def halo():
        load_middle.wait()
        below.wait_recv()
        above.wait_recv()
        edged[top, :] = jnp.where(at.z > 0, edged[top, :], jnp.zeros((lead, cout), BF))
        edged[bottom, :] = jnp.where(at.z < fsdp - 1, edged[bottom, :], jnp.zeros((lead, cout), BF))
        exchanged.extend(
            links.copy(edged.at[part, col], target.at[part], target.at[part], at.near(mask)).start()
            for target, mask, col in pairs
            for part in (top, bottom)
        )

    def widen():
        def body(r):
            ext[pl.ds(r, 32), :] = edged[pl.ds(r, 32), :].astype(F32)

        rows_loop(rows + 2 * lead, 32, body)

    def widen_two():
        for copy in exchanged:
            copy.wait_recv()

        def body(r):
            ext[pl.ds(r, 32), 0:half_out] = edged_x[pl.ds(r, 32), :].astype(F32)
            ext[pl.ds(r, 32), half_out:cout] = edged_y[pl.ds(r, 32), :].astype(F32)

        rows_loop(rows + 2 * lead, 32, body)

    half_width = (taps - 1) // 2

    def shift(target, k):
        start = lead + half_width - k

        def body(i, carry):
            col = ds(i * 128, 128, 128)
            target[:, col] = ext[pl.ds(start, rows), col].astype(BF)
            return carry

        lax.fori_loop(0, cout // 128, body, 0)

    def back(k):
        for i in (2 * k, 2 * k + 1):
            load_weight(i).wait()

            for j in range(2):
                at_row = j * (half_in // 2)
                col = slice((i % 2) * half_in + at_row, (i % 2) * half_in + at_row + half_in // 2)
                v = dot(shifted[k], weight[i % 2, at_row : at_row + half_in // 2, :], 1, 1)
                grad_active[:, col] = v if k == 0 else grad_active[:, col] + v
            if i + 2 < 2 * taps:
                load_weight(i + 2).start()

    columns = (ds(at.x * half_in, half_in, 128), ds(at.y * half_in, half_in, 128))
    tile = 256

    def product(k, i):
        other = (active_x, active_y)[i]

        def body(j, carry):
            col = ds(i * half_out + j * tile, tile, 128)
            v = dot(active_one[:, columns[i]], shifted[k, :, col], 0, 0)
            v = v + dot(other[...], shifted_two[:, col], 0, 0)
            slots[k, :, col] = v.astype(BF)
            return carry

        lax.fori_loop(0, half_out // tile, body, 0)

    steps = []
    for k in range(taps):
        mine_rows = pl.ds(k * tap_share, tap_share)
        steps.append(
            Tap(
                links,
                at,
                slots.at[k],
                (
                    core_slots.at[k],
                    from_x.at[mine_rows],
                    from_y.at[mine_rows],
                    own.at[mine_rows],
                    from_z.at[:, mine_rows],
                    total.at[mine_rows],
                ),
            )
        )
    mean_one, scale_one, gain_one, shift_one = (vectors[i : i + 1, :cin] for i in range(4))
    sems = (seq_send, seq_recv, fsdp_send, fsdp_recv)
    stats = Exchange(at, mine, seq_slots, fsdp_slots, sems)

    def normed(r):
        return (features[pl.ds(r, 32), :].astype(F32) - mean_one) * scale_one

    def sums():
        def grad_before(r):
            n = normed(r)
            v = normal(n * gain_one + shift_one)[1] * grad_active[pl.ds(r, 32), :]
            grad_active[pl.ds(r, 32), :] = v
            return v, v * n

        sum_shift, sum_gain = row_sums(rows, 32, cin, 2, grad_before)
        pad = jnp.zeros((1, cout - cin), F32)
        wide = lambda v: jnp.concatenate([v, pad], axis=1)
        stats.start(pack(wide(sum_shift), wide(sum_gain), vectors[6:7, :], vectors[7:8, :]))

    def store():
        everyone = unpack(stats.end(combine_sums))
        shift_grad, gain_grad = everyone[0][:, :cin], everyone[1][:, :cin]

        def body(r):
            v = grad_active[pl.ds(r, 32), :] - shift_grad / all_rows - normed(r) * gain_grad / all_rows
            grad_features[pl.ds(r, 32), :] = (gain_one * scale_one * v).astype(BF)

        rows_loop(rows, 32, body)
        sums_out[0:4, :] = jnp.concatenate(everyone, axis=0)

    spreads = {}

    def mix_core():
        load_mix.wait()
        mix.core()

    mix_along = Along(links, at, mix_own, mix_z, mix_total)

    def mix_depth():
        mix.depth()
        mix_along.start()

    def finish(name, along, target, start, order):
        along().finish()
        spreads[name] = spread(along().total, target, start, order)

    def first(k):
        shift(shifted_two, k)
        product(k, 0)

    def second(k):
        product(k, 1)
        steps[k].core()

    actions = {
        "halo": halo,
        "widen": widen,
        "w2": widen_two,
        "sums": sums,
        "e1": lambda: stats.middle(combine_sums),
        "store": store,
        "mc": mix_core,
        "mp": mix.plane,
        "mx": mix.cross,
        "md": mix_depth,
        "mh0": lambda: mix_along.hop(0),
        "mh1": lambda: mix_along.hop(1),
        "mf": lambda: finish("m", lambda: mix_along, grad_mix, 0, natural_order),
        "m2": lambda: spreads["m"].two(),
        "m3": lambda: spreads["m"].three(),
        "ph0": lambda: pool.hop(0),
        "ph1": lambda: pool.hop(1),
        "pf": lambda: finish("p", lambda: pool, grad_pool, 0, natural_order),
        "p2": lambda: spreads["p"].two(),
        "p3": lambda: spreads["p"].three(),
    }
    of_tap = {
        "s": lambda k: shift(shifted.at[k], k),
        "b": back,
        "t": first,
        "u": second,
        "pl": lambda k: steps[k].plane(),
        "d": lambda k: steps[k].depth(),
        "h": lambda k: steps[k].hop(0),
        "g": lambda k: steps[k].hop(1),
        "f": lambda k: finish(k, lambda: steps[k].along, grad_conv, k * cin, tap_order),
        "q": lambda k: spreads[k].two(),
        "r": lambda k: spreads[k].three(),
    }
    for name, action in of_tap.items():
        for k in range(taps):
            actions[f"{name}{k}"] = functools.partial(action, k)
    for name in ORDER:
        actions.pop(name)()
    assert not actions
    for group, keep in groups:
        group.four()
        keep.wait()
    links.drain()


def run_backward(sizes, features, active_one, active_x, active_y, vectors, pool_own, middle_low, full_conv, term_mix):
    seq, fsdp = sizes
    rows, cin = features.shape
    deep, cout = full_conv.shape
    taps = deep // cin
    width = cout // fsdp
    tap_share = cin // GROUP
    shape = jax.ShapeDtypeStruct
    vmem = pl.BlockSpec(memory_space=pltpu.VMEM)
    hbm = pl.BlockSpec(memory_space=pl.ANY)
    copies = 160
    return pl.pallas_call(
        functools.partial(backward_kernel, sizes),
        out_shape=(
            shape((deep, width), BF),
            shape((cout, width), BF),
            shape((cout, width), BF),
            shape((rows, cin), BF),
            shape((8, cout), F32),
        ),
        in_specs=[vmem, vmem, vmem, vmem, vmem, vmem, hbm, hbm, hbm],
        out_specs=(hbm, hbm, hbm, vmem, vmem),
        scratch_shapes=[
            pltpu.VMEM((rows + 32, cout), BF),
            pltpu.VMEM((rows + 32, cout // 2), BF),
            pltpu.VMEM((rows + 32, cout // 2), BF),
            pltpu.VMEM((rows + 32, cout), F32),
            pltpu.VMEM((taps, rows, cout), BF),
            pltpu.VMEM((rows, cout), BF),
            pltpu.VMEM((2, cin // 2, cout), BF),
            pltpu.VMEM((rows, cin), F32),
            pltpu.VMEM((taps, cin // 2, cout), BF),
            pltpu.VMEM((taps, cin // 4, cout), BF),
            pltpu.VMEM((taps * tap_share, cout // 2), BF),
            pltpu.VMEM((taps * tap_share, cout // 2), BF),
            pltpu.VMEM((taps * tap_share, cout), BF),
            pltpu.VMEM((fsdp - 1, taps * tap_share, width), BF),
            pltpu.VMEM((taps * tap_share, width), BF),
            pltpu.VMEM((cout, cout), BF),
            *Reduce.scratch(cout, cout),
            pltpu.VMEM((cout // GROUP, cout), BF),
            pltpu.VMEM((fsdp - 1, cout // GROUP, width), BF),
            pltpu.VMEM((cout // GROUP, width), BF),
            pltpu.VMEM((fsdp - 1, cout // GROUP, width), BF),
            pltpu.VMEM((cout // GROUP, width), BF),
            pltpu.VMEM((2, 16, cout // 4), F32),
            pltpu.VMEM((seq, 16, cout // 4), F32),
            pltpu.VMEM((fsdp, 16, cout // 4), F32),
            pltpu.SemaphoreType.DMA((copies,)),
            pltpu.SemaphoreType.DMA((copies,)),
            pltpu.SemaphoreType.DMA((seq,)),
            pltpu.SemaphoreType.DMA((seq,)),
            pltpu.SemaphoreType.DMA((fsdp,)),
            pltpu.SemaphoreType.DMA((fsdp,)),
            pltpu.SemaphoreType.DMA((6 + taps,)),
        ],
        compiler_params=pltpu.CompilerParams(
            collective_id=1, has_side_effects=True, vmem_limit_bytes=62 * 2**20
        ),
    )(features, active_one, active_x, active_y, vectors, pool_own, middle_low, full_conv, term_mix)


def spread_sum(v):
    size = lax.axis_size("seq")
    bit = GROUP
    while bit < size:
        v = v + lax.ppermute(v, "seq", [(i, i ^ bit) for i in range(size)])
        bit *= 2
    return v


def on_device(
    features,
    conv_weight,
    mix_weight,
    pool_weight,
    gain_first,
    shift_first,
    gain_second,
    shift_second,
    bias_conv,
    bias_mix,
    cotangent,
    track_counts,
):
    rows, cin = features.shape
    seq, fsdp = lax.axis_size("seq"), lax.axis_size("fsdp")
    position = lax.axis_index(("seq", "fsdp"))
    owner = lax.axis_index("fsdp")
    window = position * rows // WIN
    width = conv_weight.shape[2]
    cout = width * fsdp
    taps = conv_weight.shape[0]
    scale = lax.dynamic_slice_in_dim(track_counts, window, 1).astype(F32) / TRACKS
    scale = jnp.broadcast_to(scale[:, None], (1, cout))
    rest = ((0, width - gain_first.shape[0]),)
    own_vectors = [jnp.pad(gain_first, rest), jnp.pad(shift_first, rest), gain_second, shift_second, bias_conv, bias_mix]
    own_vectors = jnp.stack(own_vectors + [jnp.zeros_like(bias_mix)] * 2).astype(F32)
    full_conv, _, _, term_mix, active_x, active_y, pool_own, pooled, active_one, middle_low, vectors = run_forward(
        (seq, fsdp),
        features,
        conv_weight.reshape(taps * cin, width),
        mix_weight,
        pool_weight,
        own_vectors,
        cotangent,
        scale,
    )
    grad_conv, grad_mix, grad_pool, grad_features, sums = run_backward(
        (seq, fsdp), features, active_one, active_x, active_y, vectors, pool_own, middle_low, full_conv, term_mix
    )
    grad_conv, grad_mix, grad_pool = (spread_sum(v.astype(F32)) for v in (grad_conv, grad_mix, grad_pool))
    grad_conv = grad_conv.reshape(taps, cin, width)
    shift_two_grad, gain_two_grad = vectors[4], vectors[5]
    shift_one_grad, gain_one_grad, bias_one_grad, bias_two_grad = sums[0], sums[1], sums[2], sums[3]

    def share(v, size):
        return lax.dynamic_slice_in_dim(v, owner * size, size)

    first, second = gain_first.shape[0], gain_second.shape[0]
    return (
        pooled,
        grad_features,
        grad_conv,
        grad_mix,
        grad_pool,
        share(gain_one_grad, first),
        share(shift_one_grad, first),
        share(gain_two_grad, second),
        share(shift_two_grad, second),
        share(bias_one_grad, second),
        share(bias_two_grad, second),
    )


def solution(mesh):
    rows = P(("seq", "fsdp"), None)
    vector = P("fsdp")
    in_specs = (rows, P(None, None, "fsdp"), P(None, "fsdp"), P(None, "fsdp")) + (vector,) * 6 + (rows, P())
    out_specs = (rows, rows, P(None, None, "fsdp"), P(None, "fsdp"), P(None, "fsdp")) + (vector,) * 6
    return jax.shard_map(on_device, mesh=mesh, in_specs=in_specs, out_specs=out_specs, check_vma=False)
```

```python
import functools
import math
import jax
import jax.numpy as jnp
from jax import lax
from jax.experimental import pallas as pl
from jax.experimental.pallas import tpu as pltpu
from jax.sharding import PartitionSpec as P

TRACKS = 5313
WIN = 2048
EPSILON = 1e-05
MESH = pl.DeviceIdType.MESH
BF = jnp.bfloat16
F32 = jnp.float32
GROUP = 8


def dot(a, b, ca, cb):
    return lax.dot_general(a, b, (((ca,), (cb,)), ((), ())), preferred_element_type=F32)


def ds(start, size, step):
    return pl.ds(pl.multiple_of(start, step), size)


def fold(v):
    rows, width = v.shape
    return jnp.sum(v.reshape(rows // 8, 8, width), axis=0)


def rows_loop(total, step, body):
    def run(i, carry):
        body(pl.multiple_of(i * step, step))
        return carry

    lax.fori_loop(0, total // step, run, 0)


def row_sums(total, step, width, count, body):
    def run(i, carry):
        parts = body(pl.multiple_of(i * step, step))
        return tuple(c + fold(v) for c, v in zip(carry, parts))

    zero = tuple(jnp.zeros((8, width), F32) for _ in range(count))
    sums = lax.fori_loop(0, total // step, run, zero)
    return [jnp.sum(v, axis=0, keepdims=True) for v in sums]


def normal(b):
    cdf = 0.5 * (1.0 + lax.erf(b * math.sqrt(0.5)))
    pdf = jnp.exp(-0.5 * b * b) * (1.0 / math.sqrt(2.0 * math.pi))
    return cdf, cdf + b * pdf


class Copy:
    def __init__(self, links, src, there, here, device):
        i = links.count
        links.count += 1
        send, recv = links.send.at[i], links.recv.at[i]

        def make(dst):
            return pltpu.make_async_remote_copy(
                src_ref=src,
                dst_ref=dst,
                send_sem=send,
                recv_sem=recv,
                device_id=device,
                device_id_type=MESH,
            )

        self.links = links
        self.out, self.into = functools.partial(make, there), functools.partial(make, here)

    def start(self):
        self.out().start()
        self.links.started.append(self)
        return self

    def wait_recv(self):
        self.into().wait_recv()

    def wait_send(self):
        self.out().wait_send()


class Links:
    def __init__(self, send, recv):
        self.send, self.recv = send, recv
        self.count = 0
        self.started = []

    def copy(self, src, there, here, device):
        return Copy(self, src, there, here, device)

    def drain(self):
        for item in self.started:
            item.wait_send()
        self.started = []


class Place:
    def __init__(self, seq, fsdp):
        self.seq_size, self.fsdp_size = seq, fsdp
        self.s, self.z = lax.axis_index("seq"), lax.axis_index("fsdp")
        self.part = lax.rem(self.s, GROUP)
        self.base = self.s - self.part
        self.c, self.x, self.y = self.part & 1, (self.part >> 1) & 1, self.part >> 2

    def near(self, mask):
        return (self.base + jnp.bitwise_xor(self.part, mask), self.z)

    def up(self, d):
        return (self.s, lax.rem(self.z + d, self.fsdp_size))

    def barrier(self):
        bar = pltpu.get_barrier_semaphore()

        def greet(i, carry):
            peer = lax.rem(self.s + i, self.seq_size)
            pl.semaphore_signal(bar, inc=1, device_id=(peer, self.z), device_id_type=MESH)
            return carry

        lax.fori_loop(1, self.seq_size, greet, 0)
        for d in range(1, self.fsdp_size):
            pl.semaphore_signal(bar, inc=1, device_id=self.up(d), device_id_type=MESH)
        pl.semaphore_wait(bar, self.seq_size + self.fsdp_size - 2)


class Exchange:
    def __init__(self, place, mine, seq_slots, fsdp_slots, sems):
        self.place, self.mine = place, mine
        self.seq_slots, self.fsdp_slots = seq_slots, fsdp_slots
        self.seq_send, self.seq_recv, self.fsdp_send, self.fsdp_recv = sems

    def _copy(self, i, stage):
        at = self.place
        if stage == 0:
            peer = lax.rem(at.s + i, at.seq_size)
            source = lax.rem(at.s - i + at.seq_size, at.seq_size)
            device, slots, send, recv, me = (peer, at.z), self.seq_slots, self.seq_send, self.seq_recv, at.s
        else:
            peer = lax.rem(at.z + i, at.fsdp_size)
            source = lax.rem(at.z - i + at.fsdp_size, at.fsdp_size)
            device, slots, send, recv, me = (at.s, peer), self.fsdp_slots, self.fsdp_send, self.fsdp_recv, at.z
        make = lambda slot: pltpu.make_async_remote_copy(
            src_ref=self.mine.at[stage],
            dst_ref=slots.at[slot],
            send_sem=send.at[i],
            recv_sem=recv.at[i],
            device_id=device,
            device_id_type=MESH,
        )
        return functools.partial(make, me), functools.partial(make, source)

    def _each(self, stage, what):
        size = self.place.seq_size if stage == 0 else self.place.fsdp_size

        def run(i, carry):
            what(*self._copy(i, stage))
            return carry

        lax.fori_loop(1, size, run, 0)

    def start(self, block):
        self.mine[0] = block
        self.seq_slots[self.place.s] = block
        self._each(0, lambda out, into: out().start())

    def middle(self, combine):
        self._each(0, lambda out, into: into().wait_recv())
        block = combine(self.seq_slots)
        self.mine[1] = block
        self.fsdp_slots[self.place.z] = block
        self._each(1, lambda out, into: out().start())

    def end(self, combine):
        self._each(1, lambda out, into: into().wait_recv())
        block = combine(self.fsdp_slots)
        self._each(0, lambda out, into: out().wait_send())
        self._each(1, lambda out, into: out().wait_send())
        return block

    def finish(self, combine):
        self.middle(combine)
        return self.end(combine)


def pack(*vectors):
    width = vectors[0].shape[1] // 4
    pieces = [v[:, i * width : (i + 1) * width] for v in vectors for i in range(4)]
    return jnp.concatenate(pieces, axis=0)


def unpack(block):
    count = block.shape[0] // 4
    return [jnp.concatenate([block[4 * j + i : 4 * j + i + 1] for i in range(4)], axis=1) for j in range(count)]


def combine_sums(slots):
    return jnp.sum(slots[...], axis=0)


def combine_moments(slots):
    v = slots[...]
    center, spread = v[:, :4], v[:, 4:]
    mean = jnp.mean(center, axis=0)
    rest = jnp.mean(spread + jnp.square(center - mean[None]), axis=0)
    return jnp.concatenate([mean, rest], axis=0)


class Spread:
    def __init__(self, links, at, place, source=None):
        self.links, self.at, self.place, self.source = links, at, place, source
        self.held = {}

    def _send(self, name, mask, of, half=None):
        part = self.at.part
        mine = self.place(jnp.bitwise_xor(part, of), half)
        theirs = self.place(jnp.bitwise_xor(part, of ^ mask), half)
        src = mine if of or self.source is None else self.source
        self.held[name] = self.links.copy(src, mine, theirs, self.at.near(mask)).start()

    def one(self):
        self._send("x", 2, 0)
        self._send("y", 4, 0)
        self._send("c", 1, 0)

    def two(self):
        self.held["x"].wait_recv()
        self._send("xa", 4, 2, 0)
        self._send("xc", 1, 2)
        self.held["y"].wait_recv()
        self._send("yb", 2, 4, 1)
        self._send("yc", 1, 4)

    def three(self):
        self.held["xa"].wait_recv()
        self._send("ac", 1, 6, 0)
        self.held["yb"].wait_recv()
        self._send("bc", 1, 6, 1)

    def four(self):
        for name in ("c", "xc", "yc", "ac", "bc"):
            self.held[name].wait_recv()


class Gather:
    def __init__(self, links, at, shard, full, d, lo, size):
        self.links, self.at, self.shard, self.full, self.d = links, at, shard, full, d
        self.lo, self.size = lo, size
        self.share, self.width = shard.shape[0] // GROUP, shard.shape[1]
        self.z = lax.rem(at.z - d + at.fsdp_size, at.fsdp_size)
        spread = Spread(links, at, lambda part, half: self.full.at[self._rows(part, half), self._columns(self.z)])
        self.spread, self.two, self.three, self.four = spread, spread.two, spread.three, spread.four

    def _rows(self, part, half=None):
        start = part * self.share + self.lo
        if half is None:
            return ds(start, self.size, 16)
        return ds(start + half * (self.size // 2), self.size // 2, 16)

    def _columns(self, z):
        return ds(z * self.width, self.width, 128)

    def send(self):
        at = self.at
        rows = self._rows(at.part)
        passed = self._columns(lax.rem(self.z + 1, at.fsdp_size))
        there = self.full.at[rows, passed]
        here = self.full.at[rows, self._columns(self.z)]
        src = self.shard.at[rows] if self.d == 1 else there
        self.along = self.links.copy(src, there, here, at.up(1)).start()

    def arrive(self):
        self.along.wait_recv()

    def one(self):
        self.arrive()
        self.spread.one()


def put_blocks(target, half, values, col):
    size = values.shape[0] // 8
    for i in range(8):
        part, side = 4 * half + i // 2, i % 2
        c, x, y = part & 1, part >> 1 & 1, part >> 2
        at = 8 * c + 4 * side + (2 * x + y if side == 0 else 2 * y + x)
        target[at * size : (at + 1) * size, col] = values[i * size : (i + 1) * size].astype(BF)


def forward_kernel(
    sizes,
    features,
    conv_shard,
    mix_shard,
    pool_shard,
    vectors_in,
    cotangent,
    track_counts,
    full_conv,
    full_mix,
    full_pool,
    term_mix,
    active_x,
    active_y,
    pool_own,
    pooled,
    active_out,
    middle_low,
    vectors,
    ext,
    taps,
    wbuf,
    mixw,
    middle,
    deriv,
    work,
    a2,
    low,
    low2,
    gbuf,
    pair_one,
    pair_two,
    pool_core,
    pool_x,
    pool_y,
    pool_yx,
    pool_xy,
    mine,
    seq_slots,
    fsdp_slots,
    packs,
    edges,
    moment,
    send,
    recv,
    seq_send,
    seq_recv,
    fsdp_send,
    fsdp_recv,
    local,
):
    seq, fsdp = sizes
    at = Place(seq, fsdp)
    links = Links(send, recv)
    rows, cin = features.shape
    cout = full_conv.shape[1]
    width = cout // fsdp
    total = float(rows * seq * fsdp)
    taps_count = conv_shard.shape[0] // cin
    lead = 8

    def exchange(i):
        sems = (seq_send.at[i], seq_recv.at[i], fsdp_send.at[i], fsdp_recv.at[i])
        return Exchange(at, mine.at[i], seq_slots.at[i], fsdp_slots.at[i], sems)

    own_conv = pltpu.make_async_copy(wbuf.at[0], full_conv.at[:, ds(at.z * width, width, 128)], local.at[0])
    mixing, pooling = pl.ds(0, cout), pl.ds(cout, cout)
    own_mix = pltpu.make_async_copy(mix_shard, mixw.at[mixing, ds(at.z * width, width, 128)], local.at[1])
    own_pool = pltpu.make_async_copy(pool_shard, mixw.at[pooling, ds(at.z * width, width, 128)], local.at[4])
    own_load = pltpu.make_async_copy(conv_shard, wbuf.at[0], local.at[2])

    at.barrier()
    near = range(1, fsdp)
    share = conv_shard.shape[0] // GROUP
    cut = share * 3 // 5 // 32 * 32
    conv = [Gather(links, at, conv_shard, full_conv, d, *piece) for d in near for piece in ((0, cut), (cut, share - cut))]
    mix, poolw = (
        [Gather(links, at, shard, full, d, 0, cout // GROUP) for d in near]
        for shard, full in ((mix_shard, full_mix), (pool_shard, full_pool))
    )
    parcels = []
    for d in near:
        source = lax.rem(at.z - d + fsdp, fsdp)
        parcels.append(links.copy(vectors_in, packs.at[at.z], packs.at[source], at.up(d)).start())
    parcels.append(links.copy(features.at[pl.ds(0, 16)], edges.at[1], edges.at[1], at.up(fsdp - 1)).start())
    parcels.append(links.copy(features.at[pl.ds(rows - 16, 16)], edges.at[0], edges.at[0], at.up(1)).start())
    conv[0].send()
    own_load.start()
    own_mix.start()
    own_pool.start()

    (sum_one,) = row_sums(rows, 64, cin, 1, lambda r: (features[pl.ds(r, 64), :].astype(F32),))
    mean = sum_one / rows
    (dev_one,) = row_sums(rows, 64, cin, 1, lambda r: (jnp.square(features[pl.ds(r, 64), :].astype(F32) - mean),))
    pad = jnp.zeros((1, cout - cin), F32)
    stats = exchange(0)
    stats.start(pack(jnp.concatenate([mean, pad], axis=1), jnp.concatenate([dev_one / rows, pad], axis=1)))
    packs[at.z] = vectors_in[...]
    stats.middle(combine_moments)
    conv[0].one()
    for parcel in parcels:
        parcel.wait_recv()
    share_in = cin // fsdp

    def vector(first, size):
        pieces = []
        for z in range(fsdp):
            for row in range(first // 128, -(-(first + size) // 128)):
                lo, hi = max(first - row * 128, 0), min(first + size - row * 128, 128)
                pieces.append(packs[z, row : row + 1, lo:hi])
        return jnp.concatenate(pieces, axis=1)

    gain_one, shift_one = vector(0, share_in), vector(share_in, share_in)
    gain_two, shift_two, bias_one, bias_two = (vector(2 * share_in + i * width, width) for i in range(4))
    moment[2:3, :] = bias_one
    mean_one, var_one = unpack(stats.end(combine_moments))
    conv[1].send()
    conv[2].send()
    mean_one, scale_one = mean_one[:, :cin], lax.rsqrt(var_one[:, :cin] + EPSILON)

    def active(v):
        b = (v - mean_one) * scale_one * gain_one + shift_one
        return b * (0.5 * (1.0 + lax.erf(b * math.sqrt(0.5))))

    def first_active(r):
        v = active(features[pl.ds(r, 32), :].astype(F32)).astype(BF)
        active_out[pl.ds(r, 32), :] = v
        ext[pl.ds(lead + r, 32), :cin] = v.astype(F32)

    rows_loop(rows, 32, first_active)
    conv[1].one()
    conv[3].send()
    conv[0].two()
    row = lax.broadcasted_iota(jnp.int32, (8, cin), 0)
    before, after = edges[0].astype(F32)[8:16], edges[1].astype(F32)[0:8]
    ext[0:lead, :cin] = jnp.where((row >= 6) & (at.z > 0), active(before), 0.0)
    ext[lead + rows : lead + rows + 8, :cin] = jnp.where((row < 2) & (at.z < fsdp - 1), active(after), 0.0)
    def shifted(k):
        def body(i, carry):
            col = ds(i * 128, 128, 128)
            taps[:, ds(k * cin + i * 128, 128, 128)] = ext[pl.ds(lead - 2 + k, rows), col].astype(BF)
            return carry

        lax.fori_loop(0, cin // 128, body, 0)

    for k in range(taps_count):
        shifted(k)
    conv[2].one()
    conv[4].send()
    conv[1].two()
    conv[0].three()

    def load_block(slot, z):
        copy = pltpu.make_async_copy(full_conv.at[:, ds(z * width, width, 128)], wbuf.at[slot], local.at[3])
        copy.start()
        return copy

    def multiply(slot, z, half):
        row = pl.ds(half * (rows // 2), rows // 2)
        middle[row, ds(z * width, width, 128)] = dot(taps[row, :], wbuf[slot], 1, 0)

    def moments(z):
        col = ds(z * width, width, 128)
        bias = moment[2:3, col]

        def plus_bias(r):
            v = middle[pl.ds(r, 64), col] + bias
            middle[pl.ds(r, 64), col] = v
            return (v,)

        (total_two,) = row_sums(rows, 64, width, 1, plus_bias)
        mean = total_two / rows
        (dev_two,) = row_sums(rows, 64, width, 1, lambda r: (jnp.square(middle[pl.ds(r, 64), col] - mean),))
        moment[0:1, col] = mean
        moment[1:2, col] = dev_two / rows

    def load_later(part, i, target):
        col = ds(part[i].z * width, width, 128)
        copy = pltpu.make_async_copy(part[i].full.at[:, col], mixw.at[target, col], local.at[5 + i])
        copy.start()
        return copy

    own_load.wait()
    own_conv.start()
    multiply(0, at.z, 0)
    conv[3].one()
    conv[5].send()
    conv[2].two()
    conv[1].three()
    conv[0].four()
    multiply(0, at.z, 1)
    own_conv.wait()
    moments(at.z)
    conv[4].one()
    mix[0].send()
    conv[3].two()
    conv[2].three()
    conv[1].four()
    block = load_block(1, conv[0].z)
    conv[5].one()
    poolw[0].send()
    conv[4].two()
    conv[3].three()
    conv[2].four()
    block.wait()
    multiply(1, conv[0].z, 0)
    mix[0].one()
    mix[1].send()
    conv[5].two()
    conv[4].three()
    conv[3].four()
    block = load_block(0, conv[2].z)
    multiply(1, conv[0].z, 1)
    moments(conv[0].z)
    mix[1].one()
    mix[2].send()
    block.wait()
    multiply(0, conv[2].z, 0)
    conv[5].three()
    conv[4].four()
    multiply(0, conv[2].z, 1)
    moments(conv[2].z)
    mix[0].two()
    mix[2].one()
    poolw[0].arrive()
    poolw[1].send()
    conv[5].four()
    block = load_block(1, conv[4].z)
    mix[1].two()
    mix[0].three()
    poolw[0].spread.one()
    block.wait()
    multiply(1, conv[4].z, 0)
    mix[1].three()
    mix[2].two()
    poolw[1].arrive()
    poolw[2].send()
    multiply(1, conv[4].z, 1)
    moments(conv[4].z)
    poolw[0].two()
    mix[2].three()

    stats = exchange(1)
    stats.start(pack(moment[0:1, :], moment[1:2, :]))
    for part in mix:
        part.four()
    loads = [load_later(mix, i, mixing) for i in range(fsdp - 1)]
    stats.middle(combine_moments)
    poolw[1].spread.one()
    poolw[2].one()
    mean_two, var_two = unpack(stats.end(combine_moments))
    scale_two = lax.rsqrt(var_two + EPSILON)

    def second_active(r):
        b = (middle[pl.ds(r, 32), :] - mean_two) * scale_two * gain_two + shift_two
        cdf, slope = normal(b)
        a2[pl.ds(r, 32), :] = (b * cdf).astype(BF)
        deriv[pl.ds(r, 32), :] = slope

    rows_loop(rows // 2, 32, second_active)
    poolw[0].three()
    poolw[1].two()
    rows_loop(rows // 2, 32, lambda r: second_active(rows // 2 + r))
    poolw[2].two()
    half = cin // 2
    actives = [
        links.copy(active_out.at[:, ds((1 - at.x) * half, half, 128)], active_x, active_x, at.near(2)).start(),
        links.copy(active_out.at[:, ds((1 - at.y) * half, half, 128)], active_y, active_y, at.near(4)).start(),
    ]
    poolw[1].three()
    own_mix.wait()
    for load in loads:
        load.wait()

    tile = 512
    tiles = cout // tile

    def block_columns(z):
        return ds(z * width, width, 128)

    def column_loop(body):
        def run(i, carry):
            body(ds(i * tile, tile, 128))
            return carry

        lax.fori_loop(0, tiles, run, 0)

    def add_mix(col):
        work[:, col] = dot(a2[...], mixw[0:cout, col], 1, 0)

    column_loop(add_mix)
    poolw[2].three()

    def add_residual(r):
        v = middle[pl.ds(r, 32), :] + work[pl.ds(r, 32), :] + bias_two
        ext[pl.ds(r, 32), :] = v
        low[pl.ds(r, 32), :] = v.astype(BF)

    rows_loop(rows, 32, add_residual)

    def add_pool(col):
        work[:, col] = dot(low[...], mixw[cout : 2 * cout, col], 1, 0)

    own_pool.wait()
    add_pool(block_columns(at.z))
    ready = None
    for i in range(fsdp - 1):
        poolw[i].four()
        load = load_later(poolw, i, pooling)
        if ready is not None:
            ready.wait()
            add_pool(block_columns(poolw[i - 1].z))
        ready = load
    ready.wait()
    add_pool(block_columns(poolw[fsdp - 2].z))

    scale = track_counts[(at.s * fsdp + at.z) * rows // WIN].astype(F32) / TRACKS

    def pairs(i, carry):
        col = ds(i * 128, 128, 128)
        even, odd = pl.ds(0, rows // 2, 2), pl.ds(1, rows // 2, 2)
        one, two = pair_one, pair_two
        one[...], two[...] = work[:, col], ext[0:rows, col]
        l0, l1 = one[even, :], one[odd, :]
        s0, s1 = two[even, :], two[odd, :]
        top = jnp.maximum(l0, l1)
        e0, e1 = jnp.exp(l0 - top), jnp.exp(l1 - top)
        inverse = 1.0 / (e0 + e1)
        w0, w1 = e0 * inverse, e1 * inverse
        up = cotangent[:, col].astype(F32) * scale
        pooled[:, col] = (w0 * s0 + w1 * s1).astype(BF)
        g0, g1 = s0 * up, s1 * up
        both = w0 * g0 + w1 * g1
        one[even, :] = w0 * up
        one[odd, :] = w1 * up
        two[even, :] = w0 * (g0 - both)
        two[odd, :] = w1 * (g1 - both)
        work[:, col] = one[...]
        low2[:, col] = two[...].astype(BF)
        return carry

    lax.fori_loop(0, cout // 128, pairs, 0)

    def product(left, right, gbuf):
        half = cout // 2
        for i in range(2):
            def body(j, carry):
                col = ds(j * tile, tile, 128)
                put_blocks(gbuf, i, dot(left[:, i * half : (i + 1) * half], right[:, col], 0, 0), col)
                return carry

            lax.fori_loop(0, tiles, body, 0)

    product(low, low2, gbuf)
    pool_buffers = (pool_core, pool_x, pool_y, pool_yx, pool_xy, pool_own)
    pool = Reduce(links, at, gbuf, pool_buffers)
    pool.core()

    def back_pool(col):
        ext[0:rows, col] = dot(low2[...], mixw[ds(cout + col.start, tile, 128), :], 1, 1)

    column_loop(back_pool)

    def grad_summed(r):
        v = work[pl.ds(r, 32), :] + ext[pl.ds(r, 32), :]
        work[pl.ds(r, 32), :] = v
        low[pl.ds(r, 32), :] = v.astype(BF)
        return (v,)

    pool.plane()
    (sum_bias_two,) = row_sums(rows, 32, cout, 1, grad_summed)

    def back_mix(col):
        ext[0:rows, col] = dot(low[...], mixw[ds(col.start, tile, 128), :], 1, 1)

    column_loop(back_mix)

    def normed(r):
        return (middle[pl.ds(r, 32), :] - mean_two) * scale_two

    def grad_before(r):
        v = ext[pl.ds(r, 32), :] * deriv[pl.ds(r, 32), :]
        ext[pl.ds(r, 32), :] = v
        return v, v * normed(r)

    sum_shift, sum_gain = row_sums(rows, 32, cout, 2, grad_before)
    stats = exchange(2)
    stats.start(pack(sum_shift, sum_gain))
    product(a2, low, mixw.at[pooling])
    out_mix = pltpu.make_async_copy(mixw.at[pooling], term_mix, local.at[4])
    out_mix.start()
    stats.middle(combine_sums)
    pool.cross()
    shift_two_grad, gain_two_grad = unpack(stats.end(combine_sums))

    def grad_middle(r):
        v = work[pl.ds(r, 32), :] + gain_two * scale_two * (
            ext[pl.ds(r, 32), :] - shift_two_grad / total - normed(r) * gain_two_grad / total
        )
        middle_low[pl.ds(r, 32), :] = v.astype(BF)
        return (v,)

    (sum_bias_one,) = row_sums(rows, 32, cout, 1, grad_middle)
    fill = lambda v: jnp.concatenate([v, pad], axis=1)
    vectors[0:8, :] = jnp.concatenate(
        [fill(mean_one), fill(scale_one), fill(gain_one), fill(shift_one), shift_two_grad, gain_two_grad, sum_bias_one, sum_bias_two],
        axis=0,
    )
    pool.depth()
    for copy in actives:
        copy.wait_recv()
    out_mix.wait()
    links.drain()


def run_forward(sizes, features, conv_shard, mix_shard, pool_shard, vectors_in, cotangent, track_counts):
    seq, fsdp = sizes
    rows, cin = features.shape
    cout = conv_shard.shape[1] * fsdp
    deep = conv_shard.shape[0]
    two = 2 * cout
    shape = jax.ShapeDtypeStruct
    vmem = pl.BlockSpec(memory_space=pltpu.VMEM)
    hbm = pl.BlockSpec(memory_space=pl.ANY)
    copies = 140
    half = (rows, cin // 2)
    pool = Reduce.scratch(cout, cout)
    return pl.pallas_call(
        functools.partial(forward_kernel, sizes),
        out_shape=(
            shape((deep, cout), BF),
            shape((cout, cout), BF),
            shape((cout, cout), BF),
            shape((cout, cout), BF),
            shape(half, BF),
            shape(half, BF),
            shape((cout // GROUP, cout), BF),
            shape((rows // 2, cout), BF),
            shape((rows, cin), BF),
            shape((rows, cout), BF),
            shape((8, cout), F32),
        ),
        in_specs=[vmem, hbm, hbm, hbm, vmem, vmem, pl.BlockSpec(memory_space=pltpu.SMEM)],
        out_specs=(hbm, hbm, hbm, hbm, hbm, hbm, vmem, vmem, vmem, vmem, vmem),
        scratch_shapes=[
            pltpu.VMEM((rows + 16, cout), F32),
            pltpu.VMEM((rows, deep), BF),
            pltpu.VMEM((2, deep, cout // fsdp), BF),
            pltpu.VMEM((two, cout), BF),
            pltpu.VMEM((rows, cout), F32),
            pltpu.VMEM((rows, cout), F32),
            pltpu.VMEM((rows, cout), F32),
            pltpu.VMEM((rows, cout), BF),
            pltpu.VMEM((rows, cout), BF),
            pltpu.VMEM((rows, cout), BF),
            pltpu.VMEM((cout, cout), BF),
            pltpu.VMEM((rows, 128), F32),
            pltpu.VMEM((rows, 128), F32),
            *pool,
            pltpu.VMEM((3, 2, 8, cout // 4), F32),
            pltpu.VMEM((3, seq, 8, cout // 4), F32),
            pltpu.VMEM((3, fsdp, 8, cout // 4), F32),
            pltpu.VMEM((fsdp,) + vectors_in.shape, F32),
            pltpu.VMEM((2, 16, cin), BF),
            pltpu.VMEM((8, cout), F32),
            pltpu.SemaphoreType.DMA((copies,)),
            pltpu.SemaphoreType.DMA((copies,)),
            pltpu.SemaphoreType.DMA((3, seq)),
            pltpu.SemaphoreType.DMA((3, seq)),
            pltpu.SemaphoreType.DMA((3, fsdp)),
            pltpu.SemaphoreType.DMA((3, fsdp)),
            pltpu.SemaphoreType.DMA((4 + fsdp,)),
        ],
        compiler_params=pltpu.CompilerParams(
            collective_id=0, has_side_effects=True, vmem_limit_bytes=62 * 2**20
        ),
    )(features, conv_shard, mix_shard, pool_shard, vectors_in, cotangent, track_counts)


class Reduce:
    def __init__(self, links, at, slot, buffers):
        self.links, self.at, self.slot = links, at, slot
        self.unit = slot.shape[0] // 16
        self.core_slot, self.from_x, self.from_y, self.from_yx, self.from_xy, self.own = buffers

    @staticmethod
    def scratch(height, width):
        unit = height // 16
        return [pltpu.VMEM((r, width), BF) for r in (8 * unit, 2 * unit, 2 * unit, unit, unit)]

    def _rows(self, start, count):
        return self.slot.at[ds(start * self.unit, count * self.unit, 16)]

    def _send(self, src, dst, device):
        return self.links.copy(src, dst, dst, device).start()

    def core(self):
        self.by_core = self._send(self._rows((1 - self.at.c) * 8, 8), self.core_slot, self.at.near(1))

    def _add(self, start, other, count, out=None):
        step = 16
        mine = self._rows(start, count)
        out = mine if out is None else out

        def body(r):
            v = mine[pl.ds(r, step), :].astype(F32) + other[pl.ds(r, step), :].astype(F32)
            out[pl.ds(r, step), :] = v.astype(BF)

        rows_loop(count * self.unit, step, body)

    def plane(self):
        at = self.at
        self.by_core.wait_recv()
        self._add(at.c * 8, self.core_slot, 8)
        self.a, self.b = at.c * 8, at.c * 8 + 4
        self.by_x = self._send(self._rows(self.a + (1 - at.x) * 2, 2), self.from_x, at.near(2))
        self.by_y = self._send(self._rows(self.b + (1 - at.y) * 2, 2), self.from_y, at.near(4))

    def cross(self):
        x, y = self.at.x, self.at.y
        a, b = self.a + x * 2, self.b + y * 2
        self.by_x.wait_recv()
        self._add(a, self.from_x, 2)
        self.by_yx = self._send(self._rows(a + 1 - y, 1), self.from_yx, self.at.near(4))
        self.by_y.wait_recv()
        self._add(b, self.from_y, 2)
        self.by_xy = self._send(self._rows(b + 1 - x, 1), self.from_xy, self.at.near(2))
        self.a, self.b = a + y, b + x

    def depth(self):
        self.by_yx.wait_recv()
        self._add(self.a, self.from_yx, 1, self.own.at[pl.ds(0, self.unit)])
        self.by_xy.wait_recv()
        self._add(self.b, self.from_xy, 1, self.own.at[pl.ds(self.unit, self.unit)])


class Along:
    def __init__(self, links, at, own, from_z, total):
        self.links, self.at, self.own, self.from_z, self.total = links, at, own, from_z, total
        self.width = total.shape[1]
        self.last = at.fsdp_size - 2

    def _column(self, back):
        at = self.at
        return ds(lax.rem(at.z - back + at.fsdp_size, at.fsdp_size) * self.width, self.width, 128)

    def _send(self, src, i):
        dst = self.from_z.at[i]
        self.copy = self.links.copy(src, dst, dst, self.at.up(1)).start()

    def _add(self, i, back, out):
        self.copy.wait_recv()
        col = self._column(back)

        def body(r):
            v = self.own[pl.ds(r, 16), col].astype(F32) + self.from_z[i, pl.ds(r, 16), :].astype(F32)
            out[pl.ds(r, 16), :] = v.astype(BF)

        rows_loop(self.own.shape[0], 16, body)

    def start(self):
        self._send(self.own.at[:, self._column(1)], 0)
        return self

    def hop(self, i):
        self._add(i, i + 2, self.from_z.at[i])
        self._send(self.from_z.at[i], i + 1)

    def finish(self):
        self._add(self.last, 0, self.total)


class Tap:
    def __init__(self, links, at, slot, buffers):
        self.links, self.at, self.slot = links, at, slot
        self.core_slot, self.from_x, self.from_y, self.own, self.from_z, self.total = buffers
        self.size = slot.shape[0] // 4
        self.half = slot.shape[1] // 2

    def core(self):
        at = self.at
        src = self.slot.at[ds((1 - at.c) * 2 * self.size, 2 * self.size, 16)]
        self.by_core = self.links.copy(src, self.core_slot, self.core_slot, at.near(1)).start()

    def plane(self):
        at, size, half = self.at, self.size, self.half
        self.by_core.wait_recv()
        start = at.c * 2 * size

        def body(r):
            row = ds(start + r, 16, 16)
            v = self.slot[row, :].astype(F32) + self.core_slot[pl.ds(r, 16), :].astype(F32)
            self.slot[row, :] = v.astype(BF)

        rows_loop(2 * size, 16, body)
        low = self.slot.at[ds(start + (1 - at.y) * size, size, 16), 0:half]
        high = self.slot.at[ds(start + (1 - at.x) * size, size, 16), half : 2 * half]
        self.by_y = self.links.copy(low, self.from_y, self.from_y, at.near(4)).start()
        self.by_x = self.links.copy(high, self.from_x, self.from_x, at.near(2)).start()

    def depth(self):
        at, size, half = self.at, self.size, self.half
        start = at.c * 2 * size
        for copy, mine, other, col in (
            (self.by_y, at.y, self.from_y, slice(0, half)),
            (self.by_x, at.x, self.from_x, slice(half, 2 * half)),
        ):
            copy.wait_recv()

            def body(r):
                v = self.slot[ds(start + mine * size + r, 16, 16), col].astype(F32) + other[pl.ds(r, 16), :].astype(F32)
                self.own[pl.ds(r, 16), col] = v.astype(BF)

            rows_loop(size, 16, body)
        self.along = Along(self.links, at, self.own, self.from_z, self.total).start()

    def hop(self, i):
        self.along.hop(i)

    def finish(self):
        self.along.finish()


ORDER = (
    "mc", "halo", "widen", "s4", "s3", "s1", "ph0", "mp", "s2", "s0", "b0", "ph1", "b1", "w2", "t0", "u0", "t1",
    "u1", "pl0", "t2", "u2", "pl1", "t3", "d0", "u3", "pl2", "t4", "h0", "d1", "u4", "mx", "pf", "pl3", "d2",
    "g0", "b2", "h1", "pl4", "h2", "b3", "md", "f0", "p2", "g1", "b4", "g2", "sums", "mh0", "d3", "f1", "d4",
    "f2", "q0", "p3", "mh1", "e1", "h3", "q1", "h4", "q2", "r0", "r1", "mf", "store", "r2", "g3", "m2", "g4",
    "f3", "m3", "f4", "q3", "q4", "r3", "r4",
)


def backward_kernel(
    sizes,
    features,
    active_one,
    active_x,
    active_y,
    vectors,
    pool_own,
    middle_low,
    full_conv,
    term_mix,
    grad_conv,
    grad_mix,
    grad_pool,
    grad_features,
    sums_out,
    edged,
    edged_x,
    edged_y,
    ext,
    shifted,
    shifted_two,
    weight,
    grad_active,
    slots,
    core_slots,
    from_x,
    from_y,
    own,
    from_z,
    total,
    mix_slot,
    mix_core,
    mix_x,
    mix_y,
    mix_yx,
    mix_xy,
    mix_own,
    mix_z,
    mix_total,
    pool_z,
    pool_total,
    mine,
    seq_slots,
    fsdp_slots,
    send,
    recv,
    seq_send,
    seq_recv,
    fsdp_send,
    fsdp_recv,
    local,
):
    seq, fsdp = sizes
    at = Place(seq, fsdp)
    links = Links(send, recv)
    rows, cin = features.shape
    cout = full_conv.shape[1]
    taps = full_conv.shape[0] // cin
    all_rows = float(rows * seq * fsdp)
    lead = 16
    half_in, half_out = cin // 2, cout // 2
    tap_share = cin // GROUP

    def load_weight(i):
        return pltpu.make_async_copy(full_conv.at[pl.ds(i * half_in, half_in)], weight.at[i % 2], local.at[i % 2])

    top, bottom, inner = pl.ds(0, lead), pl.ds(lead + rows, lead), pl.ds(lead, rows)
    load_middle = pltpu.make_async_copy(middle_low, edged.at[inner], local.at[3])
    load_middle.start()
    load_mix = pltpu.make_async_copy(term_mix, mix_slot, local.at[2])
    load_mix.start()
    load_weight(0).start()
    load_weight(1).start()
    at.barrier()
    below = links.copy(middle_low.at[pl.ds(0, lead)], edged.at[bottom], edged.at[bottom], at.up(fsdp - 1)).start()
    above = links.copy(middle_low.at[pl.ds(rows - lead, lead)], edged.at[top], edged.at[top], at.up(1)).start()
    pairs = ((edged_x, 2, slice(0, half_out)), (edged_y, 4, slice(half_out, cout)))
    exchanged = [
        links.copy(middle_low.at[:, col], target.at[inner], target.at[inner], at.near(mask)).start()
        for target, mask, col in pairs
    ]
    pool = Along(links, at, pool_own, pool_z, pool_total).start()
    groups = []

    def spread(block, target, start, order):
        size = block.shape[0]

        def place(part, half):
            first = start + order(part) * size
            if half is None:
                return target.at[ds(first, size, 16)]
            return target.at[ds(first + half * (size // 2), size // 2, 16)]

        keep = pltpu.make_async_copy(block, place(at.part, None), local.at[4 + len(groups)])
        group = Spread(links, at, place, block)
        groups.append((group, keep))
        group.one()
        keep.start()
        return group

    def tap_order(part):
        c, x, y = part & 1, (part >> 1) & 1, part >> 2
        low = at.z < fsdp // 2
        return jnp.where(low, x, y) * 4 + c * 2 + jnp.where(low, y, x)

    def natural_order(part):
        return part

    mix = Reduce(links, at, mix_slot, (mix_core, mix_x, mix_y, mix_yx, mix_xy, mix_own))
    def halo():
        load_middle.wait()
        below.wait_recv()
        above.wait_recv()
        edged[top, :] = jnp.where(at.z > 0, edged[top, :], jnp.zeros((lead, cout), BF))
        edged[bottom, :] = jnp.where(at.z < fsdp - 1, edged[bottom, :], jnp.zeros((lead, cout), BF))
        exchanged.extend(
            links.copy(edged.at[part, col], target.at[part], target.at[part], at.near(mask)).start()
            for target, mask, col in pairs
            for part in (top, bottom)
        )

    def widen():
        def body(r):
            ext[pl.ds(r, 32), :] = edged[pl.ds(r, 32), :].astype(F32)

        rows_loop(rows + 2 * lead, 32, body)

    def widen_two():
        for copy in exchanged:
            copy.wait_recv()

        def body(r):
            ext[pl.ds(r, 32), 0:half_out] = edged_x[pl.ds(r, 32), :].astype(F32)
            ext[pl.ds(r, 32), half_out:cout] = edged_y[pl.ds(r, 32), :].astype(F32)

        rows_loop(rows + 2 * lead, 32, body)

    half_width = (taps - 1) // 2

    def shift(target, k):
        start = lead + half_width - k

        def body(i, carry):
            col = ds(i * 128, 128, 128)
            target[:, col] = ext[pl.ds(start, rows), col].astype(BF)
            return carry

        lax.fori_loop(0, cout // 128, body, 0)

    def back(k):
        for i in (2 * k, 2 * k + 1):
            load_weight(i).wait()

            for j in range(2):
                at_row = j * (half_in // 2)
                col = slice((i % 2) * half_in + at_row, (i % 2) * half_in + at_row + half_in // 2)
                v = dot(shifted[k], weight[i % 2, at_row : at_row + half_in // 2, :], 1, 1)
                grad_active[:, col] = v if k == 0 else grad_active[:, col] + v
            if i + 2 < 2 * taps:
                load_weight(i + 2).start()

    columns = (ds(at.x * half_in, half_in, 128), ds(at.y * half_in, half_in, 128))
    tile = 256

    def product(k, i):
        other = (active_x, active_y)[i]

        def body(j, carry):
            col = ds(i * half_out + j * tile, tile, 128)
            v = dot(active_one[:, columns[i]], shifted[k, :, col], 0, 0)
            v = v + dot(other[...], shifted_two[:, col], 0, 0)
            slots[k, :, col] = v.astype(BF)
            return carry

        lax.fori_loop(0, half_out // tile, body, 0)

    steps = []
    for k in range(taps):
        mine_rows = pl.ds(k * tap_share, tap_share)
        steps.append(
            Tap(
                links,
                at,
                slots.at[k],
                (
                    core_slots.at[k],
                    from_x.at[mine_rows],
                    from_y.at[mine_rows],
                    own.at[mine_rows],
                    from_z.at[:, mine_rows],
                    total.at[mine_rows],
                ),
            )
        )
    mean_one, scale_one, gain_one, shift_one = (vectors[i : i + 1, :cin] for i in range(4))
    sems = (seq_send, seq_recv, fsdp_send, fsdp_recv)
    stats = Exchange(at, mine, seq_slots, fsdp_slots, sems)

    def normed(r):
        return (features[pl.ds(r, 32), :].astype(F32) - mean_one) * scale_one

    def sums():
        def grad_before(r):
            n = normed(r)
            v = normal(n * gain_one + shift_one)[1] * grad_active[pl.ds(r, 32), :]
            grad_active[pl.ds(r, 32), :] = v
            return v, v * n

        sum_shift, sum_gain = row_sums(rows, 32, cin, 2, grad_before)
        pad = jnp.zeros((1, cout - cin), F32)
        wide = lambda v: jnp.concatenate([v, pad], axis=1)
        stats.start(pack(wide(sum_shift), wide(sum_gain), vectors[6:7, :], vectors[7:8, :]))

    def store():
        everyone = unpack(stats.end(combine_sums))
        shift_grad, gain_grad = everyone[0][:, :cin], everyone[1][:, :cin]

        def body(r):
            v = grad_active[pl.ds(r, 32), :] - shift_grad / all_rows - normed(r) * gain_grad / all_rows
            grad_features[pl.ds(r, 32), :] = (gain_one * scale_one * v).astype(BF)

        rows_loop(rows, 32, body)
        sums_out[0:4, :] = jnp.concatenate(everyone, axis=0)

    spreads = {}

    def mix_core():
        load_mix.wait()
        mix.core()

    mix_along = Along(links, at, mix_own, mix_z, mix_total)

    def mix_depth():
        mix.depth()
        mix_along.start()

    def finish(name, along, target, start, order):
        along().finish()
        spreads[name] = spread(along().total, target, start, order)

    def first(k):
        shift(shifted_two, k)
        product(k, 0)

    def second(k):
        product(k, 1)
        steps[k].core()

    actions = {
        "halo": halo,
        "widen": widen,
        "w2": widen_two,
        "sums": sums,
        "e1": lambda: stats.middle(combine_sums),
        "store": store,
        "mc": mix_core,
        "mp": mix.plane,
        "mx": mix.cross,
        "md": mix_depth,
        "mh0": lambda: mix_along.hop(0),
        "mh1": lambda: mix_along.hop(1),
        "mf": lambda: finish("m", lambda: mix_along, grad_mix, 0, natural_order),
        "m2": lambda: spreads["m"].two(),
        "m3": lambda: spreads["m"].three(),
        "ph0": lambda: pool.hop(0),
        "ph1": lambda: pool.hop(1),
        "pf": lambda: finish("p", lambda: pool, grad_pool, 0, natural_order),
        "p2": lambda: spreads["p"].two(),
        "p3": lambda: spreads["p"].three(),
    }
    of_tap = {
        "s": lambda k: shift(shifted.at[k], k),
        "b": back,
        "t": first,
        "u": second,
        "pl": lambda k: steps[k].plane(),
        "d": lambda k: steps[k].depth(),
        "h": lambda k: steps[k].hop(0),
        "g": lambda k: steps[k].hop(1),
        "f": lambda k: finish(k, lambda: steps[k].along, grad_conv, k * cin, tap_order),
        "q": lambda k: spreads[k].two(),
        "r": lambda k: spreads[k].three(),
    }
    for name, action in of_tap.items():
        for k in range(taps):
            actions[f"{name}{k}"] = functools.partial(action, k)
    for name in ORDER:
        actions.pop(name)()
    assert not actions
    for group, keep in groups:
        group.four()
        keep.wait()
    links.drain()


def run_backward(sizes, features, active_one, active_x, active_y, vectors, pool_own, middle_low, full_conv, term_mix):
    seq, fsdp = sizes
    rows, cin = features.shape
    deep, cout = full_conv.shape
    taps = deep // cin
    width = cout // fsdp
    tap_share = cin // GROUP
    shape = jax.ShapeDtypeStruct
    vmem = pl.BlockSpec(memory_space=pltpu.VMEM)
    hbm = pl.BlockSpec(memory_space=pl.ANY)
    copies = 160
    return pl.pallas_call(
        functools.partial(backward_kernel, sizes),
        out_shape=(
            shape((deep, width), BF),
            shape((cout, width), BF),
            shape((cout, width), BF),
            shape((rows, cin), BF),
            shape((8, cout), F32),
        ),
        in_specs=[vmem, vmem, vmem, vmem, vmem, vmem, hbm, hbm, hbm],
        out_specs=(hbm, hbm, hbm, vmem, vmem),
        scratch_shapes=[
            pltpu.VMEM((rows + 32, cout), BF),
            pltpu.VMEM((rows + 32, cout // 2), BF),
            pltpu.VMEM((rows + 32, cout // 2), BF),
            pltpu.VMEM((rows + 32, cout), F32),
            pltpu.VMEM((taps, rows, cout), BF),
            pltpu.VMEM((rows, cout), BF),
            pltpu.VMEM((2, cin // 2, cout), BF),
            pltpu.VMEM((rows, cin), F32),
            pltpu.VMEM((taps, cin // 2, cout), BF),
            pltpu.VMEM((taps, cin // 4, cout), BF),
            pltpu.VMEM((taps * tap_share, cout // 2), BF),
            pltpu.VMEM((taps * tap_share, cout // 2), BF),
            pltpu.VMEM((taps * tap_share, cout), BF),
            pltpu.VMEM((fsdp - 1, taps * tap_share, width), BF),
            pltpu.VMEM((taps * tap_share, width), BF),
            pltpu.VMEM((cout, cout), BF),
            *Reduce.scratch(cout, cout),
            pltpu.VMEM((cout // GROUP, cout), BF),
            pltpu.VMEM((fsdp - 1, cout // GROUP, width), BF),
            pltpu.VMEM((cout // GROUP, width), BF),
            pltpu.VMEM((fsdp - 1, cout // GROUP, width), BF),
            pltpu.VMEM((cout // GROUP, width), BF),
            pltpu.VMEM((2, 16, cout // 4), F32),
            pltpu.VMEM((seq, 16, cout // 4), F32),
            pltpu.VMEM((fsdp, 16, cout // 4), F32),
            pltpu.SemaphoreType.DMA((copies,)),
            pltpu.SemaphoreType.DMA((copies,)),
            pltpu.SemaphoreType.DMA((seq,)),
            pltpu.SemaphoreType.DMA((seq,)),
            pltpu.SemaphoreType.DMA((fsdp,)),
            pltpu.SemaphoreType.DMA((fsdp,)),
            pltpu.SemaphoreType.DMA((6 + taps,)),
        ],
        compiler_params=pltpu.CompilerParams(
            collective_id=1, has_side_effects=True, vmem_limit_bytes=62 * 2**20
        ),
    )(features, active_one, active_x, active_y, vectors, pool_own, middle_low, full_conv, term_mix)


def widen_kernel(*refs):
    count = len(refs) // 2
    for source, target in zip(refs[:count], refs[count:]):
        target[...] = source[...].astype(F32)


def widened(*arrays):
    steps = 8
    specs = [pl.BlockSpec((v.shape[0] // steps, v.shape[1]), lambda i: (i, 0)) for v in arrays]
    return pl.pallas_call(
        widen_kernel,
        grid=(steps,),
        in_specs=specs,
        out_specs=specs,
        out_shape=[jax.ShapeDtypeStruct(v.shape, F32) for v in arrays],
    )(*arrays)


def spread_sum(v):
    size = lax.axis_size("seq")
    bit = GROUP
    while bit < size:
        v = v + lax.ppermute(v, "seq", [(i, i ^ bit) for i in range(size)])
        bit *= 2
    return v


def on_device(
    features,
    conv_weight,
    mix_weight,
    pool_weight,
    gain_first,
    shift_first,
    gain_second,
    shift_second,
    bias_conv,
    bias_mix,
    cotangent,
    track_counts,
):
    rows, cin = features.shape
    seq, fsdp = lax.axis_size("seq"), lax.axis_size("fsdp")
    owner = lax.axis_index("fsdp")
    width = conv_weight.shape[2]
    cout = width * fsdp
    taps = conv_weight.shape[0]
    own_vectors = [gain_first, shift_first, gain_second, shift_second, bias_conv, bias_mix]
    ends = [sum(v.shape[0] for v in own_vectors[: i + 1]) for i in range(len(own_vectors))]
    size = -(-ends[-1] // 1024) * 1024
    own_vectors = sum(jnp.pad(v.astype(F32), (end - v.shape[0], size - end)) for v, end in zip(own_vectors, ends))
    own_vectors = own_vectors.reshape(-1, 128)
    full_conv, _, _, term_mix, active_x, active_y, pool_own, pooled, active_one, middle_low, vectors = run_forward(
        (seq, fsdp),
        features,
        conv_weight.reshape(taps * cin, width),
        mix_weight,
        pool_weight,
        own_vectors,
        cotangent,
        track_counts,
    )
    grad_conv, grad_mix, grad_pool, grad_features, sums = run_backward(
        (seq, fsdp), features, active_one, active_x, active_y, vectors, pool_own, middle_low, full_conv, term_mix
    )
    grad_conv, grad_mix, grad_pool = (spread_sum(v) for v in widened(grad_conv, grad_mix, grad_pool))
    grad_conv = grad_conv.reshape(taps, cin, width)
    shift_two_grad, gain_two_grad = vectors[4], vectors[5]
    shift_one_grad, gain_one_grad, bias_one_grad, bias_two_grad = sums[0], sums[1], sums[2], sums[3]

    def share(v, size):
        return lax.dynamic_slice_in_dim(v, owner * size, size)

    first, second = gain_first.shape[0], gain_second.shape[0]
    return (
        pooled,
        grad_features,
        grad_conv,
        grad_mix,
        grad_pool,
        share(gain_one_grad, first),
        share(shift_one_grad, first),
        share(gain_two_grad, second),
        share(shift_two_grad, second),
        share(bias_one_grad, second),
        share(bias_two_grad, second),
    )


def solution(mesh):
    rows = P(("seq", "fsdp"), None)
    vector = P("fsdp")
    in_specs = (rows, P(None, None, "fsdp"), P(None, "fsdp"), P(None, "fsdp")) + (vector,) * 6 + (rows, P())
    out_specs = (rows, rows, P(None, None, "fsdp"), P(None, "fsdp"), P(None, "fsdp")) + (vector,) * 6
    return jax.shard_map(on_device, mesh=mesh, in_specs=in_specs, out_specs=out_specs, check_vma=False)
```

```python
import functools
import math
import jax
import jax.numpy as jnp
from jax import lax
from jax.experimental import pallas as pl
from jax.experimental.pallas import tpu as pltpu
from jax.sharding import PartitionSpec as P

TRACKS = 5313
WIN = 2048
EPSILON = 1e-05
MESH = pl.DeviceIdType.MESH
BF = jnp.bfloat16
F32 = jnp.float32
GROUP = 8


def dot(a, b, ca, cb):
    return lax.dot_general(a, b, (((ca,), (cb,)), ((), ())), preferred_element_type=F32)


def ds(start, size, step):
    return pl.ds(pl.multiple_of(start, step), size)


def fold(v):
    rows, width = v.shape
    return jnp.sum(v.reshape(rows // 8, 8, width), axis=0)


def rows_loop(total, step, body):
    def run(i, carry):
        body(pl.multiple_of(i * step, step))
        return carry

    lax.fori_loop(0, total // step, run, 0)


def row_sums(total, step, width, count, body):
    def run(i, carry):
        parts = body(pl.multiple_of(i * step, step))
        return tuple(c + fold(v) for c, v in zip(carry, parts))

    zero = tuple(jnp.zeros((8, width), F32) for _ in range(count))
    sums = lax.fori_loop(0, total // step, run, zero)
    return [jnp.sum(v, axis=0, keepdims=True) for v in sums]


def normal(b):
    cdf = 0.5 * (1.0 + lax.erf(b * math.sqrt(0.5)))
    pdf = jnp.exp(-0.5 * b * b) * (1.0 / math.sqrt(2.0 * math.pi))
    return cdf, cdf + b * pdf


class Copy:
    def __init__(self, links, src, there, here, device):
        i = links.count
        links.count += 1
        send, recv = links.send.at[i], links.recv.at[i]

        def make(dst):
            return pltpu.make_async_remote_copy(
                src_ref=src,
                dst_ref=dst,
                send_sem=send,
                recv_sem=recv,
                device_id=device,
                device_id_type=MESH,
            )

        self.links = links
        self.out, self.into = functools.partial(make, there), functools.partial(make, here)

    def start(self):
        self.out().start()
        self.links.started.append(self)
        return self

    def wait_recv(self):
        self.into().wait_recv()

    def wait_send(self):
        self.out().wait_send()


class Links:
    def __init__(self, send, recv):
        self.send, self.recv = send, recv
        self.count = 0
        self.started = []

    def copy(self, src, there, here, device):
        return Copy(self, src, there, here, device)

    def drain(self):
        for item in self.started:
            item.wait_send()
        self.started = []


class Place:
    def __init__(self, seq, fsdp):
        self.seq_size, self.fsdp_size = seq, fsdp
        self.s, self.z = lax.axis_index("seq"), lax.axis_index("fsdp")
        self.part = lax.rem(self.s, GROUP)
        self.base = self.s - self.part
        self.c, self.x, self.y = self.part & 1, (self.part >> 1) & 1, self.part >> 2

    def near(self, mask):
        return (self.base + jnp.bitwise_xor(self.part, mask), self.z)

    def up(self, d):
        return (self.s, lax.rem(self.z + d, self.fsdp_size))

    def barrier(self):
        bar = pltpu.get_barrier_semaphore()

        def greet(i, carry):
            peer = lax.rem(self.s + i, self.seq_size)
            pl.semaphore_signal(bar, inc=1, device_id=(peer, self.z), device_id_type=MESH)
            return carry

        lax.fori_loop(1, self.seq_size, greet, 0)
        for d in range(1, self.fsdp_size):
            pl.semaphore_signal(bar, inc=1, device_id=self.up(d), device_id_type=MESH)
        pl.semaphore_wait(bar, self.seq_size + self.fsdp_size - 2)


class Exchange:
    def __init__(self, place, mine, seq_slots, fsdp_slots, sems):
        self.place, self.mine = place, mine
        self.seq_slots, self.fsdp_slots = seq_slots, fsdp_slots
        self.seq_send, self.seq_recv, self.fsdp_send, self.fsdp_recv = sems

    def _copy(self, i, stage):
        at = self.place
        if stage == 0:
            peer = lax.rem(at.s + i, at.seq_size)
            source = lax.rem(at.s - i + at.seq_size, at.seq_size)
            device, slots, send, recv, me = (peer, at.z), self.seq_slots, self.seq_send, self.seq_recv, at.s
        else:
            peer = lax.rem(at.z + i, at.fsdp_size)
            source = lax.rem(at.z - i + at.fsdp_size, at.fsdp_size)
            device, slots, send, recv, me = (at.s, peer), self.fsdp_slots, self.fsdp_send, self.fsdp_recv, at.z
        make = lambda slot: pltpu.make_async_remote_copy(
            src_ref=self.mine.at[stage],
            dst_ref=slots.at[slot],
            send_sem=send.at[i],
            recv_sem=recv.at[i],
            device_id=device,
            device_id_type=MESH,
        )
        return functools.partial(make, me), functools.partial(make, source)

    def _each(self, stage, what):
        size = self.place.seq_size if stage == 0 else self.place.fsdp_size

        def run(i, carry):
            what(*self._copy(i, stage))
            return carry

        lax.fori_loop(1, size, run, 0)

    def start(self, block):
        self.mine[0] = block
        self.seq_slots[self.place.s] = block
        self._each(0, lambda out, into: out().start())

    def middle(self, combine):
        self._each(0, lambda out, into: into().wait_recv())
        block = combine(self.seq_slots)
        self.mine[1] = block
        self.fsdp_slots[self.place.z] = block
        self._each(1, lambda out, into: out().start())

    def end(self, combine):
        self._each(1, lambda out, into: into().wait_recv())
        block = combine(self.fsdp_slots)
        self._each(0, lambda out, into: out().wait_send())
        self._each(1, lambda out, into: out().wait_send())
        return block

    def finish(self, combine):
        self.middle(combine)
        return self.end(combine)


def pack(*vectors):
    width = vectors[0].shape[1] // 4
    pieces = [v[:, i * width : (i + 1) * width] for v in vectors for i in range(4)]
    return jnp.concatenate(pieces, axis=0)


def unpack(block):
    count = block.shape[0] // 4
    return [jnp.concatenate([block[4 * j + i : 4 * j + i + 1] for i in range(4)], axis=1) for j in range(count)]


def combine_sums(slots):
    return jnp.sum(slots[...], axis=0)


def combine_moments(slots):
    v = slots[...]
    center, spread = v[:, :4], v[:, 4:]
    mean = jnp.mean(center, axis=0)
    rest = jnp.mean(spread + jnp.square(center - mean[None]), axis=0)
    return jnp.concatenate([mean, rest], axis=0)


class Spread:
    def __init__(self, links, at, place, source=None):
        self.links, self.at, self.place, self.source = links, at, place, source
        self.held = {}

    def _send(self, name, mask, of, half=None):
        part = self.at.part
        mine = self.place(jnp.bitwise_xor(part, of), half)
        theirs = self.place(jnp.bitwise_xor(part, of ^ mask), half)
        src = mine if of or self.source is None else self.source
        self.held[name] = self.links.copy(src, mine, theirs, self.at.near(mask)).start()

    def one(self):
        self._send("x", 2, 0)
        self._send("y", 4, 0)
        self._send("c", 1, 0)

    def two(self):
        self.held["x"].wait_recv()
        self._send("xa", 4, 2, 0)
        self._send("xc", 1, 2)
        self.held["y"].wait_recv()
        self._send("yb", 2, 4, 1)
        self._send("yc", 1, 4)

    def three(self):
        self.held["xa"].wait_recv()
        self._send("ac", 1, 6, 0)
        self.held["yb"].wait_recv()
        self._send("bc", 1, 6, 1)

    def four(self):
        for name in ("c", "xc", "yc", "ac", "bc"):
            self.held[name].wait_recv()


class Gather:
    def __init__(self, links, at, shard, full, d, lo, size):
        self.links, self.at, self.shard, self.full, self.d = links, at, shard, full, d
        self.lo, self.size = lo, size
        self.share, self.width = shard.shape[0] // GROUP, shard.shape[1]
        self.z = lax.rem(at.z - d + at.fsdp_size, at.fsdp_size)
        spread = Spread(links, at, lambda part, half: self.full.at[self._rows(part, half), self._columns(self.z)])
        self.spread, self.two, self.three, self.four = spread, spread.two, spread.three, spread.four

    def _rows(self, part, half=None):
        start = part * self.share + self.lo
        if half is None:
            return ds(start, self.size, 16)
        return ds(start + half * (self.size // 2), self.size // 2, 16)

    def _columns(self, z):
        return ds(z * self.width, self.width, 128)

    def send(self):
        at = self.at
        rows = self._rows(at.part)
        passed = self._columns(lax.rem(self.z + 1, at.fsdp_size))
        there = self.full.at[rows, passed]
        here = self.full.at[rows, self._columns(self.z)]
        src = self.shard.at[rows] if self.d == 1 else there
        self.along = self.links.copy(src, there, here, at.up(1)).start()

    def arrive(self):
        self.along.wait_recv()

    def one(self):
        self.arrive()
        self.spread.one()


def put_blocks(target, half, values, col):
    size = values.shape[0] // 8
    for i in range(8):
        part, side = 4 * half + i // 2, i % 2
        c, x, y = part & 1, part >> 1 & 1, part >> 2
        at = 8 * c + 4 * side + (2 * x + y if side == 0 else 2 * y + x)
        target[at * size : (at + 1) * size, col] = values[i * size : (i + 1) * size].astype(BF)


def forward_kernel(
    sizes,
    features,
    conv_shard,
    mix_shard,
    pool_shard,
    vectors_in,
    cotangent,
    track_counts,
    full_conv,
    full_mix,
    full_pool,
    term_mix,
    active_x,
    active_y,
    pool_own,
    pooled,
    active_out,
    middle_low,
    vectors,
    ext,
    taps,
    wbuf,
    mixw,
    middle,
    deriv,
    work,
    a2,
    low,
    low2,
    gbuf,
    pair_one,
    pair_two,
    pool_core,
    pool_x,
    pool_y,
    pool_yx,
    pool_xy,
    mine,
    seq_slots,
    fsdp_slots,
    packs,
    edges,
    moment,
    send,
    recv,
    seq_send,
    seq_recv,
    fsdp_send,
    fsdp_recv,
    local,
):
    seq, fsdp = sizes
    at = Place(seq, fsdp)
    links = Links(send, recv)
    rows, cin = features.shape
    cout = full_conv.shape[1]
    width = cout // fsdp
    total = float(rows * seq * fsdp)
    taps_count = conv_shard.shape[0] // cin
    lead = 8

    def exchange(i):
        sems = (seq_send.at[i], seq_recv.at[i], fsdp_send.at[i], fsdp_recv.at[i])
        return Exchange(at, mine.at[i], seq_slots.at[i], fsdp_slots.at[i], sems)

    own_conv = pltpu.make_async_copy(wbuf.at[0], full_conv.at[:, ds(at.z * width, width, 128)], local.at[0])
    mixing, pooling = pl.ds(0, cout), pl.ds(cout, cout)
    own_mix = pltpu.make_async_copy(mix_shard, mixw.at[mixing, ds(at.z * width, width, 128)], local.at[1])
    own_pool = pltpu.make_async_copy(pool_shard, mixw.at[pooling, ds(at.z * width, width, 128)], local.at[4])
    own_load = pltpu.make_async_copy(conv_shard, wbuf.at[0], local.at[2])

    at.barrier()
    near = range(1, fsdp)
    share = conv_shard.shape[0] // GROUP
    cut = share * 2 // 5 // 32 * 32
    conv = [Gather(links, at, conv_shard, full_conv, d, *piece) for d in near for piece in ((0, cut), (cut, share - cut))]
    mix, poolw = (
        [Gather(links, at, shard, full, d, 0, cout // GROUP) for d in near]
        for shard, full in ((mix_shard, full_mix), (pool_shard, full_pool))
    )
    parcels = []
    for d in near:
        source = lax.rem(at.z - d + fsdp, fsdp)
        parcels.append(links.copy(vectors_in, packs.at[at.z], packs.at[source], at.up(d)).start())
    parcels.append(links.copy(features.at[pl.ds(0, 16)], edges.at[1], edges.at[1], at.up(fsdp - 1)).start())
    parcels.append(links.copy(features.at[pl.ds(rows - 16, 16)], edges.at[0], edges.at[0], at.up(1)).start())
    conv[0].send()
    own_load.start()
    own_mix.start()
    own_pool.start()

    (sum_one,) = row_sums(rows, 64, cin, 1, lambda r: (features[pl.ds(r, 64), :].astype(F32),))
    mean = sum_one / rows
    (dev_one,) = row_sums(rows, 64, cin, 1, lambda r: (jnp.square(features[pl.ds(r, 64), :].astype(F32) - mean),))
    pad = jnp.zeros((1, cout - cin), F32)
    stats = exchange(0)
    stats.start(pack(jnp.concatenate([mean, pad], axis=1), jnp.concatenate([dev_one / rows, pad], axis=1)))
    packs[at.z] = vectors_in[...]
    stats.middle(combine_moments)
    conv[0].one()
    for parcel in parcels:
        parcel.wait_recv()
    share_in = cin // fsdp

    def vector(first, size):
        pieces = []
        for z in range(fsdp):
            for row in range(first // 128, -(-(first + size) // 128)):
                lo, hi = max(first - row * 128, 0), min(first + size - row * 128, 128)
                pieces.append(packs[z, row : row + 1, lo:hi])
        return jnp.concatenate(pieces, axis=1)

    gain_one, shift_one = vector(0, share_in), vector(share_in, share_in)
    gain_two, shift_two, bias_one, bias_two = (vector(2 * share_in + i * width, width) for i in range(4))
    moment[2:3, :] = bias_one
    mean_one, var_one = unpack(stats.end(combine_moments))
    conv[1].send()
    conv[2].send()
    mean_one, scale_one = mean_one[:, :cin], lax.rsqrt(var_one[:, :cin] + EPSILON)

    def active(v):
        b = (v - mean_one) * scale_one * gain_one + shift_one
        return b * (0.5 * (1.0 + lax.erf(b * math.sqrt(0.5))))

    def first_active(r):
        v = active(features[pl.ds(r, 32), :].astype(F32)).astype(BF)
        active_out[pl.ds(r, 32), :] = v
        ext[pl.ds(lead + r, 32), :cin] = v.astype(F32)

    rows_loop(rows, 32, first_active)
    conv[1].one()
    conv[3].send()
    conv[0].two()
    row = lax.broadcasted_iota(jnp.int32, (8, cin), 0)
    before, after = edges[0].astype(F32)[8:16], edges[1].astype(F32)[0:8]
    ext[0:lead, :cin] = jnp.where((row >= 6) & (at.z > 0), active(before), 0.0)
    ext[lead + rows : lead + rows + 8, :cin] = jnp.where((row < 2) & (at.z < fsdp - 1), active(after), 0.0)
    def shifted(k):
        def body(i, carry):
            col = ds(i * 128, 128, 128)
            taps[:, ds(k * cin + i * 128, 128, 128)] = ext[pl.ds(lead - 2 + k, rows), col].astype(BF)
            return carry

        lax.fori_loop(0, cin // 128, body, 0)

    for k in range(taps_count):
        shifted(k)
    conv[2].one()
    conv[4].send()
    conv[1].two()
    conv[0].three()

    def load_block(slot, z):
        copy = pltpu.make_async_copy(full_conv.at[:, ds(z * width, width, 128)], wbuf.at[slot], local.at[3])
        copy.start()
        return copy

    def multiply(slot, z, half):
        row = pl.ds(half * (rows // 2), rows // 2)
        middle[row, ds(z * width, width, 128)] = dot(taps[row, :], wbuf[slot], 1, 0)

    def moments(z):
        col = ds(z * width, width, 128)
        bias = moment[2:3, col]

        def plus_bias(r):
            v = middle[pl.ds(r, 64), col] + bias
            middle[pl.ds(r, 64), col] = v
            return (v,)

        (total_two,) = row_sums(rows, 64, width, 1, plus_bias)
        mean = total_two / rows
        (dev_two,) = row_sums(rows, 64, width, 1, lambda r: (jnp.square(middle[pl.ds(r, 64), col] - mean),))
        moment[0:1, col] = mean
        moment[1:2, col] = dev_two / rows

    def load_later(part, i, target):
        col = ds(part[i].z * width, width, 128)
        copy = pltpu.make_async_copy(part[i].full.at[:, col], mixw.at[target, col], local.at[5 + i])
        copy.start()
        return copy

    own_load.wait()
    own_conv.start()
    multiply(0, at.z, 0)
    conv[3].one()
    conv[5].send()
    conv[2].two()
    conv[1].three()
    conv[0].four()
    multiply(0, at.z, 1)
    own_conv.wait()
    moments(at.z)
    conv[4].one()
    mix[0].send()
    conv[3].two()
    conv[2].three()
    conv[1].four()
    block = load_block(1, conv[0].z)
    conv[5].one()
    poolw[0].send()
    conv[4].two()
    conv[3].three()
    conv[2].four()
    block.wait()
    multiply(1, conv[0].z, 0)
    mix[0].one()
    mix[1].send()
    conv[5].two()
    conv[4].three()
    conv[3].four()
    block = load_block(0, conv[2].z)
    multiply(1, conv[0].z, 1)
    moments(conv[0].z)
    mix[1].one()
    mix[2].send()
    block.wait()
    multiply(0, conv[2].z, 0)
    conv[5].three()
    conv[4].four()
    multiply(0, conv[2].z, 1)
    moments(conv[2].z)
    mix[0].two()
    mix[2].one()
    poolw[0].arrive()
    poolw[1].send()
    conv[5].four()
    block = load_block(1, conv[4].z)
    mix[1].two()
    mix[0].three()
    poolw[0].spread.one()
    block.wait()
    multiply(1, conv[4].z, 0)
    mix[1].three()
    mix[2].two()
    poolw[1].arrive()
    poolw[2].send()
    multiply(1, conv[4].z, 1)
    moments(conv[4].z)
    poolw[0].two()
    mix[2].three()

    stats = exchange(1)
    stats.start(pack(moment[0:1, :], moment[1:2, :]))
    for part in mix:
        part.four()
    loads = [load_later(mix, i, mixing) for i in range(fsdp - 1)]
    stats.middle(combine_moments)
    poolw[1].spread.one()
    poolw[2].one()
    mean_two, var_two = unpack(stats.end(combine_moments))
    scale_two = lax.rsqrt(var_two + EPSILON)

    def second_active(r):
        b = (middle[pl.ds(r, 32), :] - mean_two) * scale_two * gain_two + shift_two
        cdf, slope = normal(b)
        a2[pl.ds(r, 32), :] = (b * cdf).astype(BF)
        deriv[pl.ds(r, 32), :] = slope

    rows_loop(rows // 2, 32, second_active)
    poolw[0].three()
    poolw[1].two()
    rows_loop(rows // 2, 32, lambda r: second_active(rows // 2 + r))
    poolw[2].two()
    half = cin // 2
    actives = [
        links.copy(active_out.at[:, ds((1 - at.x) * half, half, 128)], active_x, active_x, at.near(2)).start(),
        links.copy(active_out.at[:, ds((1 - at.y) * half, half, 128)], active_y, active_y, at.near(4)).start(),
    ]
    poolw[1].three()
    own_mix.wait()
    for load in loads:
        load.wait()

    tile = 512
    tiles = cout // tile

    def block_columns(z):
        return ds(z * width, width, 128)

    def column_loop(body):
        def run(i, carry):
            body(ds(i * tile, tile, 128))
            return carry

        lax.fori_loop(0, tiles, run, 0)

    def add_mix(col):
        work[:, col] = dot(a2[...], mixw[0:cout, col], 1, 0)

    column_loop(add_mix)
    poolw[2].three()

    def add_residual(r):
        v = middle[pl.ds(r, 32), :] + work[pl.ds(r, 32), :] + bias_two
        ext[pl.ds(r, 32), :] = v
        low[pl.ds(r, 32), :] = v.astype(BF)

    rows_loop(rows, 32, add_residual)

    def add_pool(col):
        work[:, col] = dot(low[...], mixw[cout : 2 * cout, col], 1, 0)

    own_pool.wait()
    add_pool(block_columns(at.z))
    ready = None
    for i in range(fsdp - 1):
        poolw[i].four()
        load = load_later(poolw, i, pooling)
        if ready is not None:
            ready.wait()
            add_pool(block_columns(poolw[i - 1].z))
        ready = load
    ready.wait()
    add_pool(block_columns(poolw[fsdp - 2].z))

    scale = track_counts[(at.s * fsdp + at.z) * rows // WIN].astype(F32) / TRACKS

    def pairs(i, carry):
        col = ds(i * 128, 128, 128)
        even, odd = pl.ds(0, rows // 2, 2), pl.ds(1, rows // 2, 2)
        one, two = pair_one, pair_two
        one[...], two[...] = work[:, col], ext[0:rows, col]
        l0, l1 = one[even, :], one[odd, :]
        s0, s1 = two[even, :], two[odd, :]
        top = jnp.maximum(l0, l1)
        e0, e1 = jnp.exp(l0 - top), jnp.exp(l1 - top)
        inverse = 1.0 / (e0 + e1)
        w0, w1 = e0 * inverse, e1 * inverse
        up = cotangent[:, col].astype(F32) * scale
        pooled[:, col] = (w0 * s0 + w1 * s1).astype(BF)
        g0, g1 = s0 * up, s1 * up
        both = w0 * g0 + w1 * g1
        one[even, :] = w0 * up
        one[odd, :] = w1 * up
        two[even, :] = w0 * (g0 - both)
        two[odd, :] = w1 * (g1 - both)
        work[:, col] = one[...]
        low2[:, col] = two[...].astype(BF)
        return carry

    lax.fori_loop(0, cout // 128, pairs, 0)

    def product(left, right, gbuf):
        half = cout // 2
        for i in range(2):
            def body(j, carry):
                col = ds(j * tile, tile, 128)
                put_blocks(gbuf, i, dot(left[:, i * half : (i + 1) * half], right[:, col], 0, 0), col)
                return carry

            lax.fori_loop(0, tiles, body, 0)

    product(low, low2, gbuf)
    pool_buffers = (pool_core, pool_x, pool_y, pool_yx, pool_xy, pool_own)
    pool = Reduce(links, at, gbuf, pool_buffers)
    pool.core()

    def back_pool(col):
        ext[0:rows, col] = dot(low2[...], mixw[ds(cout + col.start, tile, 128), :], 1, 1)

    column_loop(back_pool)

    def grad_summed(r):
        v = work[pl.ds(r, 32), :] + ext[pl.ds(r, 32), :]
        work[pl.ds(r, 32), :] = v
        low[pl.ds(r, 32), :] = v.astype(BF)
        return (v,)

    pool.plane()
    (sum_bias_two,) = row_sums(rows, 32, cout, 1, grad_summed)

    def back_mix(col):
        ext[0:rows, col] = dot(low[...], mixw[ds(col.start, tile, 128), :], 1, 1)

    column_loop(back_mix)

    def normed(r):
        return (middle[pl.ds(r, 32), :] - mean_two) * scale_two

    def grad_before(r):
        v = ext[pl.ds(r, 32), :] * deriv[pl.ds(r, 32), :]
        ext[pl.ds(r, 32), :] = v
        return v, v * normed(r)

    sum_shift, sum_gain = row_sums(rows, 32, cout, 2, grad_before)
    stats = exchange(2)
    stats.start(pack(sum_shift, sum_gain))
    product(a2, low, mixw.at[pooling])
    out_mix = pltpu.make_async_copy(mixw.at[pooling], term_mix, local.at[4])
    out_mix.start()
    stats.middle(combine_sums)
    pool.cross()
    shift_two_grad, gain_two_grad = unpack(stats.end(combine_sums))

    def grad_middle(r):
        v = work[pl.ds(r, 32), :] + gain_two * scale_two * (
            ext[pl.ds(r, 32), :] - shift_two_grad / total - normed(r) * gain_two_grad / total
        )
        middle_low[pl.ds(r, 32), :] = v.astype(BF)
        return (v,)

    (sum_bias_one,) = row_sums(rows, 32, cout, 1, grad_middle)
    fill = lambda v: jnp.concatenate([v, pad], axis=1)
    vectors[0:8, :] = jnp.concatenate(
        [fill(mean_one), fill(scale_one), fill(gain_one), fill(shift_one), shift_two_grad, gain_two_grad, sum_bias_one, sum_bias_two],
        axis=0,
    )
    pool.depth()
    for copy in actives:
        copy.wait_recv()
    out_mix.wait()
    links.drain()


def run_forward(sizes, features, conv_shard, mix_shard, pool_shard, vectors_in, cotangent, track_counts):
    seq, fsdp = sizes
    rows, cin = features.shape
    cout = conv_shard.shape[1] * fsdp
    deep = conv_shard.shape[0]
    two = 2 * cout
    shape = jax.ShapeDtypeStruct
    vmem = pl.BlockSpec(memory_space=pltpu.VMEM)
    hbm = pl.BlockSpec(memory_space=pl.ANY)
    copies = 140
    half = (rows, cin // 2)
    pool = Reduce.scratch(cout, cout)
    return pl.pallas_call(
        functools.partial(forward_kernel, sizes),
        out_shape=(
            shape((deep, cout), BF),
            shape((cout, cout), BF),
            shape((cout, cout), BF),
            shape((cout, cout), BF),
            shape(half, BF),
            shape(half, BF),
            shape((cout // GROUP, cout), BF),
            shape((rows // 2, cout), BF),
            shape((rows, cin), BF),
            shape((rows, cout), BF),
            shape((8, cout), F32),
        ),
        in_specs=[vmem, hbm, hbm, hbm, vmem, vmem, pl.BlockSpec(memory_space=pltpu.SMEM)],
        out_specs=(hbm, hbm, hbm, hbm, hbm, hbm, vmem, vmem, vmem, vmem, vmem),
        scratch_shapes=[
            pltpu.VMEM((rows + 16, cout), F32),
            pltpu.VMEM((rows, deep), BF),
            pltpu.VMEM((2, deep, cout // fsdp), BF),
            pltpu.VMEM((two, cout), BF),
            pltpu.VMEM((rows, cout), F32),
            pltpu.VMEM((rows, cout), F32),
            pltpu.VMEM((rows, cout), F32),
            pltpu.VMEM((rows, cout), BF),
            pltpu.VMEM((rows, cout), BF),
            pltpu.VMEM((rows, cout), BF),
            pltpu.VMEM((cout, cout), BF),
            pltpu.VMEM((rows, 128), F32),
            pltpu.VMEM((rows, 128), F32),
            *pool,
            pltpu.VMEM((3, 2, 8, cout // 4), F32),
            pltpu.VMEM((3, seq, 8, cout // 4), F32),
            pltpu.VMEM((3, fsdp, 8, cout // 4), F32),
            pltpu.VMEM((fsdp,) + vectors_in.shape, F32),
            pltpu.VMEM((2, 16, cin), BF),
            pltpu.VMEM((8, cout), F32),
            pltpu.SemaphoreType.DMA((copies,)),
            pltpu.SemaphoreType.DMA((copies,)),
            pltpu.SemaphoreType.DMA((3, seq)),
            pltpu.SemaphoreType.DMA((3, seq)),
            pltpu.SemaphoreType.DMA((3, fsdp)),
            pltpu.SemaphoreType.DMA((3, fsdp)),
            pltpu.SemaphoreType.DMA((4 + fsdp,)),
        ],
        compiler_params=pltpu.CompilerParams(
            collective_id=0, has_side_effects=True, vmem_limit_bytes=62 * 2**20
        ),
    )(features, conv_shard, mix_shard, pool_shard, vectors_in, cotangent, track_counts)


class Reduce:
    def __init__(self, links, at, slot, buffers):
        self.links, self.at, self.slot = links, at, slot
        self.unit = slot.shape[0] // 16
        self.core_slot, self.from_x, self.from_y, self.from_yx, self.from_xy, self.own = buffers

    @staticmethod
    def scratch(height, width):
        unit = height // 16
        return [pltpu.VMEM((r, width), BF) for r in (8 * unit, 2 * unit, 2 * unit, unit, unit)]

    def _rows(self, start, count):
        return self.slot.at[ds(start * self.unit, count * self.unit, 16)]

    def _send(self, src, dst, device):
        return self.links.copy(src, dst, dst, device).start()

    def core(self):
        self.by_core = self._send(self._rows((1 - self.at.c) * 8, 8), self.core_slot, self.at.near(1))

    def _add(self, start, other, count, out=None):
        step = 16
        mine = self._rows(start, count)
        out = mine if out is None else out

        def body(r):
            v = mine[pl.ds(r, step), :].astype(F32) + other[pl.ds(r, step), :].astype(F32)
            out[pl.ds(r, step), :] = v.astype(BF)

        rows_loop(count * self.unit, step, body)

    def plane(self):
        at = self.at
        self.by_core.wait_recv()
        self._add(at.c * 8, self.core_slot, 8)
        self.a, self.b = at.c * 8, at.c * 8 + 4
        self.by_x = self._send(self._rows(self.a + (1 - at.x) * 2, 2), self.from_x, at.near(2))
        self.by_y = self._send(self._rows(self.b + (1 - at.y) * 2, 2), self.from_y, at.near(4))

    def cross(self):
        x, y = self.at.x, self.at.y
        a, b = self.a + x * 2, self.b + y * 2
        self.by_x.wait_recv()
        self._add(a, self.from_x, 2)
        self.by_yx = self._send(self._rows(a + 1 - y, 1), self.from_yx, self.at.near(4))
        self.by_y.wait_recv()
        self._add(b, self.from_y, 2)
        self.by_xy = self._send(self._rows(b + 1 - x, 1), self.from_xy, self.at.near(2))
        self.a, self.b = a + y, b + x

    def depth(self):
        self.by_yx.wait_recv()
        self._add(self.a, self.from_yx, 1, self.own.at[pl.ds(0, self.unit)])
        self.by_xy.wait_recv()
        self._add(self.b, self.from_xy, 1, self.own.at[pl.ds(self.unit, self.unit)])


class Along:
    def __init__(self, links, at, own, from_z, total):
        self.links, self.at, self.own, self.from_z, self.total = links, at, own, from_z, total
        self.width = total.shape[1]
        self.last = at.fsdp_size - 2

    def _column(self, back):
        at = self.at
        return ds(lax.rem(at.z - back + at.fsdp_size, at.fsdp_size) * self.width, self.width, 128)

    def _send(self, src, i):
        dst = self.from_z.at[i]
        self.copy = self.links.copy(src, dst, dst, self.at.up(1)).start()

    def _add(self, i, back, out):
        self.copy.wait_recv()
        col = self._column(back)

        def body(r):
            v = self.own[pl.ds(r, 16), col].astype(F32) + self.from_z[i, pl.ds(r, 16), :].astype(F32)
            out[pl.ds(r, 16), :] = v.astype(BF)

        rows_loop(self.own.shape[0], 16, body)

    def start(self):
        self._send(self.own.at[:, self._column(1)], 0)
        return self

    def hop(self, i):
        self._add(i, i + 2, self.from_z.at[i])
        self._send(self.from_z.at[i], i + 1)

    def finish(self):
        self._add(self.last, 0, self.total)


class Tap:
    def __init__(self, links, at, slot, buffers):
        self.links, self.at, self.slot = links, at, slot
        self.core_slot, self.from_x, self.from_y, self.own, self.from_z, self.total = buffers
        self.size = slot.shape[0] // 4
        self.half = slot.shape[1] // 2

    def core(self):
        at = self.at
        src = self.slot.at[ds((1 - at.c) * 2 * self.size, 2 * self.size, 16)]
        self.by_core = self.links.copy(src, self.core_slot, self.core_slot, at.near(1)).start()

    def plane(self):
        at, size, half = self.at, self.size, self.half
        self.by_core.wait_recv()
        start = at.c * 2 * size

        def body(r):
            row = ds(start + r, 16, 16)
            v = self.slot[row, :].astype(F32) + self.core_slot[pl.ds(r, 16), :].astype(F32)
            self.slot[row, :] = v.astype(BF)

        rows_loop(2 * size, 16, body)
        low = self.slot.at[ds(start + (1 - at.y) * size, size, 16), 0:half]
        high = self.slot.at[ds(start + (1 - at.x) * size, size, 16), half : 2 * half]
        self.by_y = self.links.copy(low, self.from_y, self.from_y, at.near(4)).start()
        self.by_x = self.links.copy(high, self.from_x, self.from_x, at.near(2)).start()

    def depth(self):
        at, size, half = self.at, self.size, self.half
        start = at.c * 2 * size
        for copy, mine, other, col in (
            (self.by_y, at.y, self.from_y, slice(0, half)),
            (self.by_x, at.x, self.from_x, slice(half, 2 * half)),
        ):
            copy.wait_recv()

            def body(r):
                v = self.slot[ds(start + mine * size + r, 16, 16), col].astype(F32) + other[pl.ds(r, 16), :].astype(F32)
                self.own[pl.ds(r, 16), col] = v.astype(BF)

            rows_loop(size, 16, body)
        self.along = Along(self.links, at, self.own, self.from_z, self.total).start()

    def hop(self, i):
        self.along.hop(i)

    def finish(self):
        self.along.finish()


ORDER = (
    "mc", "halo", "widen", "s4", "s3", "s1", "ph0", "mp", "s2", "s0", "b0", "ph1", "b1", "w2", "t0", "u0", "t1",
    "u1", "pl0", "t2", "u2", "pl1", "t3", "d0", "u3", "pl2", "t4", "h0", "d1", "u4", "mx", "pf", "pl3", "d2",
    "g0", "b2", "h1", "pl4", "h2", "b3", "md", "f0", "p2", "g1", "b4", "g2", "sums", "mh0", "d3", "f1", "d4",
    "f2", "q0", "p3", "mh1", "e1", "h3", "q1", "h4", "q2", "r0", "r1", "mf", "store", "r2", "g3", "m2", "g4",
    "f3", "m3", "f4", "q3", "q4", "r3", "r4",
)


def backward_kernel(
    sizes,
    features,
    active_one,
    active_x,
    active_y,
    vectors,
    pool_own,
    middle_low,
    full_conv,
    term_mix,
    grad_conv,
    grad_mix,
    grad_pool,
    grad_features,
    sums_out,
    edged,
    edged_x,
    edged_y,
    ext,
    shifted,
    shifted_two,
    weight,
    grad_active,
    slots,
    core_slots,
    from_x,
    from_y,
    own,
    from_z,
    total,
    mix_slot,
    mix_core,
    mix_x,
    mix_y,
    mix_yx,
    mix_xy,
    mix_own,
    mix_z,
    mix_total,
    pool_z,
    pool_total,
    mine,
    seq_slots,
    fsdp_slots,
    send,
    recv,
    seq_send,
    seq_recv,
    fsdp_send,
    fsdp_recv,
    local,
):
    seq, fsdp = sizes
    at = Place(seq, fsdp)
    links = Links(send, recv)
    rows, cin = features.shape
    cout = full_conv.shape[1]
    taps = full_conv.shape[0] // cin
    all_rows = float(rows * seq * fsdp)
    lead = 16
    half_in, half_out = cin // 2, cout // 2
    tap_share = cin // GROUP

    def load_weight(i):
        return pltpu.make_async_copy(full_conv.at[pl.ds(i * half_in, half_in)], weight.at[i % 2], local.at[i % 2])

    top, bottom, inner = pl.ds(0, lead), pl.ds(lead + rows, lead), pl.ds(lead, rows)
    load_middle = pltpu.make_async_copy(middle_low, edged.at[inner], local.at[3])
    load_middle.start()
    load_mix = pltpu.make_async_copy(term_mix, mix_slot, local.at[2])
    load_mix.start()
    load_weight(0).start()
    load_weight(1).start()
    at.barrier()
    below = links.copy(middle_low.at[pl.ds(0, lead)], edged.at[bottom], edged.at[bottom], at.up(fsdp - 1)).start()
    above = links.copy(middle_low.at[pl.ds(rows - lead, lead)], edged.at[top], edged.at[top], at.up(1)).start()
    pairs = ((edged_x, 2, slice(0, half_out)), (edged_y, 4, slice(half_out, cout)))
    exchanged = [
        links.copy(middle_low.at[:, col], target.at[inner], target.at[inner], at.near(mask)).start()
        for target, mask, col in pairs
    ]
    pool = Along(links, at, pool_own, pool_z, pool_total).start()
    groups = []

    def spread(block, target, start, order):
        size = block.shape[0]

        def place(part, half):
            first = start + order(part) * size
            if half is None:
                return target.at[ds(first, size, 16)]
            return target.at[ds(first + half * (size // 2), size // 2, 16)]

        keep = pltpu.make_async_copy(block, place(at.part, None), local.at[4 + len(groups)])
        group = Spread(links, at, place, block)
        groups.append((group, keep))
        group.one()
        keep.start()
        return group

    def tap_order(part):
        c, x, y = part & 1, (part >> 1) & 1, part >> 2
        low = at.z < fsdp // 2
        return jnp.where(low, x, y) * 4 + c * 2 + jnp.where(low, y, x)

    def natural_order(part):
        return part

    mix = Reduce(links, at, mix_slot, (mix_core, mix_x, mix_y, mix_yx, mix_xy, mix_own))
    def halo():
        load_middle.wait()
        below.wait_recv()
        above.wait_recv()
        edged[top, :] = jnp.where(at.z > 0, edged[top, :], jnp.zeros((lead, cout), BF))
        edged[bottom, :] = jnp.where(at.z < fsdp - 1, edged[bottom, :], jnp.zeros((lead, cout), BF))
        exchanged.extend(
            links.copy(edged.at[part, col], target.at[part], target.at[part], at.near(mask)).start()
            for target, mask, col in pairs
            for part in (top, bottom)
        )

    def widen():
        def body(r):
            ext[pl.ds(r, 32), :] = edged[pl.ds(r, 32), :].astype(F32)

        rows_loop(rows + 2 * lead, 32, body)

    def widen_two():
        for copy in exchanged:
            copy.wait_recv()

        def body(r):
            ext[pl.ds(r, 32), 0:half_out] = edged_x[pl.ds(r, 32), :].astype(F32)
            ext[pl.ds(r, 32), half_out:cout] = edged_y[pl.ds(r, 32), :].astype(F32)

        rows_loop(rows + 2 * lead, 32, body)

    half_width = (taps - 1) // 2

    def shift(target, k):
        start = lead + half_width - k

        def body(i, carry):
            col = ds(i * 128, 128, 128)
            target[:, col] = ext[pl.ds(start, rows), col].astype(BF)
            return carry

        lax.fori_loop(0, cout // 128, body, 0)

    def back(k):
        for i in (2 * k, 2 * k + 1):
            load_weight(i).wait()

            for j in range(2):
                at_row = j * (half_in // 2)
                col = slice((i % 2) * half_in + at_row, (i % 2) * half_in + at_row + half_in // 2)
                v = dot(shifted[k], weight[i % 2, at_row : at_row + half_in // 2, :], 1, 1)
                grad_active[:, col] = v if k == 0 else grad_active[:, col] + v
            if i + 2 < 2 * taps:
                load_weight(i + 2).start()

    columns = (ds(at.x * half_in, half_in, 128), ds(at.y * half_in, half_in, 128))
    tile = 256

    def product(k, i):
        other = (active_x, active_y)[i]

        def body(j, carry):
            col = ds(i * half_out + j * tile, tile, 128)
            v = dot(active_one[:, columns[i]], shifted[k, :, col], 0, 0)
            v = v + dot(other[...], shifted_two[:, col], 0, 0)
            slots[k, :, col] = v.astype(BF)
            return carry

        lax.fori_loop(0, half_out // tile, body, 0)

    steps = []
    for k in range(taps):
        mine_rows = pl.ds(k * tap_share, tap_share)
        steps.append(
            Tap(
                links,
                at,
                slots.at[k],
                (
                    core_slots.at[k],
                    from_x.at[mine_rows],
                    from_y.at[mine_rows],
                    own.at[mine_rows],
                    from_z.at[:, mine_rows],
                    total.at[mine_rows],
                ),
            )
        )
    mean_one, scale_one, gain_one, shift_one = (vectors[i : i + 1, :cin] for i in range(4))
    sems = (seq_send, seq_recv, fsdp_send, fsdp_recv)
    stats = Exchange(at, mine, seq_slots, fsdp_slots, sems)

    def normed(r):
        return (features[pl.ds(r, 32), :].astype(F32) - mean_one) * scale_one

    def sums():
        def grad_before(r):
            n = normed(r)
            v = normal(n * gain_one + shift_one)[1] * grad_active[pl.ds(r, 32), :]
            grad_active[pl.ds(r, 32), :] = v
            return v, v * n

        sum_shift, sum_gain = row_sums(rows, 32, cin, 2, grad_before)
        pad = jnp.zeros((1, cout - cin), F32)
        wide = lambda v: jnp.concatenate([v, pad], axis=1)
        stats.start(pack(wide(sum_shift), wide(sum_gain), vectors[6:7, :], vectors[7:8, :]))

    def store():
        everyone = unpack(stats.end(combine_sums))
        shift_grad, gain_grad = everyone[0][:, :cin], everyone[1][:, :cin]

        def body(r):
            v = grad_active[pl.ds(r, 32), :] - shift_grad / all_rows - normed(r) * gain_grad / all_rows
            grad_features[pl.ds(r, 32), :] = (gain_one * scale_one * v).astype(BF)

        rows_loop(rows, 32, body)
        sums_out[0:4, :] = jnp.concatenate(everyone, axis=0)

    spreads = {}

    def mix_core():
        load_mix.wait()
        mix.core()

    mix_along = Along(links, at, mix_own, mix_z, mix_total)

    def mix_depth():
        mix.depth()
        mix_along.start()

    def finish(name, along, target, start, order):
        along().finish()
        spreads[name] = spread(along().total, target, start, order)

    def first(k):
        shift(shifted_two, k)
        product(k, 0)

    def second(k):
        product(k, 1)
        steps[k].core()

    actions = {
        "halo": halo,
        "widen": widen,
        "w2": widen_two,
        "sums": sums,
        "e1": lambda: stats.middle(combine_sums),
        "store": store,
        "mc": mix_core,
        "mp": mix.plane,
        "mx": mix.cross,
        "md": mix_depth,
        "mh0": lambda: mix_along.hop(0),
        "mh1": lambda: mix_along.hop(1),
        "mf": lambda: finish("m", lambda: mix_along, grad_mix, 0, natural_order),
        "m2": lambda: spreads["m"].two(),
        "m3": lambda: spreads["m"].three(),
        "ph0": lambda: pool.hop(0),
        "ph1": lambda: pool.hop(1),
        "pf": lambda: finish("p", lambda: pool, grad_pool, 0, natural_order),
        "p2": lambda: spreads["p"].two(),
        "p3": lambda: spreads["p"].three(),
    }
    of_tap = {
        "s": lambda k: shift(shifted.at[k], k),
        "b": back,
        "t": first,
        "u": second,
        "pl": lambda k: steps[k].plane(),
        "d": lambda k: steps[k].depth(),
        "h": lambda k: steps[k].hop(0),
        "g": lambda k: steps[k].hop(1),
        "f": lambda k: finish(k, lambda: steps[k].along, grad_conv, k * cin, tap_order),
        "q": lambda k: spreads[k].two(),
        "r": lambda k: spreads[k].three(),
    }
    for name, action in of_tap.items():
        for k in range(taps):
            actions[f"{name}{k}"] = functools.partial(action, k)
    for name in ORDER:
        actions.pop(name)()
    assert not actions
    for group, keep in groups:
        group.four()
        keep.wait()
    links.drain()


def run_backward(sizes, features, active_one, active_x, active_y, vectors, pool_own, middle_low, full_conv, term_mix):
    seq, fsdp = sizes
    rows, cin = features.shape
    deep, cout = full_conv.shape
    taps = deep // cin
    width = cout // fsdp
    tap_share = cin // GROUP
    shape = jax.ShapeDtypeStruct
    vmem = pl.BlockSpec(memory_space=pltpu.VMEM)
    hbm = pl.BlockSpec(memory_space=pl.ANY)
    copies = 160
    return pl.pallas_call(
        functools.partial(backward_kernel, sizes),
        out_shape=(
            shape((deep, width), BF),
            shape((cout, width), BF),
            shape((cout, width), BF),
            shape((rows, cin), BF),
            shape((8, cout), F32),
        ),
        in_specs=[vmem, vmem, vmem, vmem, vmem, vmem, hbm, hbm, hbm],
        out_specs=(hbm, hbm, hbm, vmem, vmem),
        scratch_shapes=[
            pltpu.VMEM((rows + 32, cout), BF),
            pltpu.VMEM((rows + 32, cout // 2), BF),
            pltpu.VMEM((rows + 32, cout // 2), BF),
            pltpu.VMEM((rows + 32, cout), F32),
            pltpu.VMEM((taps, rows, cout), BF),
            pltpu.VMEM((rows, cout), BF),
            pltpu.VMEM((2, cin // 2, cout), BF),
            pltpu.VMEM((rows, cin), F32),
            pltpu.VMEM((taps, cin // 2, cout), BF),
            pltpu.VMEM((taps, cin // 4, cout), BF),
            pltpu.VMEM((taps * tap_share, cout // 2), BF),
            pltpu.VMEM((taps * tap_share, cout // 2), BF),
            pltpu.VMEM((taps * tap_share, cout), BF),
            pltpu.VMEM((fsdp - 1, taps * tap_share, width), BF),
            pltpu.VMEM((taps * tap_share, width), BF),
            pltpu.VMEM((cout, cout), BF),
            *Reduce.scratch(cout, cout),
            pltpu.VMEM((cout // GROUP, cout), BF),
            pltpu.VMEM((fsdp - 1, cout // GROUP, width), BF),
            pltpu.VMEM((cout // GROUP, width), BF),
            pltpu.VMEM((fsdp - 1, cout // GROUP, width), BF),
            pltpu.VMEM((cout // GROUP, width), BF),
            pltpu.VMEM((2, 16, cout // 4), F32),
            pltpu.VMEM((seq, 16, cout // 4), F32),
            pltpu.VMEM((fsdp, 16, cout // 4), F32),
            pltpu.SemaphoreType.DMA((copies,)),
            pltpu.SemaphoreType.DMA((copies,)),
            pltpu.SemaphoreType.DMA((seq,)),
            pltpu.SemaphoreType.DMA((seq,)),
            pltpu.SemaphoreType.DMA((fsdp,)),
            pltpu.SemaphoreType.DMA((fsdp,)),
            pltpu.SemaphoreType.DMA((6 + taps,)),
        ],
        compiler_params=pltpu.CompilerParams(
            collective_id=1, has_side_effects=True, vmem_limit_bytes=62 * 2**20
        ),
    )(features, active_one, active_x, active_y, vectors, pool_own, middle_low, full_conv, term_mix)


def widen_kernel(*refs):
    count = len(refs) // 2
    for source, target in zip(refs[:count], refs[count:]):
        target[...] = source[...].astype(F32)


def widened(*arrays):
    steps = 8
    specs = [pl.BlockSpec((v.shape[0] // steps, v.shape[1]), lambda i: (i, 0)) for v in arrays]
    return pl.pallas_call(
        widen_kernel,
        grid=(steps,),
        in_specs=specs,
        out_specs=specs,
        out_shape=[jax.ShapeDtypeStruct(v.shape, F32) for v in arrays],
    )(*arrays)


def spread_sum(v):
    size = lax.axis_size("seq")
    bit = GROUP
    while bit < size:
        v = v + lax.ppermute(v, "seq", [(i, i ^ bit) for i in range(size)])
        bit *= 2
    return v


def on_device(
    features,
    conv_weight,
    mix_weight,
    pool_weight,
    gain_first,
    shift_first,
    gain_second,
    shift_second,
    bias_conv,
    bias_mix,
    cotangent,
    track_counts,
):
    rows, cin = features.shape
    seq, fsdp = lax.axis_size("seq"), lax.axis_size("fsdp")
    owner = lax.axis_index("fsdp")
    width = conv_weight.shape[2]
    cout = width * fsdp
    taps = conv_weight.shape[0]
    own_vectors = [gain_first, shift_first, gain_second, shift_second, bias_conv, bias_mix]
    ends = [sum(v.shape[0] for v in own_vectors[: i + 1]) for i in range(len(own_vectors))]
    size = -(-ends[-1] // 1024) * 1024
    own_vectors = sum(jnp.pad(v.astype(F32), (end - v.shape[0], size - end)) for v, end in zip(own_vectors, ends))
    own_vectors = own_vectors.reshape(-1, 128)
    full_conv, _, _, term_mix, active_x, active_y, pool_own, pooled, active_one, middle_low, vectors = run_forward(
        (seq, fsdp),
        features,
        conv_weight.reshape(taps * cin, width),
        mix_weight,
        pool_weight,
        own_vectors,
        cotangent,
        track_counts,
    )
    grad_conv, grad_mix, grad_pool, grad_features, sums = run_backward(
        (seq, fsdp), features, active_one, active_x, active_y, vectors, pool_own, middle_low, full_conv, term_mix
    )
    grad_conv, grad_mix, grad_pool = (spread_sum(v) for v in widened(grad_conv, grad_mix, grad_pool))
    grad_conv = grad_conv.reshape(taps, cin, width)
    shift_two_grad, gain_two_grad = vectors[4], vectors[5]
    shift_one_grad, gain_one_grad, bias_one_grad, bias_two_grad = sums[0], sums[1], sums[2], sums[3]

    def share(v, size):
        return lax.dynamic_slice_in_dim(v, owner * size, size)

    first, second = gain_first.shape[0], gain_second.shape[0]
    return (
        pooled,
        grad_features,
        grad_conv,
        grad_mix,
        grad_pool,
        share(gain_one_grad, first),
        share(shift_one_grad, first),
        share(gain_two_grad, second),
        share(shift_two_grad, second),
        share(bias_one_grad, second),
        share(bias_two_grad, second),
    )


def solution(mesh):
    rows = P(("seq", "fsdp"), None)
    vector = P("fsdp")
    in_specs = (rows, P(None, None, "fsdp"), P(None, "fsdp"), P(None, "fsdp")) + (vector,) * 6 + (rows, P())
    out_specs = (rows, rows, P(None, None, "fsdp"), P(None, "fsdp"), P(None, "fsdp")) + (vector,) * 6
    return jax.shard_map(on_device, mesh=mesh, in_specs=in_specs, out_specs=out_specs, check_vma=False)
```
